32 devices in a mesh: batch: 8 (over y, x, core), blk: 4 (over z).
Axes of the slice: x: 2, y: 2, z: 4, core: 2. Of those that a mesh axis runs over, the one named last changes fastest.
Arguments:
- tokens: bfloat16 [16, 1024, 1024], P('batch', 'blk'), may hold values from -6 to 6
- doc_starts: int32 [16, 8], P('batch'), may hold values from 0 to 1023, as said below
- attn_gain: bfloat16 [1024], replicated, may hold values from 0.5 to 1.5
- attn_shift: bfloat16 [1024], replicated, may hold values from -2 to 2
- qkv_weight: bfloat16 [1024, 3072], replicated, may hold values from -0.1875 to 0.1875
- qkv_bias: bfloat16 [3072], replicated, may hold values from -2 to 2
- query_down_factor: bfloat16 [1024, 4], replicated, may hold values from -0.1875 to 0.1875
- query_up_factor: bfloat16 [4, 1024], replicated, may hold values from -0.09375 to 0.09375
- value_down_factor: bfloat16 [1024, 4], replicated, may hold values from -0.1875 to 0.1875
- value_up_factor: bfloat16 [4, 1024], replicated, may hold values from -0.09375 to 0.09375
- out_weight: bfloat16 [1024, 1024], replicated, may hold values from -0.75 to 0.75
- out_bias: bfloat16 [1024], replicated, may hold values from -2 to 2
- mlp_gain: bfloat16 [1024], replicated, may hold values from 0.5 to 1.5
- mlp_shift: bfloat16 [1024], replicated, may hold values from -2 to 2
- fc_weight: bfloat16 [1024, 4096], replicated, may hold values from -0.1875 to 0.1875
- fc_bias: bfloat16 [4096], replicated, may hold values from -2 to 2
- proj_weight: bfloat16 [4096, 1024], replicated, may hold values from -0.09375 to 0.09375
- proj_bias: bfloat16 [1024], replicated, may hold values from -2 to 2
- out_grad: bfloat16 [16, 1024, 1024], P('batch', 'blk'), may hold values from -6 to 6
Outputs:
- block_out: bfloat16 [16, 1024, 1024], P('batch', 'blk')
- tokens_grad: bfloat16 [16, 1024, 1024], P('batch', 'blk')
- grad_down_query: float32 [1024, 4], replicated
- grad_up_query: float32 [4, 1024], replicated
- grad_down_value: float32 [1024, 4], replicated
- grad_up_value: float32 [4, 1024], replicated
The draws below stay inside these ranges and needn't reach their ends.
Inputs may be any that keep to these rules, and one draw needn't show every extreme that they name: `doc_starts`: each slot holds 8 document starts, rising strictly, the first of them 0.
All inputs are finite; a program needn't handle non-finite values.
Results may differ from the reference program's by a relative error of at most 0.015.
Values may be sent and summed in bfloat16 or wider, within the bound.
A program may use at most 192 MiB of HBM per device.

```python
import math
import jax
import jax.numpy as jnp
from jax import lax

D = 1024
H = 16
FF = 4096
RANK = 4
SPAN = 256
S_DEV = 2
NDOC = 8
SLOT = 1024
SLOTS = 16


def draw_doc_starts(key, part):
    key = jax.random.fold_in(key, 11)
    key_head, key_tail, key_side = jax.random.split(key, 3)
    cuts = NDOC - 1
    head_keys = jax.random.split(key_head, SLOTS)
    tail_keys = jax.random.split(key_tail, SLOTS)
    head = jax.vmap(lambda single: jax.random.permutation(single, SPAN - 1)[:cuts] + 1)(head_keys)
    tail = jax.vmap(lambda single: jax.random.permutation(single, SPAN - 1)[:cuts] + SLOT - SPAN + 1)(tail_keys)
    side = jax.random.randint(key_side, (SLOTS, cuts), 0, 2)
    picked = jnp.sort(jnp.where(side == 1, head, tail).astype(jnp.int32), axis=1)
    return jnp.concatenate([jnp.zeros((SLOTS, 1), jnp.int32), picked], axis=1)


def steps_of(own_key, shape, cuts, smallest, top_value):
    loudness = 1.0
    for dim, blocks in cuts:
        draws = jax.random.uniform(jax.random.fold_in(jax.random.fold_in(own_key, 6), dim), (blocks,), jnp.float32, smallest / len(cuts), top_value / len(cuts))
        loudness = loudness * jnp.repeat(jnp.exp(draws), shape[dim] // blocks).reshape((-1,) + (1,) * (len(shape) - 1 - dim))
    return loudness


def bell_draw(rng, extent, deviation, reach, pieces=(), kind=jnp.bfloat16):
    level = steps_of(rng, extent, pieces, -0.22, 0.18) if pieces else 1.0
    array = jax.random.normal(rng, extent, jnp.float32) * deviation * level
    return jnp.minimum(jnp.maximum(array, -reach), reach).astype(kind)


def setup_inputs(seed: int = 0) -> dict:
    key_list = jax.random.split(jax.random.key(seed), 20)
    tokens = bell_draw(key_list[0], (SLOTS, SLOT, D), 1.0, 6.0, ((0, 8), (1, 4)))
    doc_starts = draw_doc_starts(jax.random.fold_in(key_list[19], 71), 0)
    attn_gain = jnp.clip(1.0 + 0.1 * jax.random.normal(key_list[2], (D,), jnp.float32), 0.5, 1.5).astype(jnp.bfloat16)
    attn_shift = bell_draw(key_list[3], (D,), 0.3, 2.0)
    qkv_weight = bell_draw(key_list[4], (D, 3 * D), D ** -0.5, 0.1875)
    qkv_bias = bell_draw(key_list[5], (3 * D,), 0.3, 2.0)
    query_down_factor = bell_draw(key_list[6], (D, RANK), D ** -0.5, 0.1875)
    query_up_factor = bell_draw(key_list[7], (RANK, D), (4 * D) ** -0.5, 0.09375)
    value_down_factor = bell_draw(key_list[8], (D, RANK), D ** -0.5, 0.1875)
    value_up_factor = bell_draw(key_list[9], (RANK, D), (4 * D) ** -0.5, 0.09375)
    out_weight = bell_draw(key_list[10], (D, D), (D // 16) ** -0.5, 0.75)
    out_bias = bell_draw(key_list[11], (D,), 0.3, 2.0)
    mlp_gain = jnp.clip(1.0 + 0.1 * jax.random.normal(key_list[12], (D,), jnp.float32), 0.5, 1.5).astype(jnp.bfloat16)
    mlp_shift = bell_draw(key_list[13], (D,), 0.3, 2.0)
    fc_weight = bell_draw(key_list[14], (D, FF), D ** -0.5, 0.1875)
    fc_bias = bell_draw(key_list[15], (FF,), 0.3, 2.0)
    proj_weight = bell_draw(key_list[16], (FF, D), FF ** -0.5, 0.09375)
    proj_bias = bell_draw(key_list[17], (D,), 0.3, 2.0)
    out_grad = bell_draw(key_list[18], (SLOTS, SLOT, D), 1.0, 6.0, ((0, 8), (1, 4)))
    return dict(tokens=tokens, doc_starts=doc_starts, attn_gain=attn_gain, attn_shift=attn_shift, qkv_weight=qkv_weight, qkv_bias=qkv_bias, query_down_factor=query_down_factor, query_up_factor=query_up_factor, value_down_factor=value_down_factor, value_up_factor=value_up_factor, out_weight=out_weight, out_bias=out_bias, mlp_gain=mlp_gain, mlp_shift=mlp_shift, fc_weight=fc_weight, fc_bias=fc_bias, proj_weight=proj_weight, proj_bias=proj_bias, out_grad=out_grad)


@jax.custom_vjp
def low(v):
    return lax.optimization_barrier(v.astype(jnp.bfloat16)).astype(jnp.float32)

@jax.custom_vjp
def low_back(v):
    return v

def low_keep(v):
    return (low(v), None)

def low_pass(kept, grad):
    return (grad,)

def back_keep(v):
    return (v, None)

def back_low(kept, grad):
    return (low(grad),)
low.defvjp(low_keep, low_pass)
low_back.defvjp(back_keep, back_low)
epsilon = 1e-05
adapter_scale = 8.0
neg_big = -1e+30
highest_precision = lax.Precision.HIGHEST

def layer_norm(value_rows, gain, shift):
    center = value_rows - lax.optimization_barrier(jnp.mean(value_rows, -1, keepdims=True))
    inverse = lax.rsqrt(lax.optimization_barrier(jnp.mean(center * center, -1, keepdims=True)) + epsilon)
    return center * inverse * gain + shift

def matrix_product(left, right):
    return jnp.dot(left, right, precision=highest_precision)

def slot_attention(query_rows, keys, value_rows, starts):
    length = query_rows.shape[0]
    head_size = query_rows.shape[1] // H
    positions = jnp.arange(length, dtype=jnp.int32)
    documents = lax.optimization_barrier(jnp.sum((positions[:, None] >= starts[None, :]).astype(jnp.int32), -1))
    allowed = (documents[:, None] == documents[None, :]) & (positions[None, :] <= positions[:, None])
    query_heads = query_rows.reshape(length, H, head_size)
    key_heads = keys.reshape(length, H, head_size)
    value_heads = value_rows.reshape(length, H, head_size)
    scores = jnp.einsum('qhd,khd->hqk', query_heads, key_heads, precision=highest_precision) * (1.0 / math.sqrt(head_size))
    scores = low_back(scores)
    scores = jnp.where(allowed[None], scores, neg_big)
    weights = low(jax.nn.softmax(scores, axis=-1))
    mixture = jnp.einsum('hqk,khd->qhd', weights, value_heads, precision=highest_precision)
    return mixture.reshape(length, -1)

def block_forward(inputs, starts, frozen, adapters):
    attn_gain, attn_shift, qkv_weight, qkv_bias, out_weight, out_bias, mlp_gain, mlp_shift, fc_weight, fc_bias, proj_weight, proj_bias = frozen
    query_down_factor, query_up_factor, value_down_factor, value_up_factor = adapters
    hidden_width = inputs.shape[-1]
    normalized_input = low(layer_norm(inputs, attn_gain, attn_shift))
    projected_rows = matrix_product(normalized_input, qkv_weight) + qkv_bias
    query_rows = projected_rows[..., :hidden_width] + adapter_scale * matrix_product(matrix_product(normalized_input, query_down_factor), query_up_factor)
    keys = projected_rows[..., hidden_width:2 * hidden_width]
    value_rows = projected_rows[..., 2 * hidden_width:] + adapter_scale * matrix_product(matrix_product(normalized_input, value_down_factor), value_up_factor)
    query_rows = low_back(low(query_rows))
    keys = low_back(low(keys))
    value_rows = low_back(low(value_rows))
    attended = lax.map(jax.checkpoint(lambda operands: slot_attention(*operands)), (query_rows, keys, value_rows, starts))
    attended = low_back(low(attended))
    resid = inputs + low_back(matrix_product(attended, out_weight) + out_bias)
    normed_mlp = low(layer_norm(resid, mlp_gain, mlp_shift))
    hidden = low_back(matrix_product(normed_mlp, fc_weight) + fc_bias)
    activ = low(jax.nn.gelu(hidden, approximate=True))
    return resid + low_back(matrix_product(activ, proj_weight) + proj_bias)

def reference(tokens, doc_starts, attn_gain, attn_shift, qkv_weight, qkv_bias, query_down_factor, query_up_factor, value_down_factor, value_up_factor, out_weight, out_bias, mlp_gain, mlp_shift, fc_weight, fc_bias, proj_weight, proj_bias, out_grad):
    frozen = tuple((item.astype(jnp.float32) for item in (attn_gain, attn_shift, qkv_weight, qkv_bias, out_weight, out_bias, mlp_gain, mlp_shift, fc_weight, fc_bias, proj_weight, proj_bias)))
    trainable = tuple((item.astype(jnp.float32) for item in (query_down_factor, query_up_factor, value_down_factor, value_up_factor)))
    groups = tokens.shape[0] // S_DEV
    shaped = (groups, S_DEV) + tokens.shape[1:]

    def group_step(totals, operands):
        group_tokens, group_starts, group_grad = operands

        def forward(inputs, adapters):
            return block_forward(inputs, group_starts, frozen, adapters)
        output, pullback = jax.vjp(forward, group_tokens.astype(jnp.float32), trainable)
        grad_tokens, grad_adapters = pullback(group_grad.astype(jnp.float32))
        totals = tuple((current + extra for current, extra in zip(totals, grad_adapters)))
        return (totals, (output.astype(jnp.bfloat16), grad_tokens.astype(jnp.bfloat16)))
    zeros = tuple((jnp.zeros(item.shape, jnp.float32) for item in trainable))
    totals, (outputs, grad_all) = lax.scan(group_step, zeros, (tokens.reshape(shaped), doc_starts.reshape((groups, S_DEV, -1)), out_grad.reshape(shaped)))
    return (outputs.reshape(tokens.shape), grad_all.reshape(tokens.shape), totals[0], totals[1], totals[2], totals[3])
```

```python
import jax
import jax.numpy as jnp
from jax import lax
from jax.experimental import pallas as pl
from jax.experimental.pallas import tpu as pltpu
from jax.sharding import PartitionSpec as P

F32 = jnp.float32
BF = jnp.bfloat16
MESH = pl.DeviceIdType.MESH
EPS = 1e-05
ADAPTER = 8.0
NEG = -1e30
LOG2E = 1.4426950408889634
LN2 = 0.6931471805599453
HEAD = 64
PAIR = 128
NN = (((1,), (0,)), ((), ()))
NT = (((1,), (1,)), ((), ()))
TN = (((0,), (0,)), ((), ()))


def dot(a, b, dims=NN):
    return lax.dot_general(a, b, dims, preferred_element_type=F32)


def row(ref):
    return ref[...].astype(F32).reshape(1, ref.shape[0])


def places():
    batch = lax.axis_index("batch")
    z = lax.axis_index("blk")
    core = lax.rem(batch, 2)
    base = batch - core
    outer = lax.rem(core + z, 2)
    edge = 1 - lax.rem((z + 1) // 2, 2)
    low, high = 1 - outer, 2 + outer
    hosts = [(base + lax.rem(i + edge, 2), 2 * core + i) for i in (0, 1)]
    homes = [(base + z // 2, low), (base + z // 2, high)]
    mate = (base + 1 - core, z)
    return dict(
        batch=batch, z=z, core=core, outer=outer, low=low, high=high,
        hosts=hosts, homes=homes, mate=mate,
    )


def greet(devices):
    barrier = pltpu.get_barrier_semaphore()
    for device in devices:
        pl.semaphore_signal(barrier, inc=1, device_id=device, device_id_type=MESH)
    pl.semaphore_wait(barrier, len(devices))


def remote(src, dst, send, recv, device):
    return pltpu.make_async_remote_copy(
        src_ref=src, dst_ref=dst, send_sem=send, recv_sem=recv,
        device_id=device, device_id_type=MESH,
    )


def norm_stats(x):
    center = x - jnp.mean(x, -1, keepdims=True)
    inverse = lax.rsqrt(jnp.mean(center * center, -1, keepdims=True) + EPS)
    return center * inverse, inverse


def norm_back(upstream, normed, inverse, gain):
    scaled = upstream * gain
    return inverse * (
        scaled
        - jnp.mean(scaled, -1, keepdims=True)
        - normed * jnp.mean(scaled * normed, -1, keepdims=True)
    )


def mask_bias(starts, key_span, query_span, span):
    key_pos = lax.broadcasted_iota(jnp.int32, (span, 1), 0) + key_span * span
    query_pos = lax.broadcasted_iota(jnp.int32, (1, span), 1) + query_span * span
    key_doc = jnp.zeros((span, 1), jnp.int32)
    query_doc = jnp.zeros((1, span), jnp.int32)
    for j in range(starts.shape[1]):
        start = starts[0:1, j : j + 1]
        key_doc = key_doc + (key_pos >= start).astype(jnp.int32)
        query_doc = query_doc + (query_pos >= start).astype(jnp.int32)
    allowed = (key_doc == query_doc) & (key_pos <= query_pos)
    return jnp.where(allowed, 0.0, NEG)


def half_rows(x, head):
    part = x[HEAD * head : HEAD * head + HEAD]
    zero = jnp.zeros_like(part)
    return jnp.concatenate([part, zero] if head == 0 else [zero, part], 0)


def half_lanes(x, head):
    lane = lax.broadcasted_iota(jnp.int32, x.shape, 1)
    keep = (lane < HEAD) if head == 0 else (lane >= HEAD)
    return jnp.where(keep, x, jnp.zeros_like(x))


def front_kernel(
    tok, og, wqkv, starts, gain, shift, qkv_bias, down_q, up_q, down_v, up_v,
    tok_o, og_o, q_o, k_o, v_o, e_o, ot_o, on_o, wf_o, rl_o,
    tokin, wf, n1, qn, kn, vn, qp, vt, sc, ee, bias, ot, on, starts_in,
    tok_s, tok_r, og_s, og_r, ex_s, ex_r, st_sem, loc, e_sem,
):
    at = places()
    z, core, outer = at["z"], at["core"], at["outer"]
    span, width = tokin.shape[1], tokin.shape[2]
    pairs_n = qn.shape[0]
    blocks = width // 256

    load_w = pltpu.make_async_copy(wqkv, wf, loc.at[0])
    load_w.start()
    greet(at["hosts"] + at["homes"] + [at["mate"]])
    tok_send = [
        remote(tok.at[i], tokin.at[z // 2], tok_s.at[i], tok_r.at[z // 2], at["hosts"][i])
        for i in (0, 1)
    ]
    for copy in tok_send:
        copy.start()
    starts_copy = remote(starts, starts_in, st_sem.at[0], st_sem.at[1], at["mate"])
    starts_copy.start()

    load_w.wait()
    for part, down, up in ((0, down_q, up_q), (2, down_v, up_v)):

        @pl.loop(0, blocks)
        def _(c):
            col = pl.ds(pl.multiple_of(part * width + c * 256, 256), 256)
            here = pl.ds(pl.multiple_of(c * 256, 256), 256)
            extra = dot(down[...], up[:, here])
            wf[:, col] = (wf[:, col].astype(F32) + ADAPTER * extra).astype(BF)

    save_w = pltpu.make_async_copy(wf, wf_o, loc.at[0])
    save_w.start()

    starts_copy.wait()
    mine = (z // 2 == core).astype(jnp.int32)
    both = starts[...] * mine + starts_in[...] * (1 - mine)
    second = lax.rem(z, 2)
    chosen = both[0:1] * (1 - second) + both[1:2] * second
    low, high = at["low"], at["high"]
    first_remote = 1 - low
    key_spans = (low, high, low, first_remote, first_remote + outer)
    query_spans = (low, high, high, low + outer * (high - low), high)
    for j in range(5):
        bias[j] = mask_bias(chosen, key_spans[j], query_spans[j], span)

    for i in (0, 1):
        remote(tokin.at[i], tokin.at[i], tok_s.at[i], tok_r.at[i], at["mate"]).wait_recv()
        x = tokin[i].astype(F32)
        normed, _ = norm_stats(x)
        n1[pl.ds(i * span, span), :] = (normed * row(gain) + row(shift)).astype(BF)
    for copy in tok_send:
        copy.wait_send()
    og_send = [
        remote(og.at[i], og_o.at[z // 2], og_s.at[i], og_r.at[z // 2], at["hosts"][i])
        for i in (0, 1)
    ]
    for copy in og_send:
        copy.start()
    save_tok = pltpu.make_async_copy(tokin, tok_o, loc.at[1])
    save_tok.start()

    def exchange(c):
        here = pl.ds(2 * c, 2)
        return [
            remote(ref.at[here, 0:2], ref.at[here, 2:4], ex_s.at[c, t], ex_r.at[c, t], at["mate"])
            for t, ref in enumerate((kn, vn))
        ]

    biases = row(qkv_bias)

    @pl.loop(0, blocks)
    def _(c):
        for part, store, scale in ((1, kn, None), (2, vn, None), (0, qn, LOG2E / HEAD**0.5)):
            col = pl.ds(pl.multiple_of(part * width + c * 256, 256), 256)
            made = dot(n1[...], wf[:, col]) + qkv_bias[col].astype(F32).reshape(1, 256)
            if scale is not None:
                made = made * scale
            made = made.astype(BF)
            for s in (0, 1):
                for t in (0, 1):
                    store[2 * c + t, s] = made[s * span : (s + 1) * span, t * PAIR : (t + 1) * PAIR]
            if part == 2:
                for copy in exchange(c):
                    copy.start()

    outer_f = outer.astype(F32)
    inner_f = 1.0 - outer_f
    ones = jnp.ones((16, span), BF)

    def save_e(hp):
        return pltpu.make_async_copy(ee.at[lax.rem(hp, 2)], e_o.at[hp], e_sem.at[lax.rem(hp, 2)])

    @pl.loop(0, pairs_n)
    def _(hp):
        slot = lax.rem(hp, 2)

        @pl.when(slot == 0)
        def _():
            for copy in exchange(hp // 2):
                copy.wait()

        @pl.when(hp >= 2)
        def _():
            save_e(hp - 2).wait()

        for s in (0, 1):
            q_t = qn[hp, s].T
            for head in (0, 1):
                qp[head, s] = half_rows(q_t, head)
        for kb in range(4):
            vt[kb] = vn[hp, kb].T
        key_at = (0, 1, 0, 2, 2 + outer)
        query_at = (0, 1, 1, outer, 1)
        tops = []
        for head in (0, 1):
            tops.append([])
            for j in range(5):
                s_j = dot(kn[hp, key_at[j]], qp[head, query_at[j]]) + bias[j]
                sc[head, j] = s_j
                tops[head].append(jnp.max(s_j, 0, keepdims=True))
        for head in (0, 1):
            m0, m1, m2, m3, m4 = tops[head]
            top_low = jnp.maximum(m0, m3 * inner_f + NEG * outer_f)
            top_high = jnp.maximum(
                jnp.maximum(m1, m2), jnp.maximum(m4, m3 * outer_f + NEG * inner_f)
            )
            top_x = top_high * outer_f + top_low * inner_f
            mixed = []
            for j, top in enumerate((top_low, top_high, top_high, top_x, top_high)):
                e_j = jnp.exp2(sc[head, j] - top).astype(BF)
                ee[slot, head * 5 + j] = e_j
                v_j = jnp.concatenate(
                    [vt[key_at[j], HEAD * head : HEAD * head + HEAD], ones], 0
                )
                mixed.append(dot(v_j, e_j))
            sums = (
                mixed[0] + mixed[3] * inner_f,
                mixed[1] + mixed[2] + mixed[4] + mixed[3] * outer_f,
            )
            for s in (0, 1):
                inv = 1.0 / sums[s][HEAD : HEAD + 1]
                rl_o[hp, 2 * head + s : 2 * head + s + 1, :] = inv
                ot[hp, s, HEAD * head : HEAD * head + HEAD, :] = (sums[s][:HEAD] * inv).astype(BF)
        for s in (0, 1):
            on[s, :, pl.ds(pl.multiple_of(hp * PAIR, PAIR), PAIR)] = ot[hp, s].T
        save_e(hp).start()

    outs = [
        pltpu.make_async_copy(src, dst, loc.at[k + 2])
        for k, (src, dst) in enumerate(((on, on_o), (ot, ot_o), (qn, q_o), (kn, k_o), (vn, v_o)))
    ]
    for copy in outs:
        copy.start()
    for hp in (pairs_n - 2, pairs_n - 1):
        save_e(hp).wait()
    for copy in outs:
        copy.wait()
    save_w.wait()
    save_tok.wait()
    for i in (0, 1):
        og_send[i].wait_send()
        remote(og_o.at[i], og_o.at[i], og_s.at[i], og_r.at[i], at["mate"]).wait_recv()


def mlp_kernel(
    on, tok, og, wo, out_bias, gain, shift, proj_bias, fc_bias, fc, proj,
    out, gr, da,
    resid, n2, acc_o, acc_g, og_flat,
):
    step = pl.program_id(0)
    span = tok.shape[1]

    @pl.when(step == 0)
    def _():
        for s in (0, 1):
            here = pl.ds(s * span, span)
            r = tok[s].astype(F32) + (dot(on[s], wo[...]) + row(out_bias))
            resid[here] = r
            normed, _ = norm_stats(r)
            n2[here] = (normed * row(gain) + row(shift)).astype(BF)
            acc_o[here] = r + row(proj_bias)
            acc_g[here] = jnp.zeros_like(r)
            og_flat[here] = og[s]

    x = dot(n2[...], fc[...]) + row(fc_bias)
    sq = x * x
    k0 = 0.7978845608028654
    t = jnp.tanh(x * (k0 + (k0 * 0.044715) * sq))
    half = 0.5 + 0.5 * t
    act = (x * half).astype(BF)
    slope = half + 0.5 * x * (1.0 - t * t) * (k0 + (3.0 * k0 * 0.044715) * sq)
    acc_o[...] += dot(act, proj[...])
    gh = (dot(og_flat[...], proj[...], NT) * slope).astype(BF)
    acc_g[...] += dot(gh, fc[...], NT)

    @pl.when(step == pl.num_programs(0) - 1)
    def _():
        for s in (0, 1):
            here = pl.ds(s * span, span)
            out[s] = acc_o[here].astype(BF)
            normed, inverse = norm_stats(resid[here])
            g = og[s].astype(F32) + norm_back(acc_g[here], normed, inverse, row(gain))
            gr[s] = g
            da[s] = dot(g.astype(BF), wo[...], NT).astype(BF)


def back_kernel(
    rounds,
    out_h, gr, da, tok, q_h, k_h, v_h, ot_h, e_h, wf_h, rl, gain, shift, down_q, up_q, down_v, up_v,
    out_o, tg_o, gdq_o, guq_o, gdv_o, guv_o,
    qn, kn, vn, ot, ee, wf, da_s, tok_s, gr_s, dq, dk, dv, kt, dop, don, qm, part, part_in, gn, tg, n1,
    ar, ar_in,
    out_s, out_r, tg_s, tg_r, ex_s, ex_r, ar_s, ar_r, loc, e_sem,
):
    at = places()
    z, outer = at["z"], at["outer"]
    span, width = tg.shape[1], tg.shape[2]
    pairs_n = qn.shape[0]
    batch = at["batch"]
    peers = []
    for axis, distance in rounds:
        if axis == 0:
            low_bit = lax.rem(batch // distance, 2)
            peers.append((batch + distance - 2 * distance * low_bit, z))
        else:
            low_bit = lax.rem(z // distance, 2)
            peers.append((batch, z + distance - 2 * distance * low_bit))

    def load_e(hp):
        return pltpu.make_async_copy(e_h.at[hp], ee.at[lax.rem(hp, 2)], e_sem.at[lax.rem(hp, 2)])

    loads = [
        pltpu.make_async_copy(src, dst, loc.at[k])
        for k, (src, dst) in enumerate(
            ((da, da_s), (ot_h, ot), (q_h, qn), (k_h, kn), (v_h, vn), (wf_h, wf), (tok, tok_s), (gr, gr_s))
        )
    ]
    for copy in loads[:5]:
        copy.start()
    load_e(0).start()
    for copy in loads[5:]:
        copy.start()
    greet(at["hosts"] + at["homes"] + [at["mate"]] + peers)
    out_send = [
        remote(out_h.at[i], out_o.at[lax.rem(z, 2)], out_s.at[i], out_r.at[lax.rem(z, 2)], at["homes"][i])
        for i in (0, 1)
    ]
    for copy in out_send:
        copy.start()
    for copy in loads[:5]:
        copy.wait()

    outer_f = outer.astype(F32)
    inner_f = 1.0 - outer_f
    key_at = (0, 1, 0, 2, 2 + outer)
    query_at = (0, 1, 1, outer, 1)

    def exchange(hp):
        return remote(part.at[hp], part_in.at[hp], ex_s.at[hp], ex_r.at[hp], at["mate"])

    @pl.loop(0, pairs_n)
    def _(hp):
        slot = lax.rem(hp, 2)
        lanes = pl.ds(pl.multiple_of(hp * PAIR, PAIR), PAIR)

        @pl.when(hp + 1 < pairs_n)
        def _():
            load_e(hp + 1).start()

        load_e(hp).wait()
        delta = [[None, None], [None, None]]
        for s in (0, 1):
            da_t = da_s[s, :, lanes].astype(F32).T
            o_t = ot[hp, s].astype(F32)
            prod = da_t * o_t
            scaled = []
            for head in (0, 1):
                rows_h = slice(HEAD * head, HEAD * head + HEAD)
                inv = rl[hp, 2 * head + s : 2 * head + s + 1, :]
                delta[head][s] = jnp.sum(prod[rows_h], 0, keepdims=True) * inv
                scaled.append(da_t[rows_h] * inv)
            both = jnp.concatenate(scaled, 0).astype(BF)
            natural = both.T
            q_n = qn[hp, s]
            for head in (0, 1):
                dop[head, s] = half_rows(both, head)
                don[s, head * span : (head + 1) * span] = half_lanes(natural, head)
                qm[s, head * span : (head + 1) * span] = half_lanes(q_n, head)
        for kb in range(4):
            kt[kb] = kn[hp, kb].T
        dq_t = [[None, None], [None, None]]
        grads = [[], []]
        dk_parts, dv_parts = [], []
        for j in range(5):
            ds_pair, e_pair = [], []
            for head in (0, 1):
                d_low, d_high = delta[head]
                d_j = (d_low, d_high, d_high, d_high * outer_f + d_low * inner_f, d_high)[j]
                e_j = ee[slot, head * 5 + j]
                dp = dot(vn[hp, key_at[j]], dop[head, query_at[j]])
                ds_j = (e_j.astype(F32) * (dp - d_j)).astype(BF)
                grads[head].append(
                    dot(kt[key_at[j], HEAD * head : HEAD * head + HEAD], ds_j)
                )
                ds_pair.append(ds_j)
                e_pair.append(e_j)
            dk_parts.append(dot(jnp.concatenate(ds_pair, 1), qm[query_at[j]]))
            dv_parts.append(dot(jnp.concatenate(e_pair, 1), don[query_at[j]]))
        for t, parts, scale in ((0, dk_parts, LN2), (1, dv_parts, 1.0)):
            store = (dk, dv)[t]
            store[0, :, lanes] = ((parts[0] + parts[2]) * scale).astype(BF)
            store[1, :, lanes] = (parts[1] * scale).astype(BF)
            part[hp, t, 0] = ((parts[3] + parts[4] * inner_f) * scale).astype(BF)
            part[hp, t, 1] = (parts[4] * (outer_f * scale)).astype(BF)
        exchange(hp).start()
        for s in (0, 1):
            rows_t = []
            for head in (0, 1):
                g = grads[head]
                if s == 0:
                    total = g[0] + g[3] * inner_f
                else:
                    total = g[1] + g[2] + g[4] + g[3] * outer_f
                rows_t.append(total * (1.0 / HEAD**0.5))
            dq[s, :, lanes] = jnp.concatenate(rows_t, 0).astype(BF).T

    @pl.loop(0, pairs_n)
    def _(hp):
        lanes = pl.ds(pl.multiple_of(hp * PAIR, PAIR), PAIR)
        exchange(hp).wait()
        for t, store in ((0, dk), (1, dv)):
            for s in (0, 1):
                mine = store[s, :, lanes].astype(F32)
                store[s, :, lanes] = (mine + part_in[hp, t, s].astype(F32)).astype(BF)

    for copy in loads[5:]:
        copy.wait()
    tg_send = []
    for s in (0, 1):

        @pl.loop(0, width // 256)
        def _(c):
            here = pl.ds(pl.multiple_of(c * 256, 256), 256)
            total = dot(dq[s], wf[here, 0:width], NT)
            total += dot(dk[s], wf[here, width : 2 * width], NT)
            total += dot(dv[s], wf[here, 2 * width : 3 * width], NT)
            gn[:, here] = total

        normed, inverse = norm_stats(tok_s[s].astype(F32))
        n1[s] = (normed * row(gain) + row(shift)).astype(BF)
        tg[s] = (gr_s[s] + norm_back(gn[...], normed, inverse, row(gain))).astype(BF)
        if s == 0:
            for i in (0, 1):
                out_send[i].wait_send()
        copy = remote(
            tg.at[s], tg_o.at[lax.rem(z, 2)], tg_s.at[s], tg_r.at[lax.rem(z, 2)], at["homes"][s]
        )
        copy.start()
        tg_send.append(copy)

    ar[...] = jnp.zeros_like(ar)
    for k, (grad, down, up) in enumerate(((dq, down_q, up_q), (dv, down_v, up_v))):
        up_total = down_total = 0.0
        for s in (0, 1):
            inner = dot(n1[s], down[...]).astype(BF)
            lift = dot(grad[s], up[...], NT).astype(BF)
            up_total = up_total + dot(inner, grad[s], TN)
            down_total = down_total + dot(lift, n1[s], TN)
        ar[2 * k, 0:4] = ADAPTER * up_total
        ar[2 * k + 1, 0:4] = ADAPTER * down_total
    for r, peer in enumerate(peers):
        copy = remote(ar, ar_in.at[r], ar_s.at[r], ar_r.at[r], peer)
        copy.start()
        copy.wait()
        ar[...] += ar_in[r]
    guq_o[...] = ar[0, 0:4]
    guv_o[...] = ar[2, 0:4]
    gdq_o[...] = ar[1].T[:, 0:4]
    gdv_o[...] = ar[3].T[:, 0:4]

    for i in (0, 1):
        remote(out_o.at[i], out_o.at[i], out_s.at[i], out_r.at[i], at["mate"]).wait_recv()
        tg_send[i].wait_send()
        remote(tg_o.at[i], tg_o.at[i], tg_s.at[i], tg_r.at[i], at["mate"]).wait_recv()


VMEM = pl.BlockSpec(memory_space=pltpu.VMEM)
ANY = pl.BlockSpec(memory_space=pl.ANY)
DMA = pltpu.SemaphoreType.DMA
LIMIT = 60 * 1024 * 1024


def on_device(
    tokens, doc_starts, attn_gain, attn_shift, qkv_weight, qkv_bias,
    query_down_factor, query_up_factor, value_down_factor, value_up_factor,
    out_weight, out_bias, mlp_gain, mlp_shift, fc_weight, fc_bias, proj_weight, proj_bias, out_grad,
):
    slots, span, width = tokens.shape
    hidden = fc_weight.shape[1]
    rank = query_down_factor.shape[1]
    pairs_n = width // PAIR
    shape = jax.ShapeDtypeStruct
    rows_two = shape((slots, span, width), BF)
    q_shape = (pairs_n, 2, span, PAIR)
    k_shape = (pairs_n, 4, span, PAIR)
    e_shape = (pairs_n, 10, span, span)
    t_shape = (pairs_n, 2, PAIR, span)

    tok, og, q_h, k_h, v_h, e_h, ot, on, wf, rl = pl.pallas_call(
        front_kernel,
        out_shape=(
            rows_two, rows_two, shape(q_shape, BF), shape(k_shape, BF), shape(k_shape, BF),
            shape(e_shape, BF), shape(t_shape, BF), rows_two, shape((width, 3 * width), BF),
            shape((pairs_n, 8, span), F32),
        ),
        in_specs=[ANY] * 3 + [VMEM] * 8,
        out_specs=(ANY,) * 9 + (VMEM,),
        scratch_shapes=[
            pltpu.VMEM((2, span, width), BF),
            pltpu.VMEM((width, 3 * width), BF),
            pltpu.VMEM((2 * span, width), BF),
            pltpu.VMEM(q_shape, BF),
            pltpu.VMEM(k_shape, BF),
            pltpu.VMEM(k_shape, BF),
            pltpu.VMEM((2, 2, PAIR, span), BF),
            pltpu.VMEM((4, PAIR, span), BF),
            pltpu.VMEM((2, 5, span, span), F32),
            pltpu.VMEM((2, 10, span, span), BF),
            pltpu.VMEM((5, span, span), F32),
            pltpu.VMEM(t_shape, BF),
            pltpu.VMEM((2, span, width), BF),
            pltpu.VMEM(doc_starts.shape, jnp.int32),
            DMA((2,)), DMA((2,)), DMA((2,)), DMA((2,)),
            DMA((width // 256, 2)), DMA((width // 256, 2)), DMA((2,)), DMA((7,)), DMA((2,)),
        ],
        compiler_params=pltpu.CompilerParams(
            collective_id=0, has_side_effects=True, vmem_limit_bytes=LIMIT
        ),
    )(
        tokens, out_grad, qkv_weight, doc_starts, attn_gain, attn_shift, qkv_bias,
        query_down_factor, query_up_factor, value_down_factor, value_up_factor,
    )

    chunk = 512
    whole = lambda *dims: pl.BlockSpec(dims, lambda f: (0,) * len(dims))
    out_slot, grad_resid, grad_att = pl.pallas_call(
        mlp_kernel,
        grid=(hidden // chunk,),
        out_shape=(rows_two, shape((slots, span, width), F32), rows_two),
        in_specs=[
            whole(slots, span, width), whole(slots, span, width), whole(slots, span, width),
            whole(width, width), whole(width), whole(width), whole(width), whole(width),
            pl.BlockSpec((chunk,), lambda f: (f,)),
            pl.BlockSpec((width, chunk), lambda f: (0, f)),
            pl.BlockSpec((chunk, width), lambda f: (f, 0)),
        ],
        out_specs=(whole(slots, span, width),) * 3,
        scratch_shapes=[
            pltpu.VMEM((2 * span, width), F32),
            pltpu.VMEM((2 * span, width), BF),
            pltpu.VMEM((2 * span, width), F32),
            pltpu.VMEM((2 * span, width), F32),
            pltpu.VMEM((2 * span, width), BF),
        ],
        compiler_params=pltpu.CompilerParams(
            dimension_semantics=("arbitrary",), vmem_limit_bytes=LIMIT
        ),
    )(on, tok, og, out_weight, out_bias, mlp_gain, mlp_shift, proj_bias, fc_bias, fc_weight, proj_weight)

    rounds = []
    for axis, size in ((0, lax.axis_size("batch")), (1, lax.axis_size("blk"))):
        distance = 1
        while distance < size:
            rounds.append((axis, distance))
            distance *= 2
    n_rounds = len(rounds)

    def back(*refs):
        back_kernel(rounds, *refs)

    small = lambda *dims: shape(dims, F32)
    return pl.pallas_call(
        back,
        out_shape=(
            rows_two, rows_two, small(width, rank), small(rank, width), small(width, rank), small(rank, width),
        ),
        in_specs=[ANY] * 10 + [VMEM] * 7,
        out_specs=(ANY,) * 2 + (VMEM,) * 4,
        scratch_shapes=[
            pltpu.VMEM(q_shape, BF),
            pltpu.VMEM(k_shape, BF),
            pltpu.VMEM(k_shape, BF),
            pltpu.VMEM(t_shape, BF),
            pltpu.VMEM((2, 10, span, span), BF),
            pltpu.VMEM((width, 3 * width), BF),
            pltpu.VMEM((2, span, width), BF),
            pltpu.VMEM((2, span, width), BF),
            pltpu.VMEM((2, span, width), F32),
            pltpu.VMEM((2, span, width), BF),
            pltpu.VMEM((2, span, width), BF),
            pltpu.VMEM((2, span, width), BF),
            pltpu.VMEM((4, PAIR, span), BF),
            pltpu.VMEM((2, 2, PAIR, span), BF),
            pltpu.VMEM((2, 2 * span, PAIR), BF),
            pltpu.VMEM((2, 2 * span, PAIR), BF),
            pltpu.VMEM((pairs_n, 2, 2, span, PAIR), BF),
            pltpu.VMEM((pairs_n, 2, 2, span, PAIR), BF),
            pltpu.VMEM((span, width), F32),
            pltpu.VMEM((2, span, width), BF),
            pltpu.VMEM((2, span, width), BF),
            pltpu.VMEM((4, 8, width), F32),
            pltpu.VMEM((n_rounds, 4, 8, width), F32),
            DMA((2,)), DMA((2,)), DMA((2,)), DMA((2,)), DMA((pairs_n,)), DMA((pairs_n,)),
            DMA((n_rounds,)), DMA((n_rounds,)), DMA((8,)), DMA((2,)),
        ],
        compiler_params=pltpu.CompilerParams(
            collective_id=1, has_side_effects=True, vmem_limit_bytes=LIMIT
        ),
    )(
        out_slot, grad_resid, grad_att, tok, q_h, k_h, v_h, ot, e_h, wf, rl, attn_gain, attn_shift,
        query_down_factor, query_up_factor, value_down_factor, value_up_factor,
    )


def solution(mesh):
    rows = P("batch", "blk", None)
    return jax.shard_map(
        on_device,
        mesh=mesh,
        in_specs=(rows, P("batch", None)) + (P(),) * 16 + (rows,),
        out_specs=(rows, rows, P(), P(), P(), P()),
        check_vma=False,
    )
```

```python
import jax
import jax.numpy as jnp
from jax import lax
from jax.experimental import pallas as pl
from jax.experimental.pallas import tpu as pltpu
from jax.sharding import PartitionSpec as P

F32 = jnp.float32
BF = jnp.bfloat16
MESH = pl.DeviceIdType.MESH
EPS = 1e-05
ADAPTER = 8.0
NEG = -1e30
LOG2E = 1.4426950408889634
LN2 = 0.6931471805599453
HEAD = 64
PAIR = 128
NN = (((1,), (0,)), ((), ()))
NT = (((1,), (1,)), ((), ()))
TN = (((0,), (0,)), ((), ()))


def dot(a, b, dims=NN):
    return lax.dot_general(a, b, dims, preferred_element_type=F32)


def row(ref):
    return ref[...].astype(F32).reshape(1, ref.shape[0])


def places():
    batch = lax.axis_index("batch")
    z = lax.axis_index("blk")
    core = lax.rem(batch, 2)
    base = batch - core
    outer = lax.rem(core + z, 2)
    edge = 1 - lax.rem((z + 1) // 2, 2)
    low, high = 1 - outer, 2 + outer
    hosts = [(base + lax.rem(i + edge, 2), 2 * core + i) for i in (0, 1)]
    homes = [(base + z // 2, low), (base + z // 2, high)]
    mate = (base + 1 - core, z)
    return dict(
        batch=batch, z=z, core=core, outer=outer, low=low, high=high,
        hosts=hosts, homes=homes, mate=mate,
    )


def greet(devices):
    barrier = pltpu.get_barrier_semaphore()
    for device in devices:
        pl.semaphore_signal(barrier, inc=1, device_id=device, device_id_type=MESH)
    pl.semaphore_wait(barrier, len(devices))


def remote(src, dst, send, recv, device):
    return pltpu.make_async_remote_copy(
        src_ref=src, dst_ref=dst, send_sem=send, recv_sem=recv,
        device_id=device, device_id_type=MESH,
    )


def norm_stats(x):
    center = x - jnp.mean(x, -1, keepdims=True)
    inverse = lax.rsqrt(jnp.mean(center * center, -1, keepdims=True) + EPS)
    return center * inverse, inverse


def norm_back(upstream, normed, inverse, gain):
    scaled = upstream * gain
    return inverse * (
        scaled
        - jnp.mean(scaled, -1, keepdims=True)
        - normed * jnp.mean(scaled * normed, -1, keepdims=True)
    )


def mask_bias(starts, key_span, query_span, span):
    key_pos = lax.broadcasted_iota(jnp.int32, (span, 1), 0) + key_span * span
    query_pos = lax.broadcasted_iota(jnp.int32, (1, span), 1) + query_span * span
    key_doc = jnp.zeros((span, 1), jnp.int32)
    query_doc = jnp.zeros((1, span), jnp.int32)
    for j in range(starts.shape[1]):
        start = starts[0:1, j : j + 1]
        key_doc = key_doc + (key_pos >= start).astype(jnp.int32)
        query_doc = query_doc + (query_pos >= start).astype(jnp.int32)
    allowed = (key_doc == query_doc) & (key_pos <= query_pos)
    return jnp.where(allowed, 0.0, NEG)


def half_rows(x, head):
    part = x[HEAD * head : HEAD * head + HEAD]
    zero = jnp.zeros_like(part)
    return jnp.concatenate([part, zero] if head == 0 else [zero, part], 0)


def half_lanes(x, head):
    lane = lax.broadcasted_iota(jnp.int32, x.shape, 1)
    keep = (lane < HEAD) if head == 0 else (lane >= HEAD)
    return jnp.where(keep, x, jnp.zeros_like(x))


def fused_kernel(
    rounds,
    tok, og, wqkv, wo_h, fc_h, proj_h, starts, gain, shift, qkv_bias, out_bias, gain2, shift2,
    fc_bias, proj_bias, down_q, up_q, down_v, up_v,
    out_o, tg_o, sums_o, e_h,
    tokin, ogin, wf, wo, fcb, pjb, n1, n2, qn, kn, vn, qp, vt, sc, ee, bias, ot, on, rl,
    resid, acc, slope, outst, dk, dv, dopc, don, qm, dss, part, part_in, tg, ar, ar_in, starts_in,
    tok_s, tok_r, og_s, og_r, ex_s, ex_r, st_sem, w_sem, fc_sem, pj_sem, e_sem,
    out_s, out_r, tg_s, tg_r, px_s, px_r, ar_s, ar_r,
):
    at = places()
    z, core, outer = at["z"], at["core"], at["outer"]
    low, high, mate, batch = at["low"], at["high"], at["mate"], at["batch"]
    span, width = tokin.shape[1], tokin.shape[2]
    pairs_n = qn.shape[0]
    blocks = width // 256
    chunks, chunk = slope.shape[0], slope.shape[2]
    peers = []
    for axis, distance in rounds:
        if axis == 0:
            bit = lax.rem(batch // distance, 2)
            peers.append((batch + distance - 2 * distance * bit, z))
        else:
            bit = lax.rem(z // distance, 2)
            peers.append((batch, z + distance - 2 * distance * bit))

    load_w = pltpu.make_async_copy(wqkv, wf, w_sem.at[0])
    load_w.start()
    greet(at["hosts"] + at["homes"] + [mate] + peers)
    tok_send = [
        remote(tok.at[i], tokin.at[z // 2], tok_s.at[i], tok_r.at[z // 2], at["hosts"][i])
        for i in (0, 1)
    ]
    for copy in tok_send:
        copy.start()
    starts_copy = remote(starts, starts_in, st_sem.at[0], st_sem.at[1], mate)
    starts_copy.start()

    def load_mlp(c):
        slot = lax.rem(c, 2)
        here = pl.ds(pl.multiple_of(c * chunk, chunk), chunk)
        return (
            pltpu.make_async_copy(fc_h.at[:, here], fcb.at[slot], fc_sem.at[slot]),
            pltpu.make_async_copy(proj_h.at[here, :], pjb.at[slot], pj_sem.at[slot]),
        )

    load_w.wait()
    load_o = pltpu.make_async_copy(wo_h, wo, w_sem.at[0])
    load_o.start()
    for c in (0, 1):
        for copy in load_mlp(c):
            copy.start()
    for part_w, down, up in ((0, down_q, up_q), (2, down_v, up_v)):

        @pl.loop(0, blocks)
        def _(c):
            col = pl.ds(pl.multiple_of(part_w * width + c * 256, 256), 256)
            here = pl.ds(pl.multiple_of(c * 256, 256), 256)
            extra = dot(down[...], up[:, here], TN)
            wf[:, col] = (wf[:, col].astype(F32) + ADAPTER * extra).astype(BF)

    starts_copy.wait()
    mine = (z // 2 == core).astype(jnp.int32)
    both = starts[...] * mine + starts_in[...] * (1 - mine)
    second = lax.rem(z, 2)
    chosen = both[0:1] * (1 - second) + both[1:2] * second
    first_remote = 1 - low
    key_spans = (low, high, low, first_remote, first_remote + outer)
    query_spans = (low, high, high, low + outer * (high - low), high)
    for j in range(5):
        bias[j] = mask_bias(chosen, key_spans[j], query_spans[j], span)

    def exchange(s, c):
        here = pl.ds(2 * c, 2)
        return [
            remote(ref.at[here, s], ref.at[here, 2 + s], ex_s.at[s, c, t], ex_r.at[s, c, t], mate)
            for t, ref in enumerate((kn, vn))
        ]

    for turn in (0, 1):
        s = z // 2 if turn == 0 else 1 - z // 2
        remote(tokin.at[s], tokin.at[s], tok_s.at[0], tok_r.at[s], mate).wait_recv()
        if turn == 1:
            for copy in tok_send:
                copy.wait_send()
            og_send = [
                remote(og.at[i], ogin.at[z // 2], og_s.at[i], og_r.at[z // 2], at["hosts"][i])
                for i in (0, 1)
            ]
            for copy in og_send:
                copy.start()
        normed, _ = norm_stats(tokin[s].astype(F32))
        n1[s] = (normed * row(gain) + row(shift)).astype(BF)

        @pl.loop(0, blocks)
        def _(c):
            for which, store, scale in ((1, kn, None), (2, vn, None), (0, qn, LOG2E / HEAD**0.5)):
                col = pl.ds(pl.multiple_of(which * width + c * 256, 256), 256)
                made = dot(n1[s], wf[:, col]) + qkv_bias[col].astype(F32).reshape(1, 256)
                if scale is not None:
                    made = made * scale
                made = made.astype(BF)
                for t in (0, 1):
                    store[2 * c + t, s] = made[:, t * PAIR : (t + 1) * PAIR]
                if which == 2:
                    for copy in exchange(s, c):
                        copy.start()

    outer_f = outer.astype(F32)
    inner_f = 1.0 - outer_f
    ones = jnp.ones((16, span), BF)
    key_at = (0, 1, 0, 2, 2 + outer)
    query_at = (0, 1, 1, outer, 1)

    def save_e(hp):
        slot = lax.rem(hp, 2)
        return pltpu.make_async_copy(ee.at[slot], e_h.at[hp], e_sem.at[slot])

    def load_e(hp):
        slot = lax.rem(hp, 2)
        return pltpu.make_async_copy(e_h.at[hp], ee.at[slot], e_sem.at[slot])

    @pl.loop(0, blocks)
    def _(c):
        for s in (0, 1):
            for copy in exchange(s, c):
                copy.wait()

    @pl.loop(0, pairs_n)
    def _(hp):
        slot = lax.rem(hp, 2)

        @pl.when(hp >= 2)
        def _():
            save_e(hp - 2).wait()

        for s in (0, 1):
            q_t = qn[hp, s].T
            for head in (0, 1):
                qp[head, s] = half_rows(q_t, head)
        for kb in range(4):
            vt[kb] = vn[hp, kb].T
        tops = []
        for head in (0, 1):
            tops.append([])
            for j in range(5):
                s_j = dot(kn[hp, key_at[j]], qp[head, query_at[j]]) + bias[j]
                sc[head, j] = s_j
                tops[head].append(jnp.max(s_j, 0, keepdims=True))
        for head in (0, 1):
            m0, m1, m2, m3, m4 = tops[head]
            top_low = jnp.maximum(m0, m3 * inner_f + NEG * outer_f)
            top_high = jnp.maximum(
                jnp.maximum(m1, m2), jnp.maximum(m4, m3 * outer_f + NEG * inner_f)
            )
            top_x = top_high * outer_f + top_low * inner_f
            mixed = []
            for j, top in enumerate((top_low, top_high, top_high, top_x, top_high)):
                e_j = jnp.exp2(sc[head, j] - top).astype(BF)
                ee[slot, j, :, head * span : (head + 1) * span] = e_j
                v_j = jnp.concatenate(
                    [vt[key_at[j], HEAD * head : HEAD * head + HEAD], ones], 0
                )
                mixed.append(dot(v_j, e_j))
            sums = (
                mixed[0] + mixed[3] * inner_f,
                mixed[1] + mixed[2] + mixed[4] + mixed[3] * outer_f,
            )
            for s in (0, 1):
                inv = 1.0 / sums[s][HEAD : HEAD + 1]
                rl[hp, 2 * head + s : 2 * head + s + 1, :] = inv
                ot[hp, s, HEAD * head : HEAD * head + HEAD, :] = (sums[s][:HEAD] * inv).astype(BF)
        for s in (0, 1):
            on[s, :, pl.ds(pl.multiple_of(hp * PAIR, PAIR), PAIR)] = ot[hp, s].T
        save_e(hp).start()

    load_o.wait()
    for s in (0, 1):
        here = pl.ds(s * span, span)
        r = tokin[s].astype(F32) + (dot(on[s], wo[...]) + row(out_bias))
        resid[here] = r
        normed, _ = norm_stats(r)
        n2[here] = (normed * row(gain2) + row(shift2)).astype(BF)
        acc[here] = r + row(proj_bias)

    @pl.loop(0, chunks)
    def _(c):
        slot = lax.rem(c, 2)
        for copy in load_mlp(c):
            copy.wait()
        part_b = fc_bias[pl.ds(pl.multiple_of(c * chunk, chunk), chunk)]
        x = dot(n2[...], fcb[slot]) + part_b.astype(F32).reshape(1, chunk)
        sq = x * x
        half = 0.5 * jnp.tanh(x * ((GELU * 0.044715) * sq + GELU)) + 0.5
        act = x * half
        rise = half + (act - act * half) * ((6.0 * GELU * 0.044715) * sq + 2.0 * GELU)
        slope[c] = rise.astype(BF)
        acc[...] += dot(act.astype(BF), pjb[slot])

        @pl.when(c + 2 < chunks)
        def _():
            for copy in load_mlp(c + 2):
                copy.start()

    for s in (0, 1):
        outst[s] = acc[pl.ds(s * span, span)].astype(BF)
    for i in (0, 1):
        og_send[i].wait_send()
    out_send = [
        remote(
            outst.at[i], out_o.at[lax.rem(z, 2)], out_s.at[i], out_r.at[lax.rem(z, 2)], at["homes"][i]
        )
        for i in (0, 1)
    ]
    for copy in out_send:
        copy.start()
    acc[...] = jnp.zeros_like(acc)
    for hp in (pairs_n - 2, pairs_n - 1):
        save_e(hp).wait()
    for i in (0, 1):
        remote(ogin.at[i], ogin.at[i], og_s.at[i], og_r.at[i], mate).wait_recv()

    @pl.loop(0, chunks)
    def _(t):
        c = chunks - 1 - t
        slot = lax.rem(c, 2)

        @pl.when(t >= 2)
        def _():
            for copy in load_mlp(c):
                copy.wait()

        og_flat = ogin[...].reshape(2 * span, width)
        gh = (dot(og_flat, pjb[slot], NT) * slope[c].astype(F32)).astype(BF)
        acc[...] += dot(gh, fcb[slot], NT)

        @pl.when(c >= 2)
        def _():
            for copy in load_mlp(c - 2):
                copy.start()

    for s in (0, 1):
        here = pl.ds(s * span, span)
        normed, inverse = norm_stats(resid[here])
        g = ogin[s].astype(F32) + norm_back(acc[here], normed, inverse, row(gain2))
        resid[here] = g
        n2[here] = dot(g.astype(BF), wo[...], NT).astype(BF)

    def part_send(hp):
        return remote(part.at[hp], part_in.at[hp], px_s.at[hp], px_r.at[hp], mate)

    @pl.loop(0, pairs_n)
    def _(turn):
        hp = pairs_n - 1 - turn
        slot = lax.rem(hp, 2)
        lanes = pl.ds(pl.multiple_of(hp * PAIR, PAIR), PAIR)

        @pl.when(turn >= 2)
        def _():
            load_e(hp).wait()

        delta = [[None, None], [None, None]]
        for s in (0, 1):
            da_t = n2[s * span : (s + 1) * span, lanes].astype(F32).T
            prod = da_t * ot[hp, s].astype(F32)
            scaled = []
            for head in (0, 1):
                rows_h = slice(HEAD * head, HEAD * head + HEAD)
                inv = rl[hp, 2 * head + s : 2 * head + s + 1, :]
                delta[head][s] = jnp.sum(prod[rows_h], 0, keepdims=True) * inv
                scaled.append(da_t[rows_h] * inv)
            scaled = jnp.concatenate(scaled, 0).astype(BF)
            natural = scaled.T
            q_n = qn[hp, s]
            for head in (0, 1):
                cols = slice(head * span, (head + 1) * span)
                dopc[s, :, cols] = half_rows(scaled, head)
                don[s, cols] = half_lanes(natural, head)
                qm[s, cols] = half_lanes(q_n, head)
        for kb in range(4):
            vt[kb] = kn[hp, kb].T
        for j in range(5):
            for head in (0, 1):
                cols = slice(head * span, (head + 1) * span)
                d_low, d_high = delta[head]
                d_j = (d_low, d_high, d_high, d_high * outer_f + d_low * inner_f, d_high)[j]
                dp = dot(vn[hp, key_at[j]], dopc[query_at[j], :, cols])
                dss[j, :, cols] = (ee[slot, j, :, cols].astype(F32) * (dp - d_j)).astype(BF)
        dk_parts, dv_parts, grads = [], [], [[], []]
        for j in range(5):
            dv_parts.append(dot(ee[slot, j], don[query_at[j]]))
        for j in range(5):
            for head in (0, 1):
                cols = slice(head * span, (head + 1) * span)
                grads[head].append(
                    dot(vt[key_at[j], HEAD * head : HEAD * head + HEAD], dss[j, :, cols])
                )
            dk_parts.append(dot(dss[j], qm[query_at[j]]))
        for t, parts, scale in ((0, dk_parts, LN2), (1, dv_parts, 1.0)):
            store = (dk, dv)[t]
            store[0, :, lanes] = ((parts[0] + parts[2]) * scale).astype(BF)
            store[1, :, lanes] = (parts[1] * scale).astype(BF)
            part[hp, t, 0] = ((parts[3] + parts[4] * inner_f) * scale).astype(BF)
            part[hp, t, 1] = (parts[4] * (outer_f * scale)).astype(BF)
        part_send(hp).start()
        for s in (0, 1):
            rows_t = []
            for head in (0, 1):
                g = grads[head]
                if s == 0:
                    total = g[0] + g[3] * inner_f
                else:
                    total = g[1] + g[2] + g[4] + g[3] * outer_f
                rows_t.append(total * (1.0 / HEAD**0.5))
            on[s, :, lanes] = jnp.concatenate(rows_t, 0).astype(BF).T

        @pl.when(hp >= 2)
        def _():
            load_e(hp - 2).start()

    dq = on

    @pl.loop(0, pairs_n)
    def _(turn):
        hp = pairs_n - 1 - turn
        lanes = pl.ds(pl.multiple_of(hp * PAIR, PAIR), PAIR)
        part_send(hp).wait()
        for t, store in ((0, dk), (1, dv)):
            for s in (0, 1):
                own = store[s, :, lanes].astype(F32)
                store[s, :, lanes] = (own + part_in[hp, t, s].astype(F32)).astype(BF)

    tg_send = []

    def ar_round(r):
        return remote(ar, ar_in.at[r], ar_s.at[r], ar_r.at[r], peers[r])

    for turn in (0, 1):
        s = 1 - z // 2 if turn == 0 else z // 2

        @pl.loop(0, blocks)
        def _(c):
            here = pl.ds(pl.multiple_of(c * 256, 256), 256)
            total = dot(dq[s], wf[here, 0:width], NT)
            total += dot(dk[s], wf[here, width : 2 * width], NT)
            total += dot(dv[s], wf[here, 2 * width : 3 * width], NT)
            acc[0:span, here] = total

        normed, inverse = norm_stats(tokin[s].astype(F32))
        rows_s = pl.ds(pl.multiple_of(s * span, span), span)
        tg[s] = (resid[rows_s] + norm_back(acc[0:span], normed, inverse, row(gain))).astype(BF)
        if turn == 0:
            for i in (0, 1):
                out_send[i].wait_send()
        home = (batch - core + z // 2, low + s * (high - low))
        copy = remote(tg.at[s], tg_o.at[lax.rem(z, 2)], tg_s.at[s], tg_r.at[lax.rem(z, 2)], home)
        copy.start()
        tg_send.append(copy)
        if turn == 0:
            ar[...] = jnp.zeros_like(ar)
            for k, (grad, down, up) in enumerate(((dq, down_q, up_q), (dv, down_v, up_v))):
                up_total = down_total = 0.0
                for i in (0, 1):
                    inner = dot(n1[i], down[...], NT).astype(BF)
                    lift = dot(grad[i], up[...], NT).astype(BF)
                    up_total = up_total + dot(inner, grad[i], TN)
                    down_total = down_total + dot(lift, n1[i], TN)
                ar[2 * k, 0:4] = ADAPTER * up_total
                ar[2 * k + 1, 0:4] = ADAPTER * down_total
            ar_round(0).start()

    for r in range(len(peers)):
        if r > 0:
            ar_round(r).start()
        ar_round(r).wait()
        ar[...] += ar_in[r]
    sums_o[...] = ar[...]

    for i in (0, 1):
        remote(out_o.at[i], out_o.at[i], out_s.at[i], out_r.at[i], mate).wait_recv()
        tg_send[i].wait_send()
        remote(tg_o.at[i], tg_o.at[i], tg_s.at[i], tg_r.at[i], mate).wait_recv()


def deliver_kernel(out_i, tg_i, sums, out_o, tg_o, down_q, up_q, down_v, up_v):
    out_o[...] = out_i[...]
    tg_o[...] = tg_i[...]
    for k, ref in enumerate((up_q, down_q, up_v, down_v)):
        ref[...] = sums[k, 0:4]


VMEM = pl.BlockSpec(memory_space=pltpu.VMEM)
ANY = pl.BlockSpec(memory_space=pl.ANY)
DMA = pltpu.SemaphoreType.DMA
LIMIT = 60 * 1024 * 1024
GELU = 0.7978845608028654


def on_device(
    tokens, doc_starts, attn_gain, attn_shift, qkv_weight, qkv_bias,
    query_down_factor, query_up_factor, value_down_factor, value_up_factor,
    out_weight, out_bias, mlp_gain, mlp_shift, fc_weight, fc_bias, proj_weight, proj_bias, out_grad,
):
    slots, span, width = tokens.shape
    hidden = fc_weight.shape[1]
    rank = query_down_factor.shape[1]
    pairs_n = width // PAIR
    chunk = 1024
    blocks = width // 256
    shape = jax.ShapeDtypeStruct
    two = (slots, span, width)
    flat = (2 * span, width)
    q_shape = (pairs_n, 2, span, PAIR)
    k_shape = (pairs_n, 4, span, PAIR)
    rounds = []
    for axis, size in ((0, lax.axis_size("batch")), (1, lax.axis_size("blk"))):
        distance = 1
        while distance < size:
            rounds.append((axis, distance))
            distance *= 2
    n_rounds = len(rounds)

    def fused(*refs):
        fused_kernel(rounds, *refs)

    bf = lambda *dims: pltpu.VMEM(dims, BF)
    f32 = lambda *dims: pltpu.VMEM(dims, F32)
    out_l, tg_l, sums, _ = pl.pallas_call(
        fused,
        out_shape=(
            shape(two, BF), shape(two, BF), shape((4, 8, width), F32),
            shape((pairs_n, 5, span, 2 * span), BF),
        ),
        in_specs=[ANY] * 6 + [VMEM] * 13,
        out_specs=(ANY, ANY, VMEM, ANY),
        scratch_shapes=[
            bf(*two), bf(*two), bf(width, 3 * width), bf(width, width),
            bf(2, width, chunk), bf(2, chunk, width), bf(*two), bf(*flat),
            bf(*q_shape), bf(*k_shape), bf(*k_shape),
            bf(2, 2, PAIR, span), bf(4, PAIR, span),
            f32(2, 5, span, span), bf(2, 5, span, 2 * span), f32(5, span, span),
            bf(pairs_n, 2, PAIR, span), bf(*two), f32(pairs_n, 8, span),
            f32(*flat), f32(*flat), bf(hidden // chunk, 2 * span, chunk), bf(*two),
            bf(*two), bf(*two),
            bf(2, PAIR, 2 * span), bf(2, 2 * span, PAIR), bf(2, 2 * span, PAIR), bf(5, span, 2 * span),
            bf(pairs_n, 2, 2, span, PAIR), bf(pairs_n, 2, 2, span, PAIR), bf(*two),
            f32(4, 8, width), f32(n_rounds, 4, 8, width), pltpu.VMEM(doc_starts.shape, jnp.int32),
            DMA((2,)), DMA((2,)), DMA((2,)), DMA((2,)),
            DMA((2, blocks, 2)), DMA((2, blocks, 2)), DMA((2,)), DMA((1,)), DMA((2,)), DMA((2,)), DMA((2,)),
            DMA((2,)), DMA((2,)), DMA((2,)), DMA((2,)),
            DMA((pairs_n,)), DMA((pairs_n,)), DMA((n_rounds,)), DMA((n_rounds,)),
        ],
        compiler_params=pltpu.CompilerParams(
            collective_id=0, has_side_effects=True, vmem_limit_bytes=LIMIT
        ),
    )(
        tokens, out_grad, qkv_weight, out_weight, fc_weight, proj_weight, doc_starts,
        attn_gain, attn_shift, qkv_bias, out_bias, mlp_gain, mlp_shift, fc_bias, proj_bias,
        query_down_factor.T, query_up_factor, value_down_factor.T, value_up_factor,
    )

    small = shape((rank, width), F32)
    block = pl.BlockSpec((1, span, width), lambda i: (i, 0, 0))
    whole = lambda *dims: pl.BlockSpec(dims, lambda i: (0,) * len(dims))
    out, tg, down_q, up_q, down_v, up_v = pl.pallas_call(
        deliver_kernel,
        grid=(slots,),
        out_shape=(shape(two, BF), shape(two, BF), small, small, small, small),
        in_specs=[block, block, whole(4, 8, width)],
        out_specs=(block, block) + (whole(rank, width),) * 4,
    )(out_l, tg_l, sums)
    return out, tg, down_q.T, up_q, down_v.T, up_v


def solution(mesh):
    rows = P("batch", "blk", None)
    return jax.shard_map(
        on_device,
        mesh=mesh,
        in_specs=(rows, P("batch", None)) + (P(),) * 16 + (rows,),
        out_specs=(rows, rows, P(), P(), P(), P()),
        check_vma=False,
    )
```

```python
import jax
import jax.numpy as jnp
from jax import lax
from jax.experimental import pallas as pl
from jax.experimental.pallas import tpu as pltpu
from jax.sharding import PartitionSpec as P

F32 = jnp.float32
BF = jnp.bfloat16
MESH = pl.DeviceIdType.MESH
EPS = 1e-05
ADAPTER = 8.0
NEG = -1e30
LOG2E = 1.4426950408889634
LN2 = 0.6931471805599453
HEAD = 64
PAIR = 128
NN = (((1,), (0,)), ((), ()))
NT = (((1,), (1,)), ((), ()))
TN = (((0,), (0,)), ((), ()))


def dot(a, b, dims=NN):
    return lax.dot_general(a, b, dims, preferred_element_type=F32)


def row(ref):
    return ref[...].astype(F32).reshape(1, ref.shape[0])


def places():
    batch = lax.axis_index("batch")
    z = lax.axis_index("blk")
    core = lax.rem(batch, 2)
    base = batch - core
    outer = lax.rem(core + z, 2)
    edge = 1 - lax.rem((z + 1) // 2, 2)
    low, high = 1 - outer, 2 + outer
    hosts = [(base + lax.rem(i + edge, 2), 2 * core + i) for i in (0, 1)]
    homes = [(base + z // 2, low), (base + z // 2, high)]
    mate = (base + 1 - core, z)
    return dict(
        batch=batch, z=z, core=core, outer=outer, low=low, high=high,
        hosts=hosts, homes=homes, mate=mate,
    )


def greet(devices):
    barrier = pltpu.get_barrier_semaphore()
    for device in devices:
        pl.semaphore_signal(barrier, inc=1, device_id=device, device_id_type=MESH)
    pl.semaphore_wait(barrier, len(devices))


def remote(src, dst, send, recv, device):
    return pltpu.make_async_remote_copy(
        src_ref=src, dst_ref=dst, send_sem=send, recv_sem=recv,
        device_id=device, device_id_type=MESH,
    )


def norm_stats(x):
    center = x - jnp.mean(x, -1, keepdims=True)
    inverse = lax.rsqrt(jnp.mean(center * center, -1, keepdims=True) + EPS)
    return center * inverse, inverse


def norm_back(upstream, normed, inverse, gain):
    scaled = upstream * gain
    return inverse * (
        scaled
        - jnp.mean(scaled, -1, keepdims=True)
        - normed * jnp.mean(scaled * normed, -1, keepdims=True)
    )


def mask_bias(starts, key_span, query_span, span):
    key_pos = lax.broadcasted_iota(jnp.int32, (span, 1), 0) + key_span * span
    query_pos = lax.broadcasted_iota(jnp.int32, (1, span), 1) + query_span * span
    key_doc = jnp.zeros((span, 1), jnp.int32)
    query_doc = jnp.zeros((1, span), jnp.int32)
    for j in range(starts.shape[1]):
        start = starts[0:1, j : j + 1]
        key_doc = key_doc + (key_pos >= start).astype(jnp.int32)
        query_doc = query_doc + (query_pos >= start).astype(jnp.int32)
    allowed = (key_doc == query_doc) & (key_pos <= query_pos)
    return jnp.where(allowed, 0.0, NEG)


def half_rows(x, head):
    part = x[HEAD * head : HEAD * head + HEAD]
    zero = jnp.zeros_like(part)
    return jnp.concatenate([part, zero] if head == 0 else [zero, part], 0)


def half_lanes(x, head):
    lane = lax.broadcasted_iota(jnp.int32, x.shape, 1)
    keep = (lane < HEAD) if head == 0 else (lane >= HEAD)
    return jnp.where(keep, x, jnp.zeros_like(x))


def fused_kernel(
    rounds,
    tok, og, wqkv, wo_h, fc_h, proj_h, starts, gain, shift, qkv_bias, out_bias, gain2, shift2,
    fc_bias, proj_bias, down_q, up_q, down_v, up_v,
    out_o, tg_o, sums_o, e_h,
    tokin, ogin, wf, wo, fcb, pjb, n1, n2, qn, kn, vn, qp, vt, sc, ee, bias, ot, on, rl,
    resid, acc, slope, outst, dk, dv, dopc, don, qm, dss, part, part_in, tg, ar, ar_in, z_all, total, starts_in,
    tok_s, tok_r, og_s, og_r, ex_s, ex_r, st_sem, w_sem, fc_sem, pj_sem, e_sem,
    out_s, out_r, tg_s, tg_r, px_s, px_r, ar_s, ar_r, z_s, z_r, all_s, all_r, sent,
):
    at = places()
    z, core, outer = at["z"], at["core"], at["outer"]
    low, high, mate, batch = at["low"], at["high"], at["mate"], at["batch"]
    span, width = tokin.shape[1], tokin.shape[2]
    pairs_n = qn.shape[0]
    blocks = width // 256
    chunks, chunk = slope.shape[0], slope.shape[2]
    peers = []
    for distance in rounds:
        bit = lax.rem(batch // distance, 2)
        peers.append((batch + distance - 2 * distance * bit, z))
    depth = z_all.shape[0]
    z_peers = [(batch, lax.rem(z + d, depth)) for d in range(1, depth)]
    beside = (batch, z + 1 - 2 * lax.rem(z, 2))

    load_w = pltpu.make_async_copy(wqkv, wf, w_sem.at[0])
    load_w.start()
    greet(at["hosts"] + at["homes"] + [mate] + peers + z_peers)
    tok_send = [
        remote(tok.at[i], tokin.at[z // 2], tok_s.at[i], tok_r.at[z // 2], at["hosts"][i])
        for i in (0, 1)
    ]
    for copy in tok_send:
        copy.start()
    starts_copy = remote(starts, starts_in, st_sem.at[0], st_sem.at[1], mate)
    starts_copy.start()

    def load_mlp(c):
        slot = lax.rem(c, 2)
        here = pl.ds(pl.multiple_of(c * chunk, chunk), chunk)
        return (
            pltpu.make_async_copy(fc_h.at[:, here], fcb.at[slot], fc_sem.at[slot]),
            pltpu.make_async_copy(proj_h.at[here, :], pjb.at[slot], pj_sem.at[slot]),
        )

    load_w.wait()
    load_o = pltpu.make_async_copy(wo_h, wo, w_sem.at[0])
    load_o.start()
    for part_w, down, up in ((0, down_q, up_q), (2, down_v, up_v)):

        @pl.loop(0, blocks)
        def _(c):
            col = pl.ds(pl.multiple_of(part_w * width + c * 256, 256), 256)
            here = pl.ds(pl.multiple_of(c * 256, 256), 256)
            extra = dot(down[...], up[:, here], TN)
            wf[:, col] = (wf[:, col].astype(F32) + ADAPTER * extra).astype(BF)

    starts_copy.wait()
    mine = (z // 2 == core).astype(jnp.int32)
    both = starts[...] * mine + starts_in[...] * (1 - mine)
    second = lax.rem(z, 2)
    chosen = both[0:1] * (1 - second) + both[1:2] * second
    first_remote = 1 - low
    key_spans = (low, high, low, first_remote, first_remote + outer)
    query_spans = (low, high, high, low + outer * (high - low), high)
    for j in range(5):
        bias[j] = mask_bias(chosen, key_spans[j], query_spans[j], span)

    def exchange(s, c):
        here = pl.ds(2 * c, 2)
        return [
            remote(ref.at[here, s], ref.at[here, 2 + s], ex_s.at[s, c, t], ex_r.at[s, c, t], mate)
            for t, ref in enumerate((kn, vn))
        ]

    for turn in (0, 1):
        s = z // 2 if turn == 0 else 1 - z // 2
        remote(tokin.at[s], tokin.at[s], tok_s.at[0], tok_r.at[s], mate).wait_recv()
        if turn == 1:
            for copy in tok_send:
                copy.wait_send()
            pl.semaphore_signal(sent, inc=1, device_id=beside, device_id_type=MESH)
            pl.semaphore_wait(sent, 1)
            og_send = [
                remote(og.at[i], ogin.at[z // 2], og_s.at[i], og_r.at[z // 2], at["hosts"][i])
                for i in (0, 1)
            ]
            for copy in og_send:
                copy.start()
            for c in (0, 1):
                for copy in load_mlp(c):
                    copy.start()
        normed, _ = norm_stats(tokin[s].astype(F32))
        n1[s] = (normed * row(gain) + row(shift)).astype(BF)

        @pl.loop(0, blocks)
        def _(c):
            for which, store, scale in ((1, kn, None), (2, vn, None), (0, qn, LOG2E / HEAD**0.5)):
                col = pl.ds(pl.multiple_of(which * width + c * 256, 256), 256)
                made = dot(n1[s], wf[:, col]) + qkv_bias[col].astype(F32).reshape(1, 256)
                if scale is not None:
                    made = made * scale
                made = made.astype(BF)
                for t in (0, 1):
                    store[2 * c + t, s] = made[:, t * PAIR : (t + 1) * PAIR]
                if which == 2:
                    for copy in exchange(s, c):
                        copy.start()

    outer_f = outer.astype(F32)
    inner_f = 1.0 - outer_f
    ones = jnp.ones((16, span), BF)
    key_at = (0, 1, 0, 2, 2 + outer)
    query_at = (0, 1, 1, outer, 1)

    def save_e(hp):
        slot = lax.rem(hp, 2)
        return pltpu.make_async_copy(ee.at[slot], e_h.at[hp], e_sem.at[slot])

    def load_e(hp):
        slot = lax.rem(hp, 2)
        return pltpu.make_async_copy(e_h.at[hp], ee.at[slot], e_sem.at[slot])

    @pl.loop(0, blocks)
    def _(c):
        for s in (0, 1):
            for copy in exchange(s, c):
                copy.wait()

    @pl.loop(0, pairs_n)
    def _(hp):
        slot = lax.rem(hp, 2)

        @pl.when(hp >= 2)
        def _():
            save_e(hp - 2).wait()

        for s in (0, 1):
            q_t = qn[hp, s].T
            for head in (0, 1):
                qp[head, s] = half_rows(q_t, head)
        for kb in range(4):
            vt[kb] = vn[hp, kb].T
        tops = []
        for head in (0, 1):
            tops.append([])
            for j in range(5):
                s_j = dot(kn[hp, key_at[j]], qp[head, query_at[j]]) + bias[j]
                sc[head, j] = s_j
                tops[head].append(jnp.max(s_j, 0, keepdims=True))
        for head in (0, 1):
            m0, m1, m2, m3, m4 = tops[head]
            top_low = jnp.maximum(m0, m3 * inner_f + NEG * outer_f)
            top_high = jnp.maximum(
                jnp.maximum(m1, m2), jnp.maximum(m4, m3 * outer_f + NEG * inner_f)
            )
            top_x = top_high * outer_f + top_low * inner_f
            mixed = []
            for j, top in enumerate((top_low, top_high, top_high, top_x, top_high)):
                e_j = jnp.exp2(sc[head, j] - top).astype(BF)
                ee[slot, head, j] = e_j
                v_j = jnp.concatenate(
                    [vt[key_at[j], HEAD * head : HEAD * head + HEAD], ones], 0
                )
                mixed.append(dot(v_j, e_j))
            sums = (
                mixed[0] + mixed[3] * inner_f,
                mixed[1] + mixed[2] + mixed[4] + mixed[3] * outer_f,
            )
            for s in (0, 1):
                inv = 1.0 / sums[s][HEAD : HEAD + 1]
                rl[hp, 2 * head + s : 2 * head + s + 1, :] = inv
                ot[hp, s, HEAD * head : HEAD * head + HEAD, :] = (sums[s][:HEAD] * inv).astype(BF)
        for s in (0, 1):
            on[s, :, pl.ds(pl.multiple_of(hp * PAIR, PAIR), PAIR)] = ot[hp, s].T
        save_e(hp).start()

    load_o.wait()
    for s in (0, 1):
        here = pl.ds(s * span, span)
        r = tokin[s].astype(F32) + (dot(on[s], wo[...]) + row(out_bias))
        resid[here] = r
        normed, _ = norm_stats(r)
        n2[here] = (normed * row(gain2) + row(shift2)).astype(BF)
        acc[here] = r + row(proj_bias)

    @pl.loop(0, chunks)
    def _(c):
        slot = lax.rem(c, 2)
        for copy in load_mlp(c):
            copy.wait()
        part_b = fc_bias[pl.ds(pl.multiple_of(c * chunk, chunk), chunk)]
        x = dot(n2[...], fcb[slot]) + part_b.astype(F32).reshape(1, chunk)
        sq = x * x
        half = 0.5 * jnp.tanh(x * ((GELU * 0.044715) * sq + GELU)) + 0.5
        act = x * half
        rise = half + (act - act * half) * ((6.0 * GELU * 0.044715) * sq + 2.0 * GELU)
        slope[c] = rise.astype(BF)
        acc[...] += dot(act.astype(BF), pjb[slot])

        @pl.when(c + 2 < chunks)
        def _():
            for copy in load_mlp(c + 2):
                copy.start()

    for s in (0, 1):
        outst[s] = acc[pl.ds(s * span, span)].astype(BF)
    for i in (0, 1):
        og_send[i].wait_send()
    out_send = [
        remote(
            outst.at[i], out_o.at[lax.rem(z, 2)], out_s.at[i], out_r.at[lax.rem(z, 2)], at["homes"][i]
        )
        for i in (0, 1)
    ]
    for copy in out_send:
        copy.start()
    acc[...] = jnp.zeros_like(acc)
    for hp in (pairs_n - 2, pairs_n - 1):
        save_e(hp).wait()
    for i in (0, 1):
        remote(ogin.at[i], ogin.at[i], og_s.at[i], og_r.at[i], mate).wait_recv()

    @pl.loop(0, chunks)
    def _(t):
        c = chunks - 1 - t
        slot = lax.rem(c, 2)

        @pl.when(t >= 2)
        def _():
            for copy in load_mlp(c):
                copy.wait()

        og_flat = ogin[...].reshape(2 * span, width)
        gh = (dot(og_flat, pjb[slot], NT) * slope[c].astype(F32)).astype(BF)
        acc[...] += dot(gh, fcb[slot], NT)

        @pl.when(c >= 2)
        def _():
            for copy in load_mlp(c - 2):
                copy.start()

    for s in (0, 1):
        here = pl.ds(s * span, span)
        normed, inverse = norm_stats(resid[here])
        g = ogin[s].astype(F32) + norm_back(acc[here], normed, inverse, row(gain2))
        resid[here] = g
        n2[here] = dot(g.astype(BF), wo[...], NT).astype(BF)

    def part_send(hp):
        return remote(part.at[hp], part_in.at[hp], px_s.at[hp], px_r.at[hp], mate)

    @pl.loop(0, pairs_n)
    def _(turn):
        hp = pairs_n - 1 - turn
        slot = lax.rem(hp, 2)
        lanes = pl.ds(pl.multiple_of(hp * PAIR, PAIR), PAIR)

        @pl.when(turn >= 2)
        def _():
            load_e(hp).wait()

        delta = [[None, None], [None, None]]
        for s in (0, 1):
            da_t = n2[s * span : (s + 1) * span, lanes].astype(F32).T
            prod = da_t * ot[hp, s].astype(F32)
            scaled = []
            for head in (0, 1):
                rows_h = slice(HEAD * head, HEAD * head + HEAD)
                inv = rl[hp, 2 * head + s : 2 * head + s + 1, :]
                delta[head][s] = jnp.sum(prod[rows_h], 0, keepdims=True) * inv
                scaled.append(da_t[rows_h] * inv)
            scaled = jnp.concatenate(scaled, 0).astype(BF)
            natural = scaled.T
            q_n = qn[hp, s]
            for head in (0, 1):
                cols = slice(head * span, (head + 1) * span)
                dopc[s, :, cols] = half_rows(scaled, head)
                don[s, cols] = half_lanes(natural, head)
                qm[s, cols] = half_lanes(q_n, head)
        for kb in range(4):
            vt[kb] = kn[hp, kb].T
        for j in range(5):
            for head in (0, 1):
                cols = slice(head * span, (head + 1) * span)
                d_low, d_high = delta[head]
                d_j = (d_low, d_high, d_high, d_high * outer_f + d_low * inner_f, d_high)[j]
                dp = dot(vn[hp, key_at[j]], dopc[query_at[j], :, cols])
                dss[j, :, cols] = (ee[slot, head, j].astype(F32) * (dp - d_j)).astype(BF)
        dk_parts, dv_parts, grads = [], [], [[], []]
        for j in range(5):
            e_pair = jnp.concatenate([ee[slot, 0, j], ee[slot, 1, j]], 1)
            dv_parts.append(dot(e_pair, don[query_at[j]]))
        for j in range(5):
            for head in (0, 1):
                cols = slice(head * span, (head + 1) * span)
                grads[head].append(
                    dot(vt[key_at[j], HEAD * head : HEAD * head + HEAD], dss[j, :, cols])
                )
            dk_parts.append(dot(dss[j], qm[query_at[j]]))
        for t, parts, scale in ((0, dk_parts, LN2), (1, dv_parts, 1.0)):
            store = (dk, dv)[t]
            store[0, :, lanes] = ((parts[0] + parts[2]) * scale).astype(BF)
            store[1, :, lanes] = (parts[1] * scale).astype(BF)
            part[hp, t, 0] = ((parts[3] + parts[4] * inner_f) * scale).astype(BF)
            part[hp, t, 1] = (parts[4] * (outer_f * scale)).astype(BF)
        part_send(hp).start()
        for s in (0, 1):
            rows_t = []
            for head in (0, 1):
                g = grads[head]
                if s == 0:
                    total = g[0] + g[3] * inner_f
                else:
                    total = g[1] + g[2] + g[4] + g[3] * outer_f
                rows_t.append(total * (1.0 / HEAD**0.5))
            on[s, :, lanes] = jnp.concatenate(rows_t, 0).astype(BF).T

        @pl.when(hp >= 2)
        def _():
            load_e(hp - 2).start()

    dq = on

    @pl.loop(0, pairs_n)
    def _(turn):
        hp = pairs_n - 1 - turn
        lanes = pl.ds(pl.multiple_of(hp * PAIR, PAIR), PAIR)
        part_send(hp).wait()
        for t, store in ((0, dk), (1, dv)):
            for s in (0, 1):
                own = store[s, :, lanes].astype(F32)
                store[s, :, lanes] = (own + part_in[hp, t, s].astype(F32)).astype(BF)

    cross, near = 1 - z // 2, z // 2
    piece = span // 4

    def tg_copy(s, k):
        rows_k = pl.ds(k * piece, piece)
        home = (batch - core + z // 2, low + s * (high - low))
        return remote(
            tg.at[s, rows_k], tg_o.at[lax.rem(z, 2), rows_k],
            tg_s.at[s, k], tg_r.at[lax.rem(z, 2), k], home,
        )

    pieces = ar.shape[0]
    group = lax.rem(batch, pieces)

    def batch_round(r):
        return remote(ar, ar_in.at[r], ar_s.at[r], ar_r.at[r], peers[r])

    def z_send(d):
        return remote(ar.at[group], z_all.at[z], z_s.at[d], z_r.at[z], z_peers[d])

    def share_round(r):
        size = 2**r
        held = pl.ds(group // size * size, size)
        return remote(total.at[held], total.at[held], all_s.at[r], all_r.at[r], peers[r])

    def share_wait(r):
        size = 2**r
        other = group // size
        other = other + 1 - 2 * lax.rem(other, 2)
        held = pl.ds(other * size, size)
        remote(total.at[held], total.at[held], all_s.at[r], all_r.at[r], peers[r]).wait_recv()

    def project_back(s):
        @pl.loop(0, blocks)
        def _(c):
            here = pl.ds(pl.multiple_of(c * 256, 256), 256)
            total = dot(dq[s], wf[here, 0:width], NT)
            total += dot(dk[s], wf[here, width : 2 * width], NT)
            total += dot(dv[s], wf[here, 2 * width : 3 * width], NT)
            acc[0:span, here] = total

        normed, inverse = norm_stats(tokin[s].astype(F32))
        rows_s = pl.ds(pl.multiple_of(s * span, span), span)
        tg[s] = (resid[rows_s] + norm_back(acc[0:span], normed, inverse, row(gain))).astype(BF)

    project_back(cross)
    for i in (0, 1):
        out_send[i].wait_send()
    for k in (0, 1):
        tg_copy(cross, k).start()
    for k, (grad, down, up) in enumerate(((dq, down_q, up_q), (dv, down_v, up_v))):
        up_total = down_total = 0.0
        for i in (0, 1):
            inner = dot(n1[i], down[...], NT).astype(BF)
            lift = dot(grad[i], up[...], NT).astype(BF)
            up_total = up_total + dot(inner, grad[i], TN)
            down_total = down_total + dot(lift, n1[i], TN)
        for c in range(pieces):
            lanes = slice(c * PAIR, (c + 1) * PAIR)
            ar[c, 8 * k : 8 * k + 4] = ADAPTER * up_total[:, lanes]
            ar[c, 8 * k + 4 : 8 * k + 8] = ADAPTER * down_total[:, lanes]
    batch_round(0).start()
    project_back(near)
    for r in range(len(peers)):
        if r > 0:
            batch_round(r).start()
        batch_round(r).wait()
        ar[...] += ar_in[r]
    for d in range(depth - 1):
        z_send(d).start()
    for k in (2, 3):
        tg_copy(cross, k).start()
    for k in range(4):
        tg_copy(near, k).start()
    z_all[z] = ar[group]
    for d in range(depth - 1):
        z_send(d).wait_send()
        from_z = lax.rem(z + depth - 1 - d, depth)
        remote(z_all.at[from_z], z_all.at[from_z], z_s.at[d], z_r.at[from_z], mate).wait_recv()
    summed = z_all[0]
    for d in range(1, depth):
        summed = summed + z_all[d]
    total[group] = summed
    for r in range(3):
        share_round(r).start()
        share_round(r).wait_send()
        share_wait(r)
    sums_o[...] = total[...]

    for i in (0, 1):
        remote(out_o.at[i], out_o.at[i], out_s.at[i], out_r.at[i], mate).wait_recv()
        for k in range(4):
            tg_copy(i, k).wait_send()
            landed = tg_o.at[i, pl.ds(k * piece, piece)]
            remote(landed, landed, tg_s.at[i, k], tg_r.at[i, k], mate).wait_recv()


def deliver_kernel(out_i, tg_i, sums, out_o, tg_o, down_q, up_q, down_v, up_v):
    out_o[...] = out_i[...]
    tg_o[...] = tg_i[...]
    for c in range(sums.shape[0]):
        lanes = slice(c * PAIR, (c + 1) * PAIR)
        for k, ref in enumerate((up_q, down_q, up_v, down_v)):
            ref[:, lanes] = sums[c, 4 * k : 4 * k + 4]


VMEM = pl.BlockSpec(memory_space=pltpu.VMEM)
ANY = pl.BlockSpec(memory_space=pl.ANY)
DMA = pltpu.SemaphoreType.DMA
LIMIT = 60 * 1024 * 1024
GELU = 0.7978845608028654


def on_device(
    tokens, doc_starts, attn_gain, attn_shift, qkv_weight, qkv_bias,
    query_down_factor, query_up_factor, value_down_factor, value_up_factor,
    out_weight, out_bias, mlp_gain, mlp_shift, fc_weight, fc_bias, proj_weight, proj_bias, out_grad,
):
    slots, span, width = tokens.shape
    hidden = fc_weight.shape[1]
    rank = query_down_factor.shape[1]
    pairs_n = width // PAIR
    chunk = 1024
    blocks = width // 256
    shape = jax.ShapeDtypeStruct
    two = (slots, span, width)
    flat = (2 * span, width)
    q_shape = (pairs_n, 2, span, PAIR)
    k_shape = (pairs_n, 4, span, PAIR)
    rounds = [2**r for r in range((lax.axis_size("batch") - 1).bit_length())]
    depth = lax.axis_size("blk")
    pieces = width // PAIR
    n_rounds = len(rounds)

    def fused(*refs):
        fused_kernel(rounds, *refs)

    bf = lambda *dims: pltpu.VMEM(dims, BF)
    f32 = lambda *dims: pltpu.VMEM(dims, F32)
    out_l, tg_l, sums, _ = pl.pallas_call(
        fused,
        out_shape=(
            shape(two, BF), shape(two, BF), shape((pieces, 16, PAIR), F32),
            shape((pairs_n, 2, 5, span, span), BF),
        ),
        in_specs=[ANY] * 6 + [VMEM] * 13,
        out_specs=(ANY, ANY, VMEM, ANY),
        scratch_shapes=[
            bf(*two), bf(*two), bf(width, 3 * width), bf(width, width),
            bf(2, width, chunk), bf(2, chunk, width), bf(*two), bf(*flat),
            bf(*q_shape), bf(*k_shape), bf(*k_shape),
            bf(2, 2, PAIR, span), bf(4, PAIR, span),
            f32(2, 5, span, span), bf(2, 2, 5, span, span), f32(5, span, span),
            bf(pairs_n, 2, PAIR, span), bf(*two), f32(pairs_n, 8, span),
            f32(*flat), f32(*flat), bf(hidden // chunk, 2 * span, chunk), bf(*two),
            bf(*two), bf(*two),
            bf(2, PAIR, 2 * span), bf(2, 2 * span, PAIR), bf(2, 2 * span, PAIR), bf(5, span, 2 * span),
            bf(pairs_n, 2, 2, span, PAIR), bf(pairs_n, 2, 2, span, PAIR), bf(*two),
            f32(pieces, 16, PAIR), f32(n_rounds, pieces, 16, PAIR), f32(depth, 16, PAIR), f32(pieces, 16, PAIR),
            pltpu.VMEM(doc_starts.shape, jnp.int32),
            DMA((2,)), DMA((2,)), DMA((2,)), DMA((2,)),
            DMA((2, blocks, 2)), DMA((2, blocks, 2)), DMA((2,)), DMA((1,)), DMA((2,)), DMA((2,)), DMA((2,)),
            DMA((2,)), DMA((2,)), DMA((2, 4)), DMA((2, 4)),
            DMA((pairs_n,)), DMA((pairs_n,)), DMA((n_rounds,)), DMA((n_rounds,)),
            DMA((depth - 1,)), DMA((depth,)), DMA((3,)), DMA((3,)), pltpu.SemaphoreType.REGULAR,
        ],
        compiler_params=pltpu.CompilerParams(
            collective_id=0, has_side_effects=True, vmem_limit_bytes=LIMIT
        ),
    )(
        tokens, out_grad, qkv_weight, out_weight, fc_weight, proj_weight, doc_starts,
        attn_gain, attn_shift, qkv_bias, out_bias, mlp_gain, mlp_shift, fc_bias, proj_bias,
        query_down_factor.T, query_up_factor, value_down_factor.T, value_up_factor,
    )

    small = shape((rank, width), F32)
    block = pl.BlockSpec((1, span, width), lambda i: (i, 0, 0))
    whole = lambda *dims: pl.BlockSpec(dims, lambda i: (0,) * len(dims))
    out, tg, down_q, up_q, down_v, up_v = pl.pallas_call(
        deliver_kernel,
        grid=(slots,),
        out_shape=(shape(two, BF), shape(two, BF), small, small, small, small),
        in_specs=[block, block, whole(pieces, 16, PAIR)],
        out_specs=(block, block) + (whole(rank, width),) * 4,
    )(out_l, tg_l, sums)
    return out, tg, down_q.T, up_q, down_v.T, up_v


def solution(mesh):
    rows = P("batch", "blk", None)
    return jax.shard_map(
        on_device,
        mesh=mesh,
        in_specs=(rows, P("batch", None)) + (P(),) * 16 + (rows,),
        out_specs=(rows, rows, P(), P(), P(), P()),
        check_vma=False,
    )
```

```python
import jax
import jax.numpy as jnp
from jax import lax
from jax.experimental import pallas as pl
from jax.experimental.pallas import tpu as pltpu
from jax.sharding import PartitionSpec as P

F32 = jnp.float32
BF = jnp.bfloat16
MESH = pl.DeviceIdType.MESH
EPS = 1e-05
ADAPTER = 8.0
NEG = -1e30
LOG2E = 1.4426950408889634
LN2 = 0.6931471805599453
HEAD = 64
PAIR = 128
NN = (((1,), (0,)), ((), ()))
NT = (((1,), (1,)), ((), ()))
TN = (((0,), (0,)), ((), ()))


def dot(a, b, dims=NN):
    return lax.dot_general(a, b, dims, preferred_element_type=F32)


def row(ref):
    return ref[...].astype(F32).reshape(1, ref.shape[0])


def places():
    batch = lax.axis_index("batch")
    z = lax.axis_index("blk")
    core = lax.rem(batch, 2)
    base = batch - core
    outer = lax.rem(core + z, 2)
    edge = 1 - lax.rem((z + 1) // 2, 2)
    low, high = 1 - outer, 2 + outer
    hosts = [(base + lax.rem(i + edge, 2), 2 * core + i) for i in (0, 1)]
    homes = [(base + z // 2, low), (base + z // 2, high)]
    mate = (base + 1 - core, z)
    return dict(
        batch=batch, z=z, core=core, outer=outer, low=low, high=high,
        hosts=hosts, homes=homes, mate=mate,
    )


def greet(devices):
    barrier = pltpu.get_barrier_semaphore()
    for device in devices:
        pl.semaphore_signal(barrier, inc=1, device_id=device, device_id_type=MESH)
    pl.semaphore_wait(barrier, len(devices))


def remote(src, dst, send, recv, device):
    return pltpu.make_async_remote_copy(
        src_ref=src, dst_ref=dst, send_sem=send, recv_sem=recv,
        device_id=device, device_id_type=MESH,
    )


def norm_stats(x):
    center = x - jnp.mean(x, -1, keepdims=True)
    inverse = lax.rsqrt(jnp.mean(center * center, -1, keepdims=True) + EPS)
    return center * inverse, inverse


def norm_back(upstream, normed, inverse, gain):
    scaled = upstream * gain
    return inverse * (
        scaled
        - jnp.mean(scaled, -1, keepdims=True)
        - normed * jnp.mean(scaled * normed, -1, keepdims=True)
    )


def mask_bias(starts, key_span, query_span, span):
    key_pos = lax.broadcasted_iota(jnp.int32, (span, 1), 0) + key_span * span
    query_pos = lax.broadcasted_iota(jnp.int32, (1, span), 1) + query_span * span
    key_doc = jnp.zeros((span, 1), jnp.int32)
    query_doc = jnp.zeros((1, span), jnp.int32)
    for j in range(starts.shape[1]):
        start = starts[0:1, j : j + 1]
        key_doc = key_doc + (key_pos >= start).astype(jnp.int32)
        query_doc = query_doc + (query_pos >= start).astype(jnp.int32)
    allowed = (key_doc == query_doc) & (key_pos <= query_pos)
    return jnp.where(allowed, 0.0, NEG)


def half_rows(x, head):
    part = x[HEAD * head : HEAD * head + HEAD]
    zero = jnp.zeros_like(part)
    return jnp.concatenate([part, zero] if head == 0 else [zero, part], 0)


def half_lanes(x, head):
    lane = lax.broadcasted_iota(jnp.int32, x.shape, 1)
    keep = (lane < HEAD) if head == 0 else (lane >= HEAD)
    return jnp.where(keep, x, jnp.zeros_like(x))


def fused_kernel(
    rounds,
    tok, og, wqkv, wo_h, fc_h, proj_h, starts, gain, shift, qkv_bias, out_bias, gain2, shift2,
    fc_bias, proj_bias, down_q, up_q, down_v, up_v,
    out_o, tg_o, sums_o, e_h,
    tokin, ogin, wf, wo, fcb, pjb, n1, n2, qn, kn, vn, qp, vt, sc, ee, bias, ot, on, rl,
    resid, acc, slope, outst, dv, dopc, don, qm, dss, part, part_in, ar, ar_in, z_all, total, starts_in,
    tok_s, tok_r, og_s, og_r, ex_s, ex_r, st_sem, w_sem, fc_sem, pj_sem, e_sem,
    out_s, out_r, tg_s, tg_r, px_s, px_r, ar_s, ar_r, z_s, z_r, all_s, all_r, sent,
):
    at = places()
    z, core, outer = at["z"], at["core"], at["outer"]
    low, high, mate, batch = at["low"], at["high"], at["mate"], at["batch"]
    span, width = tokin.shape[1], tokin.shape[2]
    pairs_n = qn.shape[0]
    blocks = width // 256
    chunks, chunk = slope.shape[0], slope.shape[2]
    peers = []
    for distance in rounds:
        bit = lax.rem(batch // distance, 2)
        peers.append((batch + distance - 2 * distance * bit, z))
    depth = z_all.shape[0]
    z_peers = [(batch, lax.rem(z + d, depth)) for d in range(1, depth)]
    beside = (batch, z + 1 - 2 * lax.rem(z, 2))

    load_w = pltpu.make_async_copy(wqkv, wf, w_sem.at[0])
    load_w.start()
    greet(at["hosts"] + at["homes"] + [mate] + peers + z_peers)
    tok_send = [
        remote(tok.at[i], tokin.at[z // 2], tok_s.at[i], tok_r.at[z // 2], at["hosts"][i])
        for i in (0, 1)
    ]
    for copy in tok_send:
        copy.start()
    starts_copy = remote(starts, starts_in, st_sem.at[0], st_sem.at[1], mate)
    starts_copy.start()

    def load_mlp(c):
        slot = lax.rem(c, 2)
        here = pl.ds(pl.multiple_of(c * chunk, chunk), chunk)
        return (
            pltpu.make_async_copy(fc_h.at[:, here], fcb.at[slot], fc_sem.at[slot]),
            pltpu.make_async_copy(proj_h.at[here, :], pjb.at[slot], pj_sem.at[slot]),
        )

    load_w.wait()
    load_o = pltpu.make_async_copy(wo_h, wo, w_sem.at[0])
    load_o.start()
    for part_w, down, up in ((0, down_q, up_q), (2, down_v, up_v)):

        @pl.loop(0, blocks)
        def _(c):
            col = pl.ds(pl.multiple_of(part_w * width + c * 256, 256), 256)
            here = pl.ds(pl.multiple_of(c * 256, 256), 256)
            extra = dot(down[...], up[:, here], TN)
            wf[:, col] = (wf[:, col].astype(F32) + ADAPTER * extra).astype(BF)

    starts_copy.wait()
    mine = (z // 2 == core).astype(jnp.int32)
    both = starts[...] * mine + starts_in[...] * (1 - mine)
    second = lax.rem(z, 2)
    chosen = both[0:1] * (1 - second) + both[1:2] * second
    first_remote = 1 - low
    key_spans = (low, high, low, first_remote, first_remote + outer)
    query_spans = (low, high, high, low + outer * (high - low), high)
    for j in range(5):
        bias[j] = mask_bias(chosen, key_spans[j], query_spans[j], span)

    def exchange(s, c):
        here = pl.ds(2 * c, 2)
        return [
            remote(ref.at[here, s], ref.at[here, 2 + s], ex_s.at[s, c, t], ex_r.at[s, c, t], mate)
            for t, ref in enumerate((kn, vn))
        ]

    for turn in (0, 1):
        s = z // 2 if turn == 0 else 1 - z // 2
        remote(tokin.at[s], tokin.at[s], tok_s.at[0], tok_r.at[s], mate).wait_recv()
        if turn == 1:
            for copy in tok_send:
                copy.wait_send()
            pl.semaphore_signal(sent, inc=1, device_id=beside, device_id_type=MESH)
            pl.semaphore_wait(sent, 1)
            og_send = [
                remote(og.at[i], ogin.at[z // 2], og_s.at[i], og_r.at[z // 2], at["hosts"][i])
                for i in (0, 1)
            ]
            for copy in og_send:
                copy.start()
            for c in (0, 1):
                for copy in load_mlp(c):
                    copy.start()
        normed, _ = norm_stats(tokin[s].astype(F32))
        n1[s] = (normed * row(gain) + row(shift)).astype(BF)

        @pl.loop(0, blocks)
        def _(c):
            for which, store, scale in ((1, kn, None), (2, vn, None), (0, qn, LOG2E / HEAD**0.5)):
                col = pl.ds(pl.multiple_of(which * width + c * 256, 256), 256)
                made = dot(n1[s], wf[:, col]) + qkv_bias[col].astype(F32).reshape(1, 256)
                if scale is not None:
                    made = made * scale
                made = made.astype(BF)
                for t in (0, 1):
                    store[2 * c + t, s] = made[:, t * PAIR : (t + 1) * PAIR]
                if which == 2:
                    for copy in exchange(s, c):
                        copy.start()

    outer_f = outer.astype(F32)
    inner_f = 1.0 - outer_f
    ones = jnp.ones((16, span), BF)
    key_at = (0, 1, 0, 2, 2 + outer)
    query_at = (0, 1, 1, outer, 1)

    kept = ee.shape[0]

    def save_e(hp):
        slot = lax.rem(hp, kept)
        return pltpu.make_async_copy(ee.at[slot], e_h.at[hp], e_sem.at[slot])

    def load_e(hp):
        slot = lax.rem(hp, kept)
        return pltpu.make_async_copy(e_h.at[hp], ee.at[slot], e_sem.at[slot])

    def attend(hp):
        slot = lax.rem(hp, kept)
        for s in (0, 1):
            q_t = qn[hp, s].T
            for head in (0, 1):
                qp[head, s] = half_rows(q_t, head)
        for kb in range(4):
            vt[kb] = vn[hp, kb].T
        tops = []
        for head in (0, 1):
            tops.append([])
            for j in range(5):
                s_j = dot(kn[hp, key_at[j]], qp[head, query_at[j]]) + bias[j]
                sc[head, j] = s_j
                tops[head].append(jnp.max(s_j, 0, keepdims=True))
        for head in (0, 1):
            m0, m1, m2, m3, m4 = tops[head]
            top_low = jnp.maximum(m0, m3 * inner_f + NEG * outer_f)
            top_high = jnp.maximum(
                jnp.maximum(m1, m2), jnp.maximum(m4, m3 * outer_f + NEG * inner_f)
            )
            top_x = top_high * outer_f + top_low * inner_f
            mixed = []
            for j, top in enumerate((top_low, top_high, top_high, top_x, top_high)):
                e_j = jnp.exp2(sc[head, j] - top).astype(BF)
                ee[slot, head, j] = e_j
                v_j = jnp.concatenate(
                    [vt[key_at[j], HEAD * head : HEAD * head + HEAD], ones], 0
                )
                mixed.append(dot(v_j, e_j))
            sums = (
                mixed[0] + mixed[3] * inner_f,
                mixed[1] + mixed[2] + mixed[4] + mixed[3] * outer_f,
            )
            for s in (0, 1):
                inv = 1.0 / sums[s][HEAD : HEAD + 1]
                rl[hp, 2 * head + s : 2 * head + s + 1, :] = inv
                ot[hp, s, HEAD * head : HEAD * head + HEAD, :] = (sums[s][:HEAD] * inv).astype(BF)
        for s in (0, 1):
            on[s, :, pl.ds(pl.multiple_of(hp * PAIR, PAIR), PAIR)] = ot[hp, s].T
        @pl.when(hp + kept < pairs_n)
        def _():
            save_e(hp).start()

    @pl.loop(0, pairs_n // 2)
    def _(step):
        for s in (0, 1):
            for copy in exchange(s, step):
                copy.wait()

        @pl.when(2 * step >= kept)
        def _():
            for t in (0, 1):
                save_e(2 * step + t - kept).wait()

        for t in (0, 1):
            attend(2 * step + t)

    load_o.wait()
    for s in (0, 1):
        here = pl.ds(s * span, span)
        r = tokin[s].astype(F32) + (dot(on[s], wo[...]) + row(out_bias))
        resid[here] = r
        normed, _ = norm_stats(r)
        n2[s] = (normed * row(gain2) + row(shift2)).astype(BF)
        acc[here] = r + row(proj_bias)

    @pl.loop(0, chunks)
    def _(c):
        slot = lax.rem(c, 2)
        for copy in load_mlp(c):
            copy.wait()
        part_b = fc_bias[pl.ds(pl.multiple_of(c * chunk, chunk), chunk)]
        x = dot(n2[...].reshape(2 * span, width), fcb[slot]) + part_b.astype(F32).reshape(1, chunk)
        sq = x * x
        half = 0.5 * jnp.tanh(x * ((GELU * 0.044715) * sq + GELU)) + 0.5
        act = x * half
        rise = half + (act - act * half) * ((6.0 * GELU * 0.044715) * sq + 2.0 * GELU)
        slope[c] = rise.astype(BF)
        acc[...] += dot(act.astype(BF), pjb[slot])

        @pl.when(c + 2 < chunks)
        def _():
            for copy in load_mlp(c + 2):
                copy.start()

    for s in (0, 1):
        outst[s] = acc[pl.ds(s * span, span)].astype(BF)
    for i in (0, 1):
        og_send[i].wait_send()
    out_send = [
        remote(
            outst.at[i], out_o.at[lax.rem(z, 2)], out_s.at[i], out_r.at[lax.rem(z, 2)], at["homes"][i]
        )
        for i in (0, 1)
    ]
    for copy in out_send:
        copy.start()
    acc[...] = jnp.zeros_like(acc)
    for i in (0, 1):
        remote(ogin.at[i], ogin.at[i], og_s.at[i], og_r.at[i], mate).wait_recv()

    @pl.loop(0, chunks)
    def _(t):
        c = chunks - 1 - t
        slot = lax.rem(c, 2)

        @pl.when(t >= 2)
        def _():
            for copy in load_mlp(c):
                copy.wait()

        og_flat = ogin[...].reshape(2 * span, width)
        gh = (dot(og_flat, pjb[slot], NT) * slope[c].astype(F32)).astype(BF)
        acc[...] += dot(gh, fcb[slot], NT)

        @pl.when(c >= 2)
        def _():
            for copy in load_mlp(c - 2):
                copy.start()

    for s in (0, 1):
        here = pl.ds(s * span, span)
        normed, inverse = norm_stats(resid[here])
        g = ogin[s].astype(F32) + norm_back(acc[here], normed, inverse, row(gain2))
        resid[here] = g
        n2[s] = dot(g.astype(BF), wo[...], NT).astype(BF)

    dk = ogin

    def part_send(hp):
        return remote(part.at[hp], part_in.at[hp], px_s.at[hp], px_r.at[hp], mate)

    def attend_back(hp):
        slot = lax.rem(hp, kept)
        lanes = pl.ds(pl.multiple_of(hp * PAIR, PAIR), PAIR)
        delta = [[None, None], [None, None]]
        for s in (0, 1):
            da_t = n2[s, :, lanes].astype(F32).T
            prod = da_t * ot[hp, s].astype(F32)
            scaled = []
            for head in (0, 1):
                rows_h = slice(HEAD * head, HEAD * head + HEAD)
                inv = rl[hp, 2 * head + s : 2 * head + s + 1, :]
                delta[head][s] = jnp.sum(prod[rows_h], 0, keepdims=True) * inv
                scaled.append(da_t[rows_h] * inv)
            scaled = jnp.concatenate(scaled, 0).astype(BF)
            natural = scaled.T
            q_n = qn[hp, s]
            for head in (0, 1):
                cols = slice(head * span, (head + 1) * span)
                dopc[s, :, cols] = half_rows(scaled, head)
                don[s, cols] = half_lanes(natural, head)
                qm[s, cols] = half_lanes(q_n, head)
        for kb in range(4):
            vt[kb] = kn[hp, kb].T
        for j in range(5):
            for head in (0, 1):
                cols = slice(head * span, (head + 1) * span)
                d_low, d_high = delta[head]
                d_j = (d_low, d_high, d_high, d_high * outer_f + d_low * inner_f, d_high)[j]
                dp = dot(vn[hp, key_at[j]], dopc[query_at[j], :, cols])
                dss[j, :, cols] = (ee[slot, head, j].astype(F32) * (dp - d_j)).astype(BF)
        dk_parts, dv_parts, grads = [], [], [[], []]
        for j in range(5):
            e_pair = jnp.concatenate([ee[slot, 0, j], ee[slot, 1, j]], 1)
            dv_parts.append(dot(e_pair, don[query_at[j]]))
        for j in range(5):
            for head in (0, 1):
                cols = slice(head * span, (head + 1) * span)
                grads[head].append(
                    dot(vt[key_at[j], HEAD * head : HEAD * head + HEAD], dss[j, :, cols])
                )
            dk_parts.append(dot(dss[j], qm[query_at[j]]))
        for t, parts, scale in ((0, dk_parts, LN2), (1, dv_parts, 1.0)):
            store = (dk, dv)[t]
            store[0, :, lanes] = ((parts[0] + parts[2]) * scale).astype(BF)
            store[1, :, lanes] = (parts[1] * scale).astype(BF)
            part[hp, t, 0] = ((parts[3] + parts[4] * inner_f) * scale).astype(BF)
            part[hp, t, 1] = (parts[4] * (outer_f * scale)).astype(BF)
        part_send(hp).start()
        for s in (0, 1):
            rows_t = []
            for head in (0, 1):
                g = grads[head]
                if s == 0:
                    total = g[0] + g[3] * inner_f
                else:
                    total = g[1] + g[2] + g[4] + g[3] * outer_f
                rows_t.append(total * (1.0 / HEAD**0.5))
            on[s, :, lanes] = jnp.concatenate(rows_t, 0).astype(BF).T

    @pl.loop(0, pairs_n // 2)
    def _(turn):
        step = pairs_n // 2 - 1 - turn

        @pl.when(2 * step + kept < pairs_n)
        def _():
            for t in (0, 1):
                load_e(2 * step + t).wait()

        for t in (1, 0):
            attend_back(2 * step + t)

        @pl.when(2 * step >= kept)
        def _():
            for t in (0, 1):
                load_e(2 * step + t - kept).start()

    dq = on

    @pl.loop(0, pairs_n)
    def _(turn):
        hp = pairs_n - 1 - turn
        lanes = pl.ds(pl.multiple_of(hp * PAIR, PAIR), PAIR)
        part_send(hp).wait()
        for t, store in ((0, dk), (1, dv)):
            for s in (0, 1):
                own = store[s, :, lanes].astype(F32)
                store[s, :, lanes] = (own + part_in[hp, t, s].astype(F32)).astype(BF)

    cross, near = 1 - z // 2, z // 2
    piece = span // 4
    tg = n2

    def tg_copy(s, k):
        rows_k = pl.ds(k * piece, piece)
        home = (batch - core + z // 2, low + s * (high - low))
        return remote(
            tg.at[s, rows_k], tg_o.at[lax.rem(z, 2), rows_k],
            tg_s.at[s, k], tg_r.at[lax.rem(z, 2), k], home,
        )

    pieces = ar.shape[0]
    group = lax.rem(batch, pieces)

    def batch_round(r):
        return remote(ar, ar_in.at[r], ar_s.at[r], ar_r.at[r], peers[r])

    def z_send(d):
        return remote(ar.at[group], z_all.at[z], z_s.at[d], z_r.at[z], z_peers[d])

    def share_round(r):
        size = 2**r
        held = pl.ds(group // size * size, size)
        return remote(total.at[held], total.at[held], all_s.at[r], all_r.at[r], peers[r])

    def share_wait(r):
        size = 2**r
        other = group // size
        other = other + 1 - 2 * lax.rem(other, 2)
        held = pl.ds(other * size, size)
        remote(total.at[held], total.at[held], all_s.at[r], all_r.at[r], peers[r]).wait_recv()

    def project_back(s):
        @pl.loop(0, blocks)
        def _(c):
            here = pl.ds(pl.multiple_of(c * 256, 256), 256)
            total = dot(dq[s], wf[here, 0:width], NT)
            total += dot(dk[s], wf[here, width : 2 * width], NT)
            total += dot(dv[s], wf[here, 2 * width : 3 * width], NT)
            acc[0:span, here] = total

        normed, inverse = norm_stats(tokin[s].astype(F32))
        rows_s = pl.ds(pl.multiple_of(s * span, span), span)
        tg[s] = (resid[rows_s] + norm_back(acc[0:span], normed, inverse, row(gain))).astype(BF)

    project_back(cross)
    for i in (0, 1):
        out_send[i].wait_send()
    for k in (0, 1):
        tg_copy(cross, k).start()
    for k, (grad, down, up) in enumerate(((dq, down_q, up_q), (dv, down_v, up_v))):
        up_total = down_total = 0.0
        for i in (0, 1):
            inner = dot(n1[i], down[...], NT).astype(BF)
            lift = dot(grad[i], up[...], NT).astype(BF)
            up_total = up_total + dot(inner, grad[i], TN)
            down_total = down_total + dot(lift, n1[i], TN)
        for c in range(pieces):
            lanes = slice(c * PAIR, (c + 1) * PAIR)
            ar[c, 8 * k : 8 * k + 4] = ADAPTER * up_total[:, lanes]
            ar[c, 8 * k + 4 : 8 * k + 8] = ADAPTER * down_total[:, lanes]
    batch_round(0).start()
    project_back(near)
    for r in range(len(peers)):
        if r > 0:
            batch_round(r).start()
        batch_round(r).wait()
        ar[...] += ar_in[r]
    for d in range(depth - 1):
        z_send(d).start()
    for k in range(4):
        tg_copy(near, k).start()
    for k in (2, 3):
        tg_copy(cross, k).start()
    z_all[z] = ar[group]
    for d in range(depth - 1):
        z_send(d).wait_send()
        from_z = lax.rem(z + depth - 1 - d, depth)
        remote(z_all.at[from_z], z_all.at[from_z], z_s.at[d], z_r.at[from_z], mate).wait_recv()
    summed = z_all[0]
    for d in range(1, depth):
        summed = summed + z_all[d]
    total[group] = summed
    for r in range(3):
        share_round(r).start()
        share_round(r).wait_send()
        share_wait(r)
    sums_o[...] = total[...]

    for i in (0, 1):
        remote(out_o.at[i], out_o.at[i], out_s.at[i], out_r.at[i], mate).wait_recv()
        for k in range(4):
            tg_copy(i, k).wait_send()
            landed = tg_o.at[i, pl.ds(k * piece, piece)]
            remote(landed, landed, tg_s.at[i, k], tg_r.at[i, k], mate).wait_recv()


def deliver_kernel(out_i, tg_i, sums, out_o, tg_o, down_q, up_q, down_v, up_v):
    out_o[...] = out_i[...]
    tg_o[...] = tg_i[...]
    for c in range(sums.shape[0]):
        lanes = slice(c * PAIR, (c + 1) * PAIR)
        for k, ref in enumerate((up_q, down_q, up_v, down_v)):
            ref[:, lanes] = sums[c, 4 * k : 4 * k + 4]


VMEM = pl.BlockSpec(memory_space=pltpu.VMEM)
ANY = pl.BlockSpec(memory_space=pl.ANY)
DMA = pltpu.SemaphoreType.DMA
LIMIT = 60 * 1024 * 1024
GELU = 0.7978845608028654


def on_device(
    tokens, doc_starts, attn_gain, attn_shift, qkv_weight, qkv_bias,
    query_down_factor, query_up_factor, value_down_factor, value_up_factor,
    out_weight, out_bias, mlp_gain, mlp_shift, fc_weight, fc_bias, proj_weight, proj_bias, out_grad,
):
    slots, span, width = tokens.shape
    hidden = fc_weight.shape[1]
    rank = query_down_factor.shape[1]
    pairs_n = width // PAIR
    chunk = 1024
    blocks = width // 256
    shape = jax.ShapeDtypeStruct
    two = (slots, span, width)
    flat = (2 * span, width)
    q_shape = (pairs_n, 2, span, PAIR)
    k_shape = (pairs_n, 4, span, PAIR)
    rounds = [2**r for r in range((lax.axis_size("batch") - 1).bit_length())]
    depth = lax.axis_size("blk")
    pieces = width // PAIR
    n_rounds = len(rounds)

    def fused(*refs):
        fused_kernel(rounds, *refs)

    bf = lambda *dims: pltpu.VMEM(dims, BF)
    f32 = lambda *dims: pltpu.VMEM(dims, F32)
    out_l, tg_l, sums, _ = pl.pallas_call(
        fused,
        out_shape=(
            shape(two, BF), shape(two, BF), shape((pieces, 16, PAIR), F32),
            shape((max(pairs_n - 4, 1), 2, 5, span, span), BF),
        ),
        in_specs=[ANY] * 6 + [VMEM] * 13,
        out_specs=(ANY, ANY, VMEM, ANY),
        scratch_shapes=[
            bf(*two), bf(*two), bf(width, 3 * width), bf(width, width),
            bf(2, width, chunk), bf(2, chunk, width), bf(*two), bf(*two),
            bf(*q_shape), bf(*k_shape), bf(*k_shape),
            bf(2, 2, PAIR, span), bf(4, PAIR, span),
            f32(2, 5, span, span), bf(4, 2, 5, span, span), f32(5, span, span),
            bf(pairs_n, 2, PAIR, span), bf(*two), f32(pairs_n, 8, span),
            f32(*flat), f32(*flat), bf(hidden // chunk, 2 * span, chunk), bf(*two),
            bf(*two),
            bf(2, PAIR, 2 * span), bf(2, 2 * span, PAIR), bf(2, 2 * span, PAIR), bf(5, span, 2 * span),
            bf(pairs_n, 2, 2, span, PAIR), bf(pairs_n, 2, 2, span, PAIR),
            f32(pieces, 16, PAIR), f32(n_rounds, pieces, 16, PAIR), f32(depth, 16, PAIR), f32(pieces, 16, PAIR),
            pltpu.VMEM(doc_starts.shape, jnp.int32),
            DMA((2,)), DMA((2,)), DMA((2,)), DMA((2,)),
            DMA((2, blocks, 2)), DMA((2, blocks, 2)), DMA((2,)), DMA((1,)), DMA((2,)), DMA((2,)), DMA((4,)),
            DMA((2,)), DMA((2,)), DMA((2, 4)), DMA((2, 4)),
            DMA((pairs_n,)), DMA((pairs_n,)), DMA((n_rounds,)), DMA((n_rounds,)),
            DMA((depth - 1,)), DMA((depth,)), DMA((3,)), DMA((3,)), pltpu.SemaphoreType.REGULAR,
        ],
        compiler_params=pltpu.CompilerParams(
            collective_id=0, has_side_effects=True, vmem_limit_bytes=LIMIT
        ),
    )(
        tokens, out_grad, qkv_weight, out_weight, fc_weight, proj_weight, doc_starts,
        attn_gain, attn_shift, qkv_bias, out_bias, mlp_gain, mlp_shift, fc_bias, proj_bias,
        query_down_factor.T, query_up_factor, value_down_factor.T, value_up_factor,
    )

    small = shape((rank, width), F32)
    block = pl.BlockSpec((1, span, width), lambda i: (i, 0, 0))
    whole = lambda *dims: pl.BlockSpec(dims, lambda i: (0,) * len(dims))
    out, tg, down_q, up_q, down_v, up_v = pl.pallas_call(
        deliver_kernel,
        grid=(slots,),
        out_shape=(shape(two, BF), shape(two, BF), small, small, small, small),
        in_specs=[block, block, whole(pieces, 16, PAIR)],
        out_specs=(block, block) + (whole(rank, width),) * 4,
    )(out_l, tg_l, sums)
    return out, tg, down_q.T, up_q, down_v.T, up_v


def solution(mesh):
    rows = P("batch", "blk", None)
    return jax.shard_map(
        on_device,
        mesh=mesh,
        in_specs=(rows, P("batch", None)) + (P(),) * 16 + (rows,),
        out_specs=(rows, rows, P(), P(), P(), P()),
        check_vma=False,
    )
```

```python
import jax
import jax.numpy as jnp
from jax import lax
from jax.experimental import pallas as pl
from jax.experimental.pallas import tpu as pltpu
from jax.sharding import PartitionSpec as P

F32 = jnp.float32
BF = jnp.bfloat16
MESH = pl.DeviceIdType.MESH
EPS = 1e-05
ADAPTER = 8.0
NEG = -1e30
LOG2E = 1.4426950408889634
LN2 = 0.6931471805599453
HEAD = 64
PAIR = 128
NN = (((1,), (0,)), ((), ()))
NT = (((1,), (1,)), ((), ()))
TN = (((0,), (0,)), ((), ()))


def dot(a, b, dims=NN):
    return lax.dot_general(a, b, dims, preferred_element_type=F32)


def row(ref):
    return ref[...].astype(F32).reshape(1, ref.shape[0])


def places():
    batch = lax.axis_index("batch")
    z = lax.axis_index("blk")
    core = lax.rem(batch, 2)
    base = batch - core
    outer = lax.rem(core + z, 2)
    edge = 1 - lax.rem((z + 1) // 2, 2)
    low, high = 1 - outer, 2 + outer
    hosts = [(base + lax.rem(i + edge, 2), 2 * core + i) for i in (0, 1)]
    homes = [(base + z // 2, low), (base + z // 2, high)]
    mate = (base + 1 - core, z)
    return dict(
        batch=batch, z=z, core=core, outer=outer, low=low, high=high,
        hosts=hosts, homes=homes, mate=mate,
    )


def greet(devices):
    barrier = pltpu.get_barrier_semaphore()
    for device in devices:
        pl.semaphore_signal(barrier, inc=1, device_id=device, device_id_type=MESH)
    pl.semaphore_wait(barrier, len(devices))


def remote(src, dst, send, recv, device):
    return pltpu.make_async_remote_copy(
        src_ref=src, dst_ref=dst, send_sem=send, recv_sem=recv,
        device_id=device, device_id_type=MESH,
    )


def norm_stats(x):
    center = x - jnp.mean(x, -1, keepdims=True)
    inverse = lax.rsqrt(jnp.mean(center * center, -1, keepdims=True) + EPS)
    return center * inverse, inverse


def norm_back(upstream, normed, inverse, gain):
    scaled = upstream * gain
    return inverse * (
        scaled
        - jnp.mean(scaled, -1, keepdims=True)
        - normed * jnp.mean(scaled * normed, -1, keepdims=True)
    )


def mask_bias(starts, key_span, query_span, span):
    key_pos = lax.broadcasted_iota(jnp.int32, (span, 1), 0) + key_span * span
    query_pos = lax.broadcasted_iota(jnp.int32, (1, span), 1) + query_span * span
    key_doc = jnp.zeros((span, 1), jnp.int32)
    query_doc = jnp.zeros((1, span), jnp.int32)
    for j in range(starts.shape[1]):
        start = starts[0:1, j : j + 1]
        key_doc = key_doc + (key_pos >= start).astype(jnp.int32)
        query_doc = query_doc + (query_pos >= start).astype(jnp.int32)
    allowed = (key_doc == query_doc) & (key_pos <= query_pos)
    return jnp.where(allowed, 0.0, NEG)


def half_rows(x, head):
    part = x[HEAD * head : HEAD * head + HEAD]
    zero = jnp.zeros_like(part)
    return jnp.concatenate([part, zero] if head == 0 else [zero, part], 0)


def half_lanes(x, head):
    lane = lax.broadcasted_iota(jnp.int32, x.shape, 1)
    keep = (lane < HEAD) if head == 0 else (lane >= HEAD)
    return jnp.where(keep, x, jnp.zeros_like(x))


def fused_kernel(
    rounds,
    tok, og, wqkv, wo_h, fc_h, proj_h, *rest,
):
    (
        starts_h, gain_h, shift_h, qkv_bias_h, out_bias_h, gain2_h, shift2_h, fc_bias_h, proj_bias_h, down_q_h, up_q_h, down_v_h, up_v_h,
        out_o, tg_o, sums_o, e_h,
        tokin, ogin, wf, wo, fcb, pjb, n1, n2, qn, kn, vn, qp, vt, sc, ee, bias, ot, on, rl,
        resid, acc, slope, outst, dv, dopc, don, qm, dss, part, part_in, ar, ar_in, piece_sum, far_in, z_all, total, starts_in,
        tok_s, tok_r, og_s, og_r, ex_s, ex_r, st_sem, w_sem, fc_sem, pj_sem, e_sem,
        out_s, out_r, tg_s, tg_r, px_s, px_r, ar_s, ar_r, far_s, far_r, z_s, z_r, all_s, all_r, sent,
        starts, gain, shift, qkv_bias, out_bias, gain2, shift2, fc_bias, proj_bias, down_q, up_q, down_v, up_v, small_sem,
    ) = rest
    at = places()
    z, core, outer = at["z"], at["core"], at["outer"]
    low, high, mate, batch = at["low"], at["high"], at["mate"], at["batch"]
    span, width = tokin.shape[1], tokin.shape[2]
    pairs_n = qn.shape[0]
    blocks = width // 256
    chunks, chunk = slope.shape[0], slope.shape[2]
    pieces = ar.shape[0]
    group = lax.rem(batch, pieces)
    around = [
        (batch - group + lax.rem(group + d, pieces), z) for d in range(1, pieces)
    ]
    far = []
    for distance in rounds:
        bit = lax.rem(batch // distance, 2)
        far.append((batch + distance - 2 * distance * bit, z))
    depth = z_all.shape[0]
    z_peers = [(batch, lax.rem(z + d, depth)) for d in range(1, depth)]
    beside = (batch, z + 1 - 2 * lax.rem(z, 2))

    load_w = pltpu.make_async_copy(wqkv, wf, w_sem.at[0])
    load_w.start()
    greet(at["hosts"] + at["homes"] + [mate] + around + far + z_peers)
    tok_send = [
        remote(tok.at[i], tokin.at[z // 2], tok_s.at[i], tok_r.at[z // 2], at["hosts"][i])
        for i in (0, 1)
    ]
    for copy in tok_send:
        copy.start()
    small = [
        pltpu.make_async_copy(src, dst, small_sem.at[k])
        for k, (src, dst) in enumerate((
            (starts_h, starts), (gain_h, gain), (shift_h, shift), (qkv_bias_h, qkv_bias), (out_bias_h, out_bias), (gain2_h, gain2), (shift2_h, shift2), (fc_bias_h, fc_bias), (proj_bias_h, proj_bias), (down_q_h, down_q), (up_q_h, up_q), (down_v_h, down_v), (up_v_h, up_v),
        ))
    ]
    for copy in small:
        copy.start()
    for copy in small:
        copy.wait()
    starts_copy = remote(starts, starts_in, st_sem.at[0], st_sem.at[1], mate)
    starts_copy.start()

    def load_mlp(c):
        slot = lax.rem(c, 2)
        here = pl.ds(pl.multiple_of(c * chunk, chunk), chunk)
        return (
            pltpu.make_async_copy(fc_h.at[:, here], fcb.at[slot], fc_sem.at[slot]),
            pltpu.make_async_copy(proj_h.at[here, :], pjb.at[slot], pj_sem.at[slot]),
        )

    load_w.wait()
    load_o = pltpu.make_async_copy(wo_h, wo, w_sem.at[0])
    load_o.start()
    for part_w, down, up in ((0, down_q, up_q), (2, down_v, up_v)):

        @pl.loop(0, blocks)
        def _(c):
            col = pl.ds(pl.multiple_of(part_w * width + c * 256, 256), 256)
            here = pl.ds(pl.multiple_of(c * 256, 256), 256)
            extra = dot(down[...], up[:, here], TN)
            wf[:, col] = (wf[:, col].astype(F32) + ADAPTER * extra).astype(BF)

    starts_copy.wait()
    mine = (z // 2 == core).astype(jnp.int32)
    both = starts[...] * mine + starts_in[...] * (1 - mine)
    second = lax.rem(z, 2)
    chosen = both[0:1] * (1 - second) + both[1:2] * second
    first_remote = 1 - low
    key_spans = (low, high, low, first_remote, first_remote + outer)
    query_spans = (low, high, high, low + outer * (high - low), high)
    for j in range(5):
        bias[j] = mask_bias(chosen, key_spans[j], query_spans[j], span)

    def exchange(s, c):
        here = pl.ds(2 * c, 2)
        return [
            remote(ref.at[here, s], ref.at[here, 2 + s], ex_s.at[s, c, t], ex_r.at[s, c, t], mate)
            for t, ref in enumerate((kn, vn))
        ]

    for turn in (0, 1):
        s = z // 2 if turn == 0 else 1 - z // 2
        if turn == 1:
            for copy in tok_send:
                copy.wait_send()
            pl.semaphore_signal(sent, inc=1, device_id=beside, device_id_type=MESH)
        remote(tokin.at[s], tokin.at[s], tok_s.at[0], tok_r.at[s], mate).wait_recv()
        if turn == 1:
            pl.semaphore_wait(sent, 1)
            og_send = [
                remote(og.at[i], ogin.at[z // 2], og_s.at[i], og_r.at[z // 2], at["hosts"][i])
                for i in (0, 1)
            ]
            for copy in og_send:
                copy.start()
            for c in (0, 1):
                for copy in load_mlp(c):
                    copy.start()
        normed, _ = norm_stats(tokin[s].astype(F32))
        n1[s] = (normed * row(gain) + row(shift)).astype(BF)

        @pl.loop(0, blocks)
        def _(c):
            for which, store, scale in ((1, kn, None), (2, vn, None), (0, qn, LOG2E / HEAD**0.5)):
                col = pl.ds(pl.multiple_of(which * width + c * 256, 256), 256)
                made = dot(n1[s], wf[:, col]) + qkv_bias[col].astype(F32).reshape(1, 256)
                if scale is not None:
                    made = made * scale
                made = made.astype(BF)
                for t in (0, 1):
                    store[2 * c + t, s] = made[:, t * PAIR : (t + 1) * PAIR]
                if which == 2:
                    for copy in exchange(s, c):
                        copy.start()

    outer_f = outer.astype(F32)
    inner_f = 1.0 - outer_f
    ones = jnp.ones((16, span), BF)
    key_at = (0, 1, 0, 2, 2 + outer)
    query_at = (0, 1, 1, outer, 1)

    kept = ee.shape[0]

    def save_e(hp):
        slot = lax.rem(hp, kept)
        return pltpu.make_async_copy(ee.at[slot], e_h.at[hp], e_sem.at[slot])

    def load_e(hp):
        slot = lax.rem(hp, kept)
        return pltpu.make_async_copy(e_h.at[hp], ee.at[slot], e_sem.at[slot])

    def attend(hp):
        slot = lax.rem(hp, kept)
        for s in (0, 1):
            q_t = qn[hp, s].T
            for head in (0, 1):
                qp[head, s] = half_rows(q_t, head)
        for kb in range(4):
            vt[kb] = vn[hp, kb].T
        tops = []
        for head in (0, 1):
            tops.append([])
            for j in range(5):
                s_j = dot(kn[hp, key_at[j]], qp[head, query_at[j]]) + bias[j]
                sc[head, j] = s_j
                tops[head].append(jnp.max(s_j, 0, keepdims=True))
        for head in (0, 1):
            m0, m1, m2, m3, m4 = tops[head]
            top_low = jnp.maximum(m0, m3 * inner_f + NEG * outer_f)
            top_high = jnp.maximum(
                jnp.maximum(m1, m2), jnp.maximum(m4, m3 * outer_f + NEG * inner_f)
            )
            top_x = top_high * outer_f + top_low * inner_f
            mixed = []
            for j, top in enumerate((top_low, top_high, top_high, top_x, top_high)):
                e_j = jnp.exp2(sc[head, j] - top).astype(BF)
                ee[slot, head, j] = e_j
                v_j = jnp.concatenate(
                    [vt[key_at[j], HEAD * head : HEAD * head + HEAD], ones], 0
                )
                mixed.append(dot(v_j, e_j))
            sums = (
                mixed[0] + mixed[3] * inner_f,
                mixed[1] + mixed[2] + mixed[4] + mixed[3] * outer_f,
            )
            for s in (0, 1):
                inv = 1.0 / sums[s][HEAD : HEAD + 1]
                rl[hp, 2 * head + s : 2 * head + s + 1, :] = inv
                ot[hp, s, HEAD * head : HEAD * head + HEAD, :] = (sums[s][:HEAD] * inv).astype(BF)
        for s in (0, 1):
            on[s, :, pl.ds(pl.multiple_of(hp * PAIR, PAIR), PAIR)] = ot[hp, s].T
        @pl.when(hp + kept < pairs_n)
        def _():
            save_e(hp).start()

    @pl.loop(0, pairs_n // 2)
    def _(step):
        for s in (0, 1):
            for copy in exchange(s, step):
                copy.wait()

        @pl.when(2 * step >= kept)
        def _():
            for t in (0, 1):
                save_e(2 * step + t - kept).wait()

        for t in (0, 1):
            attend(2 * step + t)

    load_o.wait()
    for s in (0, 1):
        here = pl.ds(s * span, span)
        r = tokin[s].astype(F32) + (dot(on[s], wo[...]) + row(out_bias))
        resid[here] = r
        normed, _ = norm_stats(r)
        n2[s] = (normed * row(gain2) + row(shift2)).astype(BF)
        acc[here] = r + row(proj_bias)

    @pl.loop(0, chunks)
    def _(c):
        slot = lax.rem(c, 2)
        for copy in load_mlp(c):
            copy.wait()
        part_b = fc_bias[pl.ds(pl.multiple_of(c * chunk, chunk), chunk)]
        x = dot(n2[...].reshape(2 * span, width), fcb[slot]) + part_b.astype(F32).reshape(1, chunk)
        sq = x * x
        half = 0.5 * jnp.tanh(x * ((GELU * 0.044715) * sq + GELU)) + 0.5
        act = x * half
        rise = half + (act - act * half) * ((6.0 * GELU * 0.044715) * sq + 2.0 * GELU)
        slope[c] = rise.astype(BF)
        acc[...] += dot(act.astype(BF), pjb[slot])

        @pl.when(c + 2 < chunks)
        def _():
            for copy in load_mlp(c + 2):
                copy.start()

    for s in (0, 1):
        outst[s] = acc[pl.ds(s * span, span)].astype(BF)
    for i in (0, 1):
        og_send[i].wait_send()
    out_send = [
        remote(
            outst.at[i], out_o.at[lax.rem(z, 2)], out_s.at[i], out_r.at[lax.rem(z, 2)], at["homes"][i]
        )
        for i in (0, 1)
    ]
    for copy in out_send:
        copy.start()
    acc[...] = jnp.zeros_like(acc)
    for i in (0, 1):
        remote(ogin.at[i], ogin.at[i], og_s.at[i], og_r.at[i], mate).wait_recv()

    @pl.loop(0, chunks)
    def _(t):
        c = chunks - 1 - t
        slot = lax.rem(c, 2)

        @pl.when(t >= 2)
        def _():
            for copy in load_mlp(c):
                copy.wait()

        og_flat = ogin[...].reshape(2 * span, width)
        gh = (dot(og_flat, pjb[slot], NT) * slope[c].astype(F32)).astype(BF)
        acc[...] += dot(gh, fcb[slot], NT)

        @pl.when(c >= 2)
        def _():
            for copy in load_mlp(c - 2):
                copy.start()

    for s in (0, 1):
        here = pl.ds(s * span, span)
        normed, inverse = norm_stats(resid[here])
        g = ogin[s].astype(F32) + norm_back(acc[here], normed, inverse, row(gain2))
        resid[here] = g
        n2[s] = dot(g.astype(BF), wo[...], NT).astype(BF)

    dk = ogin

    def part_send(hp):
        return remote(part.at[hp], part_in.at[hp], px_s.at[hp], px_r.at[hp], mate)

    def attend_back(hp):
        slot = lax.rem(hp, kept)
        lanes = pl.ds(pl.multiple_of(hp * PAIR, PAIR), PAIR)
        delta = [[None, None], [None, None]]
        for s in (0, 1):
            da_t = n2[s, :, lanes].astype(F32).T
            prod = da_t * ot[hp, s].astype(F32)
            scaled = []
            for head in (0, 1):
                rows_h = slice(HEAD * head, HEAD * head + HEAD)
                inv = rl[hp, 2 * head + s : 2 * head + s + 1, :]
                delta[head][s] = jnp.sum(prod[rows_h], 0, keepdims=True) * inv
                scaled.append(da_t[rows_h] * inv)
            scaled = jnp.concatenate(scaled, 0).astype(BF)
            natural = scaled.T
            q_n = qn[hp, s]
            for head in (0, 1):
                cols = slice(head * span, (head + 1) * span)
                dopc[s, :, cols] = half_rows(scaled, head)
                don[s, cols] = half_lanes(natural, head)
                qm[s, cols] = half_lanes(q_n, head)
        for kb in range(4):
            vt[kb] = kn[hp, kb].T
        for j in range(5):
            for head in (0, 1):
                cols = slice(head * span, (head + 1) * span)
                d_low, d_high = delta[head]
                d_j = (d_low, d_high, d_high, d_high * outer_f + d_low * inner_f, d_high)[j]
                dp = dot(vn[hp, key_at[j]], dopc[query_at[j], :, cols])
                dss[j, :, cols] = (ee[slot, head, j].astype(F32) * (dp - d_j)).astype(BF)
        dk_parts, dv_parts, grads = [], [], [[], []]
        for j in range(5):
            e_pair = jnp.concatenate([ee[slot, 0, j], ee[slot, 1, j]], 1)
            dv_parts.append(dot(e_pair, don[query_at[j]]))
        for j in range(5):
            for head in (0, 1):
                cols = slice(head * span, (head + 1) * span)
                grads[head].append(
                    dot(vt[key_at[j], HEAD * head : HEAD * head + HEAD], dss[j, :, cols])
                )
            dk_parts.append(dot(dss[j], qm[query_at[j]]))
        for t, parts, scale in ((0, dk_parts, LN2), (1, dv_parts, 1.0)):
            store = (dk, dv)[t]
            store[0, :, lanes] = ((parts[0] + parts[2]) * scale).astype(BF)
            store[1, :, lanes] = (parts[1] * scale).astype(BF)
            part[hp, t, 0] = ((parts[3] + parts[4] * inner_f) * scale).astype(BF)
            part[hp, t, 1] = (parts[4] * (outer_f * scale)).astype(BF)
        part_send(hp).start()
        for s in (0, 1):
            rows_t = []
            for head in (0, 1):
                g = grads[head]
                if s == 0:
                    total = g[0] + g[3] * inner_f
                else:
                    total = g[1] + g[2] + g[4] + g[3] * outer_f
                rows_t.append(total * (1.0 / HEAD**0.5))
            on[s, :, lanes] = jnp.concatenate(rows_t, 0).astype(BF).T

    @pl.loop(0, pairs_n // 2)
    def _(turn):
        step = pairs_n // 2 - 1 - turn

        @pl.when(2 * step + kept < pairs_n)
        def _():
            for t in (0, 1):
                load_e(2 * step + t).wait()

        for t in (1, 0):
            attend_back(2 * step + t)

        @pl.when(2 * step >= kept)
        def _():
            for t in (0, 1):
                load_e(2 * step + t - kept).start()

    dq = on

    @pl.loop(0, pairs_n)
    def _(turn):
        hp = pairs_n - 1 - turn
        lanes = pl.ds(pl.multiple_of(hp * PAIR, PAIR), PAIR)
        part_send(hp).wait()
        for t, store in ((0, dk), (1, dv)):
            for s in (0, 1):
                own = store[s, :, lanes].astype(F32)
                store[s, :, lanes] = (own + part_in[hp, t, s].astype(F32)).astype(BF)

    cross, near = 1 - z // 2, z // 2
    piece = span // 4
    tg = n2

    def tg_copy(s, k):
        rows_k = pl.ds(k * piece, piece)
        home = (batch - core + z // 2, low + s * (high - low))
        return remote(
            tg.at[s, rows_k], tg_o.at[lax.rem(z, 2), rows_k],
            tg_s.at[s, k], tg_r.at[lax.rem(z, 2), k], home,
        )

    def spread(d):
        there = lax.rem(group + d, pieces)
        return remote(
            ar.at[there], ar_in.at[group], ar_s.at[d - 1], ar_r.at[group], around[d - 1]
        )

    def spread_wait(d):
        sender = lax.rem(group + pieces - d, pieces)
        spread(d).wait_send()
        remote(
            ar_in.at[sender], ar_in.at[sender], ar_s.at[d - 1], ar_r.at[sender], mate
        ).wait_recv()

    def far_round(r):
        return remote(piece_sum, far_in.at[r], far_s.at[r], far_r.at[r], far[r])

    def z_send(d):
        return remote(piece_sum, z_all.at[z], z_s.at[d], z_r.at[z], z_peers[d])

    def share(d):
        return remote(
            total.at[group], total.at[group], all_s.at[d - 1], all_r.at[group], around[d - 1]
        )

    def share_wait(d):
        sender = lax.rem(group + pieces - d, pieces)
        share(d).wait_send()
        remote(
            total.at[sender], total.at[sender], all_s.at[d - 1], all_r.at[sender], mate
        ).wait_recv()

    def project_back(s, first, count):
        rows_p = slice(first, first + count)

        @pl.loop(0, blocks)
        def _(c):
            here = pl.ds(pl.multiple_of(c * 256, 256), 256)
            made = dot(dq[s, rows_p], wf[here, 0:width], NT)
            made += dot(dk[s, rows_p], wf[here, width : 2 * width], NT)
            made += dot(dv[s, rows_p], wf[here, 2 * width : 3 * width], NT)
            acc[rows_p, here] = made

        normed, inverse = norm_stats(tokin[s, rows_p].astype(F32))
        rows_s = pl.ds(pl.multiple_of(s * span + first, count), count)
        back = norm_back(acc[rows_p], normed, inverse, row(gain))
        tg[s, rows_p] = (resid[rows_s] + back).astype(BF)

    project_back(cross, 0, span // 2)
    for i in (0, 1):
        out_send[i].wait_send()
    tg_copy(cross, 0).start()
    project_back(cross, span // 2, span // 2)
    for k, (grad, down, up) in enumerate(((dq, down_q, up_q), (dv, down_v, up_v))):
        up_total = down_total = 0.0
        for i in (0, 1):
            inner = dot(n1[i], down[...], NT).astype(BF)
            lift = dot(grad[i], up[...], NT).astype(BF)
            up_total = up_total + dot(inner, grad[i], TN)
            down_total = down_total + dot(lift, n1[i], TN)
        for c in range(pieces):
            lanes = slice(c * PAIR, (c + 1) * PAIR)
            ar[c, 8 * k : 8 * k + 4] = ADAPTER * up_total[:, lanes]
            ar[c, 8 * k + 4 : 8 * k + 8] = ADAPTER * down_total[:, lanes]
    for d in range(1, pieces):
        spread(d).start()
    ar_in[group] = ar[group]
    tg_copy(cross, 1).start()
    project_back(near, 0, span)
    for d in range(1, pieces):
        spread_wait(d)
    added = ar_in[0]
    for d in range(1, pieces):
        added = added + ar_in[d]
    piece_sum[...] = added
    for r in range(len(far)):
        far_round(r).start()
        far_round(r).wait()
        piece_sum[...] += far_in[r]
    for d in range(depth - 1):
        z_send(d).start()
    for k in range(4):
        tg_copy(near, k).start()
    for k in (2, 3):
        tg_copy(cross, k).start()
    z_all[z] = piece_sum[...]
    for d in range(depth - 1):
        z_send(d).wait_send()
        from_z = lax.rem(z + depth - 1 - d, depth)
        remote(z_all.at[from_z], z_all.at[from_z], z_s.at[d], z_r.at[from_z], mate).wait_recv()
    summed = z_all[0]
    for d in range(1, depth):
        summed = summed + z_all[d]
    total[group] = summed
    for d in range(1, pieces):
        share(d).start()
    for d in range(1, pieces):
        share_wait(d)
    sums_o[...] = total[...]

    for i in (0, 1):
        remote(out_o.at[i], out_o.at[i], out_s.at[i], out_r.at[i], mate).wait_recv()
        for k in range(4):
            tg_copy(i, k).wait_send()
            landed = tg_o.at[i, pl.ds(k * piece, piece)]
            remote(landed, landed, tg_s.at[i, k], tg_r.at[i, k], mate).wait_recv()


def deliver_kernel(out_i, tg_i, sums, out_o, tg_o, down_q, up_q, down_v, up_v):
    out_o[...] = out_i[...]
    tg_o[...] = tg_i[...]
    for c in range(sums.shape[0]):
        lanes = slice(c * PAIR, (c + 1) * PAIR)
        for k, ref in enumerate((up_q, down_q, up_v, down_v)):
            ref[:, lanes] = sums[c, 4 * k : 4 * k + 4]


VMEM = pl.BlockSpec(memory_space=pltpu.VMEM)
ANY = pl.BlockSpec(memory_space=pl.ANY)
DMA = pltpu.SemaphoreType.DMA
LIMIT = 60 * 1024 * 1024
GELU = 0.7978845608028654


def on_device(
    tokens, doc_starts, attn_gain, attn_shift, qkv_weight, qkv_bias,
    query_down_factor, query_up_factor, value_down_factor, value_up_factor,
    out_weight, out_bias, mlp_gain, mlp_shift, fc_weight, fc_bias, proj_weight, proj_bias, out_grad,
):
    slots, span, width = tokens.shape
    hidden = fc_weight.shape[1]
    rank = query_down_factor.shape[1]
    pairs_n = width // PAIR
    chunk = 1024
    blocks = width // 256
    shape = jax.ShapeDtypeStruct
    two = (slots, span, width)
    flat = (2 * span, width)
    q_shape = (pairs_n, 2, span, PAIR)
    k_shape = (pairs_n, 4, span, PAIR)
    depth = lax.axis_size("blk")
    pieces = width // PAIR
    rounds = []
    while pieces << len(rounds) < lax.axis_size("batch"):
        rounds.append(pieces << len(rounds))
    n_rounds = max(len(rounds), 1)

    def fused(*refs):
        fused_kernel(rounds, *refs)

    bf = lambda *dims: pltpu.VMEM(dims, BF)
    f32 = lambda *dims: pltpu.VMEM(dims, F32)
    out_l, tg_l, sums, _ = pl.pallas_call(
        fused,
        out_shape=(
            shape(two, BF), shape(two, BF), shape((pieces, 16, PAIR), F32),
            shape((max(pairs_n - 4, 1), 2, 5, span, span), BF),
        ),
        in_specs=[ANY] * 19,
        out_specs=(ANY, ANY, VMEM, ANY),
        scratch_shapes=[
            bf(*two), bf(*two), bf(width, 3 * width), bf(width, width),
            bf(2, width, chunk), bf(2, chunk, width), bf(*two), bf(*two),
            bf(*q_shape), bf(*k_shape), bf(*k_shape),
            bf(2, 2, PAIR, span), bf(4, PAIR, span),
            f32(2, 5, span, span), bf(4, 2, 5, span, span), f32(5, span, span),
            bf(pairs_n, 2, PAIR, span), bf(*two), f32(pairs_n, 8, span),
            f32(*flat), f32(*flat), bf(hidden // chunk, 2 * span, chunk), bf(*two),
            bf(*two),
            bf(2, PAIR, 2 * span), bf(2, 2 * span, PAIR), bf(2, 2 * span, PAIR), bf(5, span, 2 * span),
            bf(pairs_n, 2, 2, span, PAIR), bf(pairs_n, 2, 2, span, PAIR),
            f32(pieces, 16, PAIR), f32(pieces, 16, PAIR), f32(16, PAIR), f32(n_rounds, 16, PAIR),
            f32(depth, 16, PAIR), f32(pieces, 16, PAIR),
            pltpu.VMEM(doc_starts.shape, jnp.int32),
            DMA((2,)), DMA((2,)), DMA((2,)), DMA((2,)),
            DMA((2, blocks, 2)), DMA((2, blocks, 2)), DMA((2,)), DMA((1,)), DMA((2,)), DMA((2,)), DMA((4,)),
            DMA((2,)), DMA((2,)), DMA((2, 4)), DMA((2, 4)),
            DMA((pairs_n,)), DMA((pairs_n,)), DMA((pieces - 1,)), DMA((pieces,)), DMA((n_rounds,)), DMA((n_rounds,)),
            DMA((depth - 1,)), DMA((depth,)), DMA((pieces - 1,)), DMA((pieces,)), pltpu.SemaphoreType.REGULAR,
            pltpu.VMEM(doc_starts.shape, jnp.int32), bf(width), bf(width), bf(3 * width), bf(width), bf(width), bf(width),
            bf(hidden), bf(width), bf(rank, width), bf(rank, width), bf(rank, width), bf(rank, width), DMA((13,)),
        ],
        compiler_params=pltpu.CompilerParams(
            collective_id=0, has_side_effects=True, vmem_limit_bytes=LIMIT
        ),
    )(
        tokens, out_grad, qkv_weight, out_weight, fc_weight, proj_weight, doc_starts,
        attn_gain, attn_shift, qkv_bias, out_bias, mlp_gain, mlp_shift, fc_bias, proj_bias,
        query_down_factor.T, query_up_factor, value_down_factor.T, value_up_factor,
    )

    small = shape((rank, width), F32)
    block = pl.BlockSpec((1, span, width), lambda i: (i, 0, 0))
    whole = lambda *dims: pl.BlockSpec(dims, lambda i: (0,) * len(dims))
    out, tg, down_q, up_q, down_v, up_v = pl.pallas_call(
        deliver_kernel,
        grid=(slots,),
        out_shape=(shape(two, BF), shape(two, BF), small, small, small, small),
        in_specs=[block, block, whole(pieces, 16, PAIR)],
        out_specs=(block, block) + (whole(rank, width),) * 4,
    )(out_l, tg_l, sums)
    return out, tg, down_q.T, up_q, down_v.T, up_v


def solution(mesh):
    rows = P("batch", "blk", None)
    return jax.shard_map(
        on_device,
        mesh=mesh,
        in_specs=(rows, P("batch", None)) + (P(),) * 16 + (rows,),
        out_specs=(rows, rows, P(), P(), P(), P()),
        check_vma=False,
    )
```

```python
import jax
import jax.numpy as jnp
from jax import lax
from jax.experimental import pallas as pl
from jax.experimental.pallas import tpu as pltpu
from jax.sharding import PartitionSpec as P

F32 = jnp.float32
BF = jnp.bfloat16
MESH = pl.DeviceIdType.MESH
EPS = 1e-05
ADAPTER = 8.0
NEG = -1e30
LOG2E = 1.4426950408889634
LN2 = 0.6931471805599453
HEAD = 64
PAIR = 128
NN = (((1,), (0,)), ((), ()))
NT = (((1,), (1,)), ((), ()))
TN = (((0,), (0,)), ((), ()))


def dot(a, b, dims=NN):
    return lax.dot_general(a, b, dims, preferred_element_type=F32)


def row(ref):
    return ref[...].astype(F32).reshape(1, ref.shape[0])


def places():
    batch = lax.axis_index("batch")
    z = lax.axis_index("blk")
    core = lax.rem(batch, 2)
    base = batch - core
    outer = lax.rem(core + z, 2)
    edge = 1 - lax.rem((z + 1) // 2, 2)
    low, high = 1 - outer, 2 + outer
    hosts = [(base + lax.rem(i + edge, 2), 2 * core + i) for i in (0, 1)]
    homes = [(base + z // 2, low), (base + z // 2, high)]
    mate = (base + 1 - core, z)
    return dict(
        batch=batch, z=z, core=core, outer=outer, low=low, high=high,
        hosts=hosts, homes=homes, mate=mate,
    )


def greet(devices):
    barrier = pltpu.get_barrier_semaphore()
    for device in devices:
        pl.semaphore_signal(barrier, inc=1, device_id=device, device_id_type=MESH)
    pl.semaphore_wait(barrier, len(devices))


def remote(src, dst, send, recv, device):
    return pltpu.make_async_remote_copy(
        src_ref=src, dst_ref=dst, send_sem=send, recv_sem=recv,
        device_id=device, device_id_type=MESH,
    )


def norm_stats(x):
    center = x - jnp.mean(x, -1, keepdims=True)
    inverse = lax.rsqrt(jnp.mean(center * center, -1, keepdims=True) + EPS)
    return center * inverse, inverse


def norm_back(upstream, normed, inverse, gain):
    scaled = upstream * gain
    return inverse * (
        scaled
        - jnp.mean(scaled, -1, keepdims=True)
        - normed * jnp.mean(scaled * normed, -1, keepdims=True)
    )


def mask_bias(starts, key_span, query_span, span):
    key_pos = lax.broadcasted_iota(jnp.int32, (span, 1), 0) + key_span * span
    query_pos = lax.broadcasted_iota(jnp.int32, (1, span), 1) + query_span * span
    key_doc = jnp.zeros((span, 1), jnp.int32)
    query_doc = jnp.zeros((1, span), jnp.int32)
    for j in range(starts.shape[1]):
        start = starts[0:1, j : j + 1]
        key_doc = key_doc + (key_pos >= start).astype(jnp.int32)
        query_doc = query_doc + (query_pos >= start).astype(jnp.int32)
    allowed = (key_doc == query_doc) & (key_pos <= query_pos)
    return jnp.where(allowed, 0.0, NEG)


def half_rows(x, head):
    part = x[HEAD * head : HEAD * head + HEAD]
    zero = jnp.zeros_like(part)
    return jnp.concatenate([part, zero] if head == 0 else [zero, part], 0)


def half_lanes(x, head):
    lane = lax.broadcasted_iota(jnp.int32, x.shape, 1)
    keep = (lane < HEAD) if head == 0 else (lane >= HEAD)
    return jnp.where(keep, x, jnp.zeros_like(x))


def fused_kernel(
    rounds,
    tok, og, wqkv, wo_h, fc_h, proj_h, *rest,
):
    (
        starts_h, gain_h, shift_h, qkv_bias_h, out_bias_h, gain2_h, shift2_h, fc_bias_h, proj_bias_h, down_q_h, up_q_h, down_v_h, up_v_h,
        out_o, tg_o, sums_o, e_h,
        tokin, ogin, wf, wo, fcb, pjb, n1, n2, qn, kn, vn, qp, vt, sc, ee, bias, ot, on, rl,
        resid, acc, slope, outst, dv, dopc, don, qm, dss, part, part_in, ar, ar_in, piece_sum, far_in, z_all, total, starts_in,
        tok_s, tok_r, og_s, og_r, ex_s, ex_r, st_sem, w_sem, fc_sem, pj_sem, e_sem,
        out_s, out_r, tg_s, tg_r, px_s, px_r, ar_s, ar_r, far_s, far_r, z_s, z_r, all_s, all_r, sent,
        starts, gain, shift, qkv_bias, out_bias, gain2, shift2, fc_bias, proj_bias, down_q, up_q, down_v, up_v, small_sem,
    ) = rest
    at = places()
    z, core, outer = at["z"], at["core"], at["outer"]
    low, high, mate, batch = at["low"], at["high"], at["mate"], at["batch"]
    span, width = tokin.shape[1], tokin.shape[2]
    pairs_n = qn.shape[0]
    blocks = width // 256
    chunks, chunk = slope.shape[0], slope.shape[2]
    pieces = ar.shape[0]
    group = lax.rem(batch, pieces)
    around = [
        (batch - group + lax.rem(group + d, pieces), z) for d in range(1, pieces)
    ]
    far = []
    for distance in rounds:
        bit = lax.rem(batch // distance, 2)
        far.append((batch + distance - 2 * distance * bit, z))
    depth = z_all.shape[0]
    z_peers = [(batch, lax.rem(z + d, depth)) for d in range(1, depth)]
    beside = (batch, z + 1 - 2 * lax.rem(z, 2))

    load_w = pltpu.make_async_copy(wqkv, wf, w_sem.at[0])
    load_w.start()
    greet(at["hosts"] + at["homes"] + [mate] + around + far + z_peers)
    tok_send = [
        remote(tok.at[i], tokin.at[z // 2], tok_s.at[i], tok_r.at[z // 2], at["hosts"][i])
        for i in (0, 1)
    ]
    for copy in tok_send:
        copy.start()
    small = [
        pltpu.make_async_copy(src, dst, small_sem.at[k])
        for k, (src, dst) in enumerate((
            (starts_h, starts), (gain_h, gain), (shift_h, shift), (qkv_bias_h, qkv_bias), (out_bias_h, out_bias), (gain2_h, gain2), (shift2_h, shift2), (fc_bias_h, fc_bias), (proj_bias_h, proj_bias), (down_q_h, down_q), (up_q_h, up_q), (down_v_h, down_v), (up_v_h, up_v),
        ))
    ]
    for copy in small:
        copy.start()
    for copy in small:
        copy.wait()
    starts_copy = remote(starts, starts_in, st_sem.at[0], st_sem.at[1], mate)
    starts_copy.start()

    def load_mlp(c):
        slot = lax.rem(c, 2)
        here = pl.ds(pl.multiple_of(c * chunk, chunk), chunk)
        return (
            pltpu.make_async_copy(fc_h.at[:, here], fcb.at[slot], fc_sem.at[slot]),
            pltpu.make_async_copy(proj_h.at[here, :], pjb.at[slot], pj_sem.at[slot]),
        )

    load_w.wait()
    load_o = pltpu.make_async_copy(wo_h, wo, w_sem.at[0])
    load_o.start()
    for part_w, down, up in ((0, down_q, up_q), (2, down_v, up_v)):

        @pl.loop(0, blocks)
        def _(c):
            col = pl.ds(pl.multiple_of(part_w * width + c * 256, 256), 256)
            here = pl.ds(pl.multiple_of(c * 256, 256), 256)
            extra = dot(down[...], up[:, here], TN)
            wf[:, col] = (wf[:, col].astype(F32) + ADAPTER * extra).astype(BF)

    starts_copy.wait()
    mine = (z // 2 == core).astype(jnp.int32)
    both = starts[...] * mine + starts_in[...] * (1 - mine)
    second = lax.rem(z, 2)
    chosen = both[0:1] * (1 - second) + both[1:2] * second
    first_remote = 1 - low
    key_spans = (low, high, low, first_remote, first_remote + outer)
    query_spans = (low, high, high, low + outer * (high - low), high)
    for j in range(5):
        bias[j] = mask_bias(chosen, key_spans[j], query_spans[j], span)

    def exchange(s, c):
        here = pl.ds(2 * c, 2)
        return [
            remote(ref.at[here, s], ref.at[here, 2 + s], ex_s.at[s, c, t], ex_r.at[s, c, t], mate)
            for t, ref in enumerate((kn, vn))
        ]

    for turn in (0, 1):
        s = z // 2 if turn == 0 else 1 - z // 2
        if turn == 1:
            for copy in tok_send:
                copy.wait_send()
            pl.semaphore_signal(sent, inc=1, device_id=beside, device_id_type=MESH)
        remote(tokin.at[s], tokin.at[s], tok_s.at[0], tok_r.at[s], mate).wait_recv()
        if turn == 1:
            pl.semaphore_wait(sent, 1)
            og_send = [
                remote(og.at[i], ogin.at[z // 2], og_s.at[i], og_r.at[z // 2], at["hosts"][i])
                for i in (0, 1)
            ]
            for copy in og_send:
                copy.start()
            for c in (0, 1):
                for copy in load_mlp(c):
                    copy.start()
        normed, _ = norm_stats(tokin[s].astype(F32))
        n1[s] = (normed * row(gain) + row(shift)).astype(BF)

        @pl.loop(0, blocks)
        def _(c):
            for which, store, scale in ((1, kn, None), (2, vn, None), (0, qn, LOG2E / HEAD**0.5)):
                col = pl.ds(pl.multiple_of(which * width + c * 256, 256), 256)
                made = dot(n1[s], wf[:, col]) + qkv_bias[col].astype(F32).reshape(1, 256)
                if scale is not None:
                    made = made * scale
                made = made.astype(BF)
                for t in (0, 1):
                    store[2 * c + t, s] = made[:, t * PAIR : (t + 1) * PAIR]
                if which == 2:
                    for copy in exchange(s, c):
                        copy.start()

    outer_f = outer.astype(F32)
    inner_f = 1.0 - outer_f
    ones = jnp.ones((16, span), BF)
    key_at = (0, 1, 0, 2, 2 + outer)
    query_at = (0, 1, 1, outer, 1)

    kept = ee.shape[0]

    def save_e(hp):
        slot = lax.rem(hp, kept)
        return pltpu.make_async_copy(ee.at[slot], e_h.at[hp], e_sem.at[slot])

    def load_e(hp):
        slot = lax.rem(hp, kept)
        return pltpu.make_async_copy(e_h.at[hp], ee.at[slot], e_sem.at[slot])

    def attend(hp):
        slot = lax.rem(hp, kept)
        for s in (0, 1):
            q_t = qn[hp, s].T
            for head in (0, 1):
                qp[head, s] = half_rows(q_t, head)
        for kb in range(4):
            vt[kb] = vn[hp, kb].T
        tops = []
        for head in (0, 1):
            tops.append([])
            for j in range(5):
                s_j = dot(kn[hp, key_at[j]], qp[head, query_at[j]]) + bias[j]
                sc[head, j] = s_j
                tops[head].append(jnp.max(s_j, 0, keepdims=True))
        for head in (0, 1):
            m0, m1, m2, m3, m4 = tops[head]
            top_low = jnp.maximum(m0, m3 * inner_f + NEG * outer_f)
            top_high = jnp.maximum(
                jnp.maximum(m1, m2), jnp.maximum(m4, m3 * outer_f + NEG * inner_f)
            )
            top_x = top_high * outer_f + top_low * inner_f
            mixed = []
            for j, top in enumerate((top_low, top_high, top_high, top_x, top_high)):
                e_j = jnp.exp2(sc[head, j] - top).astype(BF)
                ee[slot, head, j] = e_j
                v_j = jnp.concatenate(
                    [vt[key_at[j], HEAD * head : HEAD * head + HEAD], ones], 0
                )
                mixed.append(dot(v_j, e_j))
            sums = (
                mixed[0] + mixed[3] * inner_f,
                mixed[1] + mixed[2] + mixed[4] + mixed[3] * outer_f,
            )
            for s in (0, 1):
                inv = 1.0 / sums[s][HEAD : HEAD + 1]
                rl[hp, 2 * head + s : 2 * head + s + 1, :] = inv
                ot[hp, s, HEAD * head : HEAD * head + HEAD, :] = (sums[s][:HEAD] * inv).astype(BF)
        for s in (0, 1):
            on[s, :, pl.ds(pl.multiple_of(hp * PAIR, PAIR), PAIR)] = ot[hp, s].T
        @pl.when(hp + kept < pairs_n)
        def _():
            save_e(hp).start()

    @pl.loop(0, pairs_n // 2)
    def _(step):
        for s in (0, 1):
            for copy in exchange(s, step):
                copy.wait()

        @pl.when(2 * step >= kept)
        def _():
            for t in (0, 1):
                save_e(2 * step + t - kept).wait()

        for t in (0, 1):
            attend(2 * step + t)

    load_o.wait()
    acc[...] = dot(on[...].reshape(2 * span, width), wo[...])
    for s in (0, 1):
        here = pl.ds(s * span, span)
        r = tokin[s].astype(F32) + (acc[here] + row(out_bias))
        resid[here] = r
        normed, _ = norm_stats(r)
        n2[s] = (normed * row(gain2) + row(shift2)).astype(BF)
        acc[here] = r + row(proj_bias)

    @pl.loop(0, chunks)
    def _(c):
        slot = lax.rem(c, 2)
        for copy in load_mlp(c):
            copy.wait()
        part_b = fc_bias[pl.ds(pl.multiple_of(c * chunk, chunk), chunk)]
        x = dot(n2[...].reshape(2 * span, width), fcb[slot]) + part_b.astype(F32).reshape(1, chunk)
        sq = x * x
        half = 0.5 * jnp.tanh(x * ((GELU * 0.044715) * sq + GELU)) + 0.5
        act = x * half
        rise = half + (act - act * half) * ((6.0 * GELU * 0.044715) * sq + 2.0 * GELU)
        slope[c] = rise.astype(BF)
        acc[...] += dot(act.astype(BF), pjb[slot])

        @pl.when(c + 2 < chunks)
        def _():
            for copy in load_mlp(c + 2):
                copy.start()

    for s in (0, 1):
        outst[s] = acc[pl.ds(s * span, span)].astype(BF)
    for i in (0, 1):
        og_send[i].wait_send()
    out_send = [
        remote(
            outst.at[i], out_o.at[lax.rem(z, 2)], out_s.at[i], out_r.at[lax.rem(z, 2)], at["homes"][i]
        )
        for i in (0, 1)
    ]
    for copy in out_send:
        copy.start()
    acc[...] = jnp.zeros_like(acc)
    for i in (0, 1):
        remote(ogin.at[i], ogin.at[i], og_s.at[i], og_r.at[i], mate).wait_recv()

    @pl.loop(0, chunks)
    def _(t):
        c = chunks - 1 - t
        slot = lax.rem(c, 2)

        @pl.when(t >= 2)
        def _():
            for copy in load_mlp(c):
                copy.wait()

        og_flat = ogin[...].reshape(2 * span, width)
        gh = (dot(og_flat, pjb[slot], NT) * slope[c].astype(F32)).astype(BF)
        acc[...] += dot(gh, fcb[slot], NT)

        @pl.when(c >= 2)
        def _():
            for copy in load_mlp(c - 2):
                copy.start()

    for s in (0, 1):
        here = pl.ds(s * span, span)
        normed, inverse = norm_stats(resid[here])
        g = ogin[s].astype(F32) + norm_back(acc[here], normed, inverse, row(gain2))
        resid[here] = g
        n2[s] = g.astype(BF)
    made_att = dot(n2[...].reshape(2 * span, width), wo[...], NT).astype(BF)
    n2[...] = made_att.reshape(2, span, width)

    dk = ogin

    def part_send(hp):
        return remote(part.at[hp], part_in.at[hp], px_s.at[hp], px_r.at[hp], mate)

    def attend_back(hp):
        slot = lax.rem(hp, kept)
        lanes = pl.ds(pl.multiple_of(hp * PAIR, PAIR), PAIR)
        delta = [[None, None], [None, None]]
        for s in (0, 1):
            da_t = n2[s, :, lanes].astype(F32).T
            prod = da_t * ot[hp, s].astype(F32)
            scaled = []
            for head in (0, 1):
                rows_h = slice(HEAD * head, HEAD * head + HEAD)
                inv = rl[hp, 2 * head + s : 2 * head + s + 1, :]
                delta[head][s] = jnp.sum(prod[rows_h], 0, keepdims=True) * inv
                scaled.append(da_t[rows_h] * inv)
            scaled = jnp.concatenate(scaled, 0).astype(BF)
            natural = scaled.T
            q_n = qn[hp, s]
            for head in (0, 1):
                cols = slice(head * span, (head + 1) * span)
                dopc[s, :, cols] = half_rows(scaled, head)
                don[s, cols] = half_lanes(natural, head)
                qm[s, cols] = half_lanes(q_n, head)
        for kb in range(4):
            vt[kb] = kn[hp, kb].T
        for j in range(5):
            for head in (0, 1):
                cols = slice(head * span, (head + 1) * span)
                d_low, d_high = delta[head]
                d_j = (d_low, d_high, d_high, d_high * outer_f + d_low * inner_f, d_high)[j]
                dp = dot(vn[hp, key_at[j]], dopc[query_at[j], :, cols])
                dss[j, :, cols] = (ee[slot, head, j].astype(F32) * (dp - d_j)).astype(BF)
        dk_parts, dv_parts, grads = [], [], [[], []]
        for j in range(5):
            e_pair = jnp.concatenate([ee[slot, 0, j], ee[slot, 1, j]], 1)
            dv_parts.append(dot(e_pair, don[query_at[j]]))
        for j in range(5):
            for head in (0, 1):
                cols = slice(head * span, (head + 1) * span)
                grads[head].append(
                    dot(vt[key_at[j], HEAD * head : HEAD * head + HEAD], dss[j, :, cols])
                )
            dk_parts.append(dot(dss[j], qm[query_at[j]]))
        for t, parts, scale in ((0, dk_parts, LN2), (1, dv_parts, 1.0)):
            store = (dk, dv)[t]
            store[0, :, lanes] = ((parts[0] + parts[2]) * scale).astype(BF)
            store[1, :, lanes] = (parts[1] * scale).astype(BF)
            part[hp, t, 0] = ((parts[3] + parts[4] * inner_f) * scale).astype(BF)
            part[hp, t, 1] = (parts[4] * (outer_f * scale)).astype(BF)
        part_send(hp).start()
        for s in (0, 1):
            rows_t = []
            for head in (0, 1):
                g = grads[head]
                if s == 0:
                    total = g[0] + g[3] * inner_f
                else:
                    total = g[1] + g[2] + g[4] + g[3] * outer_f
                rows_t.append(total * (1.0 / HEAD**0.5))
            on[s, :, lanes] = jnp.concatenate(rows_t, 0).astype(BF).T

    @pl.loop(0, pairs_n // 2)
    def _(turn):
        step = pairs_n // 2 - 1 - turn

        @pl.when(2 * step + kept < pairs_n)
        def _():
            for t in (0, 1):
                load_e(2 * step + t).wait()

        for t in (1, 0):
            attend_back(2 * step + t)

        @pl.when(2 * step >= kept)
        def _():
            for t in (0, 1):
                load_e(2 * step + t - kept).start()

    dq = on
    cross, near = 1 - z // 2, z // 2

    @pl.loop(0, blocks)
    def _(c):
        here = pl.ds(pl.multiple_of(c * 256, 256), 256)
        acc[0:span, here] = dot(dq[cross], wf[here, 0:width], NT)

    @pl.loop(0, pairs_n)
    def _(turn):
        hp = pairs_n - 1 - turn
        lanes = pl.ds(pl.multiple_of(hp * PAIR, PAIR), PAIR)
        part_send(hp).wait()
        for t, store in ((0, dk), (1, dv)):
            for s in (0, 1):
                own = store[s, :, lanes].astype(F32)
                store[s, :, lanes] = (own + part_in[hp, t, s].astype(F32)).astype(BF)

    piece = span // 4
    tg = n2

    def tg_copy(s, k):
        rows_k = pl.ds(k * piece, piece)
        home = (batch - core + z // 2, low + s * (high - low))
        return remote(
            tg.at[s, rows_k], tg_o.at[lax.rem(z, 2), rows_k],
            tg_s.at[s, k], tg_r.at[lax.rem(z, 2), k], home,
        )

    def spread(d):
        there = lax.rem(group + d, pieces)
        return remote(
            ar.at[there], ar_in.at[group], ar_s.at[d - 1], ar_r.at[group], around[d - 1]
        )

    def spread_wait(d):
        sender = lax.rem(group + pieces - d, pieces)
        spread(d).wait_send()
        remote(
            ar_in.at[sender], ar_in.at[sender], ar_s.at[d - 1], ar_r.at[sender], mate
        ).wait_recv()

    def far_round(r):
        return remote(piece_sum, far_in.at[r], far_s.at[r], far_r.at[r], far[r])

    def z_send(d):
        return remote(piece_sum, z_all.at[z], z_s.at[d], z_r.at[z], z_peers[d])

    def share(d):
        return remote(
            total.at[group], total.at[group], all_s.at[d - 1], all_r.at[group], around[d - 1]
        )

    def share_wait(d):
        sender = lax.rem(group + pieces - d, pieces)
        share(d).wait_send()
        remote(
            total.at[sender], total.at[sender], all_s.at[d - 1], all_r.at[sender], mate
        ).wait_recv()

    def project_back(s, first, count, started):
        rows_p = slice(first, first + count)

        @pl.loop(0, blocks)
        def _(c):
            here = pl.ds(pl.multiple_of(c * 256, 256), 256)
            if started:
                made = acc[rows_p, here]
            else:
                made = dot(dq[s, rows_p], wf[here, 0:width], NT)
            made += dot(dk[s, rows_p], wf[here, width : 2 * width], NT)
            made += dot(dv[s, rows_p], wf[here, 2 * width : 3 * width], NT)
            acc[rows_p, here] = made

        normed, inverse = norm_stats(tokin[s, rows_p].astype(F32))
        rows_s = pl.ds(pl.multiple_of(s * span + first, count), count)
        back = norm_back(acc[rows_p], normed, inverse, row(gain))
        tg[s, rows_p] = (resid[rows_s] + back).astype(BF)

    project_back(cross, 0, span // 2, True)
    for i in (0, 1):
        out_send[i].wait_send()
    tg_copy(cross, 0).start()
    project_back(cross, span // 2, span // 2, True)
    for k, (grad, down, up) in enumerate(((dq, down_q, up_q), (dv, down_v, up_v))):
        up_total = down_total = 0.0
        for i in (0, 1):
            inner = dot(n1[i], down[...], NT).astype(BF)
            lift = dot(grad[i], up[...], NT).astype(BF)
            up_total = up_total + dot(inner, grad[i], TN)
            down_total = down_total + dot(lift, n1[i], TN)
        for c in range(pieces):
            lanes = slice(c * PAIR, (c + 1) * PAIR)
            ar[c, 8 * k : 8 * k + 4] = ADAPTER * up_total[:, lanes]
            ar[c, 8 * k + 4 : 8 * k + 8] = ADAPTER * down_total[:, lanes]
    for d in range(1, pieces):
        spread(d).start()
    ar_in[group] = ar[group]
    tg_copy(cross, 1).start()
    project_back(near, 0, span, False)
    for d in range(1, pieces):
        spread_wait(d)
    added = ar_in[0]
    for d in range(1, pieces):
        added = added + ar_in[d]
    piece_sum[...] = added
    for r in range(len(far)):
        far_round(r).start()
        far_round(r).wait()
        piece_sum[...] += far_in[r]
    for d in range(depth - 1):
        z_send(d).start()
    for k in range(4):
        tg_copy(near, k).start()
    for k in (2, 3):
        tg_copy(cross, k).start()
    z_all[z] = piece_sum[...]
    for d in range(depth - 1):
        z_send(d).wait_send()
        from_z = lax.rem(z + depth - 1 - d, depth)
        remote(z_all.at[from_z], z_all.at[from_z], z_s.at[d], z_r.at[from_z], mate).wait_recv()
    summed = z_all[0]
    for d in range(1, depth):
        summed = summed + z_all[d]
    total[group] = summed
    for d in range(1, pieces):
        share(d).start()
    for d in range(1, pieces):
        share_wait(d)
    sums_o[...] = total[...]

    for i in (0, 1):
        remote(out_o.at[i], out_o.at[i], out_s.at[i], out_r.at[i], mate).wait_recv()
        for k in range(4):
            tg_copy(i, k).wait_send()
            landed = tg_o.at[i, pl.ds(k * piece, piece)]
            remote(landed, landed, tg_s.at[i, k], tg_r.at[i, k], mate).wait_recv()


def deliver_kernel(out_i, tg_i, sums, out_o, tg_o, down_q, up_q, down_v, up_v):
    out_o[...] = out_i[...]
    tg_o[...] = tg_i[...]
    for c in range(sums.shape[0]):
        lanes = slice(c * PAIR, (c + 1) * PAIR)
        for k, ref in enumerate((up_q, down_q, up_v, down_v)):
            ref[:, lanes] = sums[c, 4 * k : 4 * k + 4]


VMEM = pl.BlockSpec(memory_space=pltpu.VMEM)
ANY = pl.BlockSpec(memory_space=pl.ANY)
DMA = pltpu.SemaphoreType.DMA
LIMIT = 60 * 1024 * 1024
GELU = 0.7978845608028654


def on_device(
    tokens, doc_starts, attn_gain, attn_shift, qkv_weight, qkv_bias,
    query_down_factor, query_up_factor, value_down_factor, value_up_factor,
    out_weight, out_bias, mlp_gain, mlp_shift, fc_weight, fc_bias, proj_weight, proj_bias, out_grad,
):
    slots, span, width = tokens.shape
    hidden = fc_weight.shape[1]
    rank = query_down_factor.shape[1]
    pairs_n = width // PAIR
    chunk = 1024
    blocks = width // 256
    shape = jax.ShapeDtypeStruct
    two = (slots, span, width)
    flat = (2 * span, width)
    q_shape = (pairs_n, 2, span, PAIR)
    k_shape = (pairs_n, 4, span, PAIR)
    depth = lax.axis_size("blk")
    pieces = width // PAIR
    rounds = []
    while pieces << len(rounds) < lax.axis_size("batch"):
        rounds.append(pieces << len(rounds))
    n_rounds = max(len(rounds), 1)

    def fused(*refs):
        fused_kernel(rounds, *refs)

    bf = lambda *dims: pltpu.VMEM(dims, BF)
    f32 = lambda *dims: pltpu.VMEM(dims, F32)
    out_l, tg_l, sums, _ = pl.pallas_call(
        fused,
        out_shape=(
            shape(two, BF), shape(two, BF), shape((pieces, 16, PAIR), F32),
            shape((max(pairs_n - 4, 1), 2, 5, span, span), BF),
        ),
        in_specs=[ANY] * 19,
        out_specs=(ANY, ANY, VMEM, ANY),
        scratch_shapes=[
            bf(*two), bf(*two), bf(width, 3 * width), bf(width, width),
            bf(2, width, chunk), bf(2, chunk, width), bf(*two), bf(*two),
            bf(*q_shape), bf(*k_shape), bf(*k_shape),
            bf(2, 2, PAIR, span), bf(4, PAIR, span),
            f32(2, 5, span, span), bf(4, 2, 5, span, span), f32(5, span, span),
            bf(pairs_n, 2, PAIR, span), bf(*two), f32(pairs_n, 8, span),
            f32(*flat), f32(*flat), bf(hidden // chunk, 2 * span, chunk), bf(*two),
            bf(*two),
            bf(2, PAIR, 2 * span), bf(2, 2 * span, PAIR), bf(2, 2 * span, PAIR), bf(5, span, 2 * span),
            bf(pairs_n, 2, 2, span, PAIR), bf(pairs_n, 2, 2, span, PAIR),
            f32(pieces, 16, PAIR), f32(pieces, 16, PAIR), f32(16, PAIR), f32(n_rounds, 16, PAIR),
            f32(depth, 16, PAIR), f32(pieces, 16, PAIR),
            pltpu.VMEM(doc_starts.shape, jnp.int32),
            DMA((2,)), DMA((2,)), DMA((2,)), DMA((2,)),
            DMA((2, blocks, 2)), DMA((2, blocks, 2)), DMA((2,)), DMA((1,)), DMA((2,)), DMA((2,)), DMA((4,)),
            DMA((2,)), DMA((2,)), DMA((2, 4)), DMA((2, 4)),
            DMA((pairs_n,)), DMA((pairs_n,)), DMA((pieces - 1,)), DMA((pieces,)), DMA((n_rounds,)), DMA((n_rounds,)),
            DMA((depth - 1,)), DMA((depth,)), DMA((pieces - 1,)), DMA((pieces,)), pltpu.SemaphoreType.REGULAR,
            pltpu.VMEM(doc_starts.shape, jnp.int32), bf(width), bf(width), bf(3 * width), bf(width), bf(width), bf(width),
            bf(hidden), bf(width), bf(rank, width), bf(rank, width), bf(rank, width), bf(rank, width), DMA((13,)),
        ],
        compiler_params=pltpu.CompilerParams(
            collective_id=0, has_side_effects=True, vmem_limit_bytes=LIMIT
        ),
    )(
        tokens, out_grad, qkv_weight, out_weight, fc_weight, proj_weight, doc_starts,
        attn_gain, attn_shift, qkv_bias, out_bias, mlp_gain, mlp_shift, fc_bias, proj_bias,
        query_down_factor.T, query_up_factor, value_down_factor.T, value_up_factor,
    )

    small = shape((rank, width), F32)
    block = pl.BlockSpec((1, span, width), lambda i: (i, 0, 0))
    whole = lambda *dims: pl.BlockSpec(dims, lambda i: (0,) * len(dims))
    out, tg, down_q, up_q, down_v, up_v = pl.pallas_call(
        deliver_kernel,
        grid=(slots,),
        out_shape=(shape(two, BF), shape(two, BF), small, small, small, small),
        in_specs=[block, block, whole(pieces, 16, PAIR)],
        out_specs=(block, block) + (whole(rank, width),) * 4,
    )(out_l, tg_l, sums)
    return out, tg, down_q.T, up_q, down_v.T, up_v


def solution(mesh):
    rows = P("batch", "blk", None)
    return jax.shard_map(
        on_device,
        mesh=mesh,
        in_specs=(rows, P("batch", None)) + (P(),) * 16 + (rows,),
        out_specs=(rows, rows, P(), P(), P(), P()),
        check_vma=False,
    )
```

```python
import jax
import jax.numpy as jnp
from jax import lax
from jax.experimental import pallas as pl
from jax.experimental.pallas import tpu as pltpu
from jax.sharding import PartitionSpec as P

F32 = jnp.float32
BF = jnp.bfloat16
MESH = pl.DeviceIdType.MESH
EPS = 1e-05
ADAPTER = 8.0
NEG = -1e30
LOG2E = 1.4426950408889634
LN2 = 0.6931471805599453
HEAD = 64
PAIR = 128
NN = (((1,), (0,)), ((), ()))
NT = (((1,), (1,)), ((), ()))
TN = (((0,), (0,)), ((), ()))


def dot(a, b, dims=NN):
    return lax.dot_general(a, b, dims, preferred_element_type=F32)


def row(ref):
    return ref[...].astype(F32).reshape(1, ref.shape[0])


def places():
    batch = lax.axis_index("batch")
    z = lax.axis_index("blk")
    core = lax.rem(batch, 2)
    base = batch - core
    outer = lax.rem(core + z, 2)
    edge = 1 - lax.rem((z + 1) // 2, 2)
    low, high = 1 - outer, 2 + outer
    hosts = [(base + lax.rem(i + edge, 2), 2 * core + i) for i in (0, 1)]
    homes = [(base + z // 2, low), (base + z // 2, high)]
    mate = (base + 1 - core, z)
    return dict(
        batch=batch, z=z, core=core, outer=outer, low=low, high=high,
        hosts=hosts, homes=homes, mate=mate,
    )


def greet(devices):
    barrier = pltpu.get_barrier_semaphore()
    for device in devices:
        pl.semaphore_signal(barrier, inc=1, device_id=device, device_id_type=MESH)
    pl.semaphore_wait(barrier, len(devices))


def remote(src, dst, send, recv, device):
    return pltpu.make_async_remote_copy(
        src_ref=src, dst_ref=dst, send_sem=send, recv_sem=recv,
        device_id=device, device_id_type=MESH,
    )


def norm_stats(x):
    center = x - jnp.mean(x, -1, keepdims=True)
    inverse = lax.rsqrt(jnp.mean(center * center, -1, keepdims=True) + EPS)
    return center * inverse, inverse


def norm_back(upstream, normed, inverse, gain):
    scaled = upstream * gain
    return inverse * (
        scaled
        - jnp.mean(scaled, -1, keepdims=True)
        - normed * jnp.mean(scaled * normed, -1, keepdims=True)
    )


def mask_bias(starts, key_span, query_span, span):
    key_pos = lax.broadcasted_iota(jnp.int32, (span, 1), 0) + key_span * span
    query_pos = lax.broadcasted_iota(jnp.int32, (1, span), 1) + query_span * span
    key_doc = jnp.zeros((span, 1), jnp.int32)
    query_doc = jnp.zeros((1, span), jnp.int32)
    for j in range(starts.shape[1]):
        start = starts[0:1, j : j + 1]
        key_doc = key_doc + (key_pos >= start).astype(jnp.int32)
        query_doc = query_doc + (query_pos >= start).astype(jnp.int32)
    allowed = (key_doc == query_doc) & (key_pos <= query_pos)
    return jnp.where(allowed, 0.0, NEG)


def half_rows(x, head):
    part = x[HEAD * head : HEAD * head + HEAD]
    zero = jnp.zeros_like(part)
    return jnp.concatenate([part, zero] if head == 0 else [zero, part], 0)


def half_lanes(x, head):
    lane = lax.broadcasted_iota(jnp.int32, x.shape, 1)
    keep = (lane < HEAD) if head == 0 else (lane >= HEAD)
    return jnp.where(keep, x, jnp.zeros_like(x))


def fused_kernel(
    rounds,
    tok, og, wqkv, wo_h, fc_h, proj_h, *rest,
):
    (
        starts_h, gain_h, shift_h, qkv_bias_h, out_bias_h, gain2_h, shift2_h, fc_bias_h, proj_bias_h, down_q_h, up_q_h, down_v_h, up_v_h,
        out_o, tg_o, sums_o, e_h,
        tokin, ogin, wf, wo, fcb, pjb, n1, n2, qn, kn, vn, qp, vt, sc, ee, bias, ot, on, rl,
        resid, acc, slope, outst, dv, dopc, don, qm, dss, part, part_in, ar, ar_in, piece_sum, far_in, z_all, total, starts_in,
        tok_s, tok_r, og_s, og_r, ex_s, ex_r, st_sem, w_sem, fc_sem, pj_sem, e_sem,
        out_s, out_r, tg_s, tg_r, px_s, px_r, ar_s, ar_r, far_s, far_r, z_s, z_r, all_s, all_r, sent,
        starts, gain, shift, qkv_bias, out_bias, gain2, shift2, fc_bias, proj_bias, down_q, up_q, down_v, up_v, small_sem,
    ) = rest
    at = places()
    z, core, outer = at["z"], at["core"], at["outer"]
    low, high, mate, batch = at["low"], at["high"], at["mate"], at["batch"]
    span, width = tokin.shape[1], tokin.shape[2]
    pairs_n = qn.shape[0]
    blocks = width // 256
    chunks, chunk = slope.shape[0], slope.shape[2]
    pieces = ar.shape[0]
    group = lax.rem(batch, pieces)
    around = [
        (batch - group + lax.rem(group + d, pieces), z) for d in range(1, pieces)
    ]
    far = []
    for distance in rounds:
        bit = lax.rem(batch // distance, 2)
        far.append((batch + distance - 2 * distance * bit, z))
    depth = z_all.shape[0]
    z_peers = [(batch, lax.rem(z + d, depth)) for d in range(1, depth)]
    beside = (batch, z + 1 - 2 * lax.rem(z, 2))

    load_w = pltpu.make_async_copy(wqkv, wf, w_sem.at[0])
    load_w.start()
    greet(at["hosts"] + at["homes"] + [mate] + around + far + z_peers)
    tok_send = [
        remote(tok.at[i], tokin.at[z // 2], tok_s.at[i], tok_r.at[z // 2], at["hosts"][i])
        for i in (0, 1)
    ]
    for copy in tok_send:
        copy.start()
    small = [
        pltpu.make_async_copy(src, dst, small_sem.at[k])
        for k, (src, dst) in enumerate((
            (starts_h, starts), (gain_h, gain), (shift_h, shift), (qkv_bias_h, qkv_bias), (out_bias_h, out_bias), (gain2_h, gain2), (shift2_h, shift2), (fc_bias_h, fc_bias), (proj_bias_h, proj_bias), (down_q_h, down_q), (up_q_h, up_q), (down_v_h, down_v), (up_v_h, up_v),
        ))
    ]
    for copy in small:
        copy.start()
    for copy in small:
        copy.wait()
    starts_copy = remote(starts, starts_in, st_sem.at[0], st_sem.at[1], mate)
    starts_copy.start()

    def load_mlp(c):
        slot = lax.rem(c, 2)
        here = pl.ds(pl.multiple_of(c * chunk, chunk), chunk)
        return (
            pltpu.make_async_copy(fc_h.at[:, here], fcb.at[slot], fc_sem.at[slot]),
            pltpu.make_async_copy(proj_h.at[here, :], pjb.at[slot], pj_sem.at[slot]),
        )

    load_w.wait()
    load_o = pltpu.make_async_copy(wo_h, wo, w_sem.at[0])
    load_o.start()
    for part_w, down, up in ((0, down_q, up_q), (2, down_v, up_v)):

        @pl.loop(0, blocks)
        def _(c):
            col = pl.ds(pl.multiple_of(part_w * width + c * 256, 256), 256)
            here = pl.ds(pl.multiple_of(c * 256, 256), 256)
            extra = dot(down[...], up[:, here], TN)
            wf[:, col] = (wf[:, col].astype(F32) + ADAPTER * extra).astype(BF)

    starts_copy.wait()
    mine = (z // 2 == core).astype(jnp.int32)
    both = starts[...] * mine + starts_in[...] * (1 - mine)
    second = lax.rem(z, 2)
    chosen = both[0:1] * (1 - second) + both[1:2] * second
    first_remote = 1 - low
    key_spans = (low, high, low, first_remote, first_remote + outer)
    query_spans = (low, high, high, low + outer * (high - low), high)
    for j in range(5):
        bias[j] = mask_bias(chosen, key_spans[j], query_spans[j], span)

    def exchange(s, c):
        here = pl.ds(2 * c, 2)
        return [
            remote(ref.at[here, s], ref.at[here, 2 + s], ex_s.at[s, c, t], ex_r.at[s, c, t], mate)
            for t, ref in enumerate((kn, vn))
        ]

    for turn in (0, 1):
        s = z // 2 if turn == 0 else 1 - z // 2
        if turn == 1:
            for copy in tok_send:
                copy.wait_send()
            pl.semaphore_signal(sent, inc=1, device_id=beside, device_id_type=MESH)
            pl.semaphore_wait(sent, 1)
            og_send = [
                remote(og.at[i], ogin.at[z // 2], og_s.at[i], og_r.at[z // 2], at["hosts"][i])
                for i in (0, 1)
            ]
            for copy in og_send:
                copy.start()
        remote(tokin.at[s], tokin.at[s], tok_s.at[0], tok_r.at[s], mate).wait_recv()
        if turn == 1:
            for c in (0, 1):
                for copy in load_mlp(c):
                    copy.start()
        normed, _ = norm_stats(tokin[s].astype(F32))
        n1[s] = (normed * row(gain) + row(shift)).astype(BF)

        @pl.loop(0, blocks)
        def _(c):
            for which, store, scale in ((1, kn, None), (2, vn, None), (0, qn, LOG2E / HEAD**0.5)):
                col = pl.ds(pl.multiple_of(which * width + c * 256, 256), 256)
                made = dot(n1[s], wf[:, col]) + qkv_bias[col].astype(F32).reshape(1, 256)
                if scale is not None:
                    made = made * scale
                made = made.astype(BF)
                for t in (0, 1):
                    store[2 * c + t, s] = made[:, t * PAIR : (t + 1) * PAIR]
                if which == 2:
                    for copy in exchange(s, c):
                        copy.start()

    outer_f = outer.astype(F32)
    inner_f = 1.0 - outer_f
    ones = jnp.ones((16, span), BF)
    key_at = (0, 1, 0, 2, 2 + outer)
    query_at = (0, 1, 1, outer, 1)

    kept = ee.shape[0]

    def save_e(hp):
        slot = lax.rem(hp, kept)
        return pltpu.make_async_copy(ee.at[slot], e_h.at[hp], e_sem.at[slot])

    def load_e(hp):
        slot = lax.rem(hp, kept)
        return pltpu.make_async_copy(e_h.at[hp], ee.at[slot], e_sem.at[slot])

    def attend(hp):
        slot = lax.rem(hp, kept)
        for s in (0, 1):
            q_t = qn[hp, s].T
            for head in (0, 1):
                qp[head, s] = half_rows(q_t, head)
        for kb in range(4):
            vt[kb] = vn[hp, kb].T
        tops = []
        for head in (0, 1):
            tops.append([])
            for j in range(5):
                s_j = dot(kn[hp, key_at[j]], qp[head, query_at[j]]) + bias[j]
                sc[head, j] = s_j
                tops[head].append(jnp.max(s_j, 0, keepdims=True))
        for head in (0, 1):
            m0, m1, m2, m3, m4 = tops[head]
            top_low = jnp.maximum(m0, m3 * inner_f + NEG * outer_f)
            top_high = jnp.maximum(
                jnp.maximum(m1, m2), jnp.maximum(m4, m3 * outer_f + NEG * inner_f)
            )
            top_x = top_high * outer_f + top_low * inner_f
            mixed = []
            for j, top in enumerate((top_low, top_high, top_high, top_x, top_high)):
                e_j = jnp.exp2(sc[head, j] - top).astype(BF)
                ee[slot, head, j] = e_j
                v_j = jnp.concatenate(
                    [vt[key_at[j], HEAD * head : HEAD * head + HEAD], ones], 0
                )
                mixed.append(dot(v_j, e_j))
            sums = (
                mixed[0] + mixed[3] * inner_f,
                mixed[1] + mixed[2] + mixed[4] + mixed[3] * outer_f,
            )
            for s in (0, 1):
                inv = 1.0 / sums[s][HEAD : HEAD + 1]
                rl[hp, 2 * head + s : 2 * head + s + 1, :] = inv
                ot[hp, s, HEAD * head : HEAD * head + HEAD, :] = (sums[s][:HEAD] * inv).astype(BF)
        for s in (0, 1):
            on[s, :, pl.ds(pl.multiple_of(hp * PAIR, PAIR), PAIR)] = ot[hp, s].T
        @pl.when(hp + kept < pairs_n)
        def _():
            save_e(hp).start()

    @pl.loop(0, pairs_n // 2)
    def _(step):
        for s in (0, 1):
            for copy in exchange(s, step):
                copy.wait()

        @pl.when(2 * step >= kept)
        def _():
            for t in (0, 1):
                save_e(2 * step + t - kept).wait()

        for t in (0, 1):
            attend(2 * step + t)

    load_o.wait()
    acc[...] = dot(on[...].reshape(2 * span, width), wo[...])
    for s in (0, 1):
        here = pl.ds(s * span, span)
        r = tokin[s].astype(F32) + (acc[here] + row(out_bias))
        resid[here] = r
        normed, _ = norm_stats(r)
        n2[s] = (normed * row(gain2) + row(shift2)).astype(BF)
        acc[here] = r + row(proj_bias)

    @pl.loop(0, chunks)
    def _(c):
        slot = lax.rem(c, 2)
        for copy in load_mlp(c):
            copy.wait()
        part_b = fc_bias[pl.ds(pl.multiple_of(c * chunk, chunk), chunk)]
        x = dot(n2[...].reshape(2 * span, width), fcb[slot]) + part_b.astype(F32).reshape(1, chunk)
        sq = x * x
        half = 0.5 * jnp.tanh(x * ((GELU * 0.044715) * sq + GELU)) + 0.5
        act = x * half
        rise = half + (act - act * half) * ((6.0 * GELU * 0.044715) * sq + 2.0 * GELU)
        slope[c] = rise.astype(BF)
        acc[...] += dot(act.astype(BF), pjb[slot])

        @pl.when(c + 2 < chunks)
        def _():
            for copy in load_mlp(c + 2):
                copy.start()

    for s in (0, 1):
        outst[s] = acc[pl.ds(s * span, span)].astype(BF)
    for i in (0, 1):
        og_send[i].wait_send()
    out_send = [
        remote(
            outst.at[i], out_o.at[lax.rem(z, 2)], out_s.at[i], out_r.at[lax.rem(z, 2)], at["homes"][i]
        )
        for i in (0, 1)
    ]
    for copy in out_send:
        copy.start()
    acc[...] = jnp.zeros_like(acc)
    for i in (0, 1):
        remote(ogin.at[i], ogin.at[i], og_s.at[i], og_r.at[i], mate).wait_recv()

    @pl.loop(0, chunks)
    def _(t):
        c = chunks - 1 - t
        slot = lax.rem(c, 2)

        @pl.when(t >= 2)
        def _():
            for copy in load_mlp(c):
                copy.wait()

        og_flat = ogin[...].reshape(2 * span, width)
        gh = (dot(og_flat, pjb[slot], NT) * slope[c].astype(F32)).astype(BF)
        acc[...] += dot(gh, fcb[slot], NT)

        @pl.when(c >= 2)
        def _():
            for copy in load_mlp(c - 2):
                copy.start()

    for s in (0, 1):
        here = pl.ds(s * span, span)
        normed, inverse = norm_stats(resid[here])
        g = ogin[s].astype(F32) + norm_back(acc[here], normed, inverse, row(gain2))
        resid[here] = g
        n2[s] = g.astype(BF)
    made_att = dot(n2[...].reshape(2 * span, width), wo[...], NT).astype(BF)
    n2[...] = made_att.reshape(2, span, width)

    dk = ogin

    def part_send(hp):
        return remote(part.at[hp], part_in.at[hp], px_s.at[hp], px_r.at[hp], mate)

    def attend_back(hp):
        slot = lax.rem(hp, kept)
        lanes = pl.ds(pl.multiple_of(hp * PAIR, PAIR), PAIR)
        delta = [[None, None], [None, None]]
        for s in (0, 1):
            da_t = n2[s, :, lanes].astype(F32).T
            prod = da_t * ot[hp, s].astype(F32)
            scaled = []
            for head in (0, 1):
                rows_h = slice(HEAD * head, HEAD * head + HEAD)
                inv = rl[hp, 2 * head + s : 2 * head + s + 1, :]
                delta[head][s] = jnp.sum(prod[rows_h], 0, keepdims=True) * inv
                scaled.append(da_t[rows_h] * inv)
            scaled = jnp.concatenate(scaled, 0).astype(BF)
            natural = scaled.T
            q_n = qn[hp, s]
            for head in (0, 1):
                cols = slice(head * span, (head + 1) * span)
                dopc[s, :, cols] = half_rows(scaled, head)
                don[s, cols] = half_lanes(natural, head)
                qm[s, cols] = half_lanes(q_n, head)
        for kb in range(4):
            vt[kb] = kn[hp, kb].T
        for j in range(5):
            for head in (0, 1):
                cols = slice(head * span, (head + 1) * span)
                d_low, d_high = delta[head]
                d_j = (d_low, d_high, d_high, d_high * outer_f + d_low * inner_f, d_high)[j]
                dp = dot(vn[hp, key_at[j]], dopc[query_at[j], :, cols])
                dss[j, :, cols] = (ee[slot, head, j].astype(F32) * (dp - d_j)).astype(BF)
        dk_parts, dv_parts, grads = [], [], [[], []]
        for j in range(5):
            e_pair = jnp.concatenate([ee[slot, 0, j], ee[slot, 1, j]], 1)
            dv_parts.append(dot(e_pair, don[query_at[j]]))
        for j in range(5):
            for head in (0, 1):
                cols = slice(head * span, (head + 1) * span)
                grads[head].append(
                    dot(vt[key_at[j], HEAD * head : HEAD * head + HEAD], dss[j, :, cols])
                )
            dk_parts.append(dot(dss[j], qm[query_at[j]]))
        for t, parts, scale in ((0, dk_parts, LN2), (1, dv_parts, 1.0)):
            store = (dk, dv)[t]
            store[0, :, lanes] = ((parts[0] + parts[2]) * scale).astype(BF)
            store[1, :, lanes] = (parts[1] * scale).astype(BF)
            part[hp, t, 0] = ((parts[3] + parts[4] * inner_f) * scale).astype(BF)
            part[hp, t, 1] = (parts[4] * (outer_f * scale)).astype(BF)
        part_send(hp).start()
        for s in (0, 1):
            rows_t = []
            for head in (0, 1):
                g = grads[head]
                if s == 0:
                    total = g[0] + g[3] * inner_f
                else:
                    total = g[1] + g[2] + g[4] + g[3] * outer_f
                rows_t.append(total * (1.0 / HEAD**0.5))
            on[s, :, lanes] = jnp.concatenate(rows_t, 0).astype(BF).T

    @pl.loop(0, pairs_n // 2)
    def _(turn):
        step = pairs_n // 2 - 1 - turn

        @pl.when(2 * step + kept < pairs_n)
        def _():
            for t in (0, 1):
                load_e(2 * step + t).wait()

        for t in (1, 0):
            attend_back(2 * step + t)

        @pl.when(2 * step >= kept)
        def _():
            for t in (0, 1):
                load_e(2 * step + t - kept).start()

    dq = on
    cross, near = 1 - z // 2, z // 2

    @pl.loop(0, blocks)
    def _(c):
        here = pl.ds(pl.multiple_of(c * 256, 256), 256)
        acc[0:span, here] = dot(dq[cross], wf[here, 0:width], NT)

    @pl.loop(0, pairs_n)
    def _(turn):
        hp = pairs_n - 1 - turn
        lanes = pl.ds(pl.multiple_of(hp * PAIR, PAIR), PAIR)
        part_send(hp).wait()
        for t, store in ((0, dk), (1, dv)):
            for s in (0, 1):
                own = store[s, :, lanes].astype(F32)
                store[s, :, lanes] = (own + part_in[hp, t, s].astype(F32)).astype(BF)

    piece = span // 4
    tg = n2

    def tg_copy(s, k):
        rows_k = pl.ds(k * piece, piece)
        home = (batch - core + z // 2, low + s * (high - low))
        return remote(
            tg.at[s, rows_k], tg_o.at[lax.rem(z, 2), rows_k],
            tg_s.at[s, k], tg_r.at[lax.rem(z, 2), k], home,
        )

    def spread(d):
        there = lax.rem(group + d, pieces)
        return remote(
            ar.at[there], ar_in.at[group], ar_s.at[d - 1], ar_r.at[group], around[d - 1]
        )

    def spread_wait(d):
        sender = lax.rem(group + pieces - d, pieces)
        spread(d).wait_send()
        remote(
            ar_in.at[sender], ar_in.at[sender], ar_s.at[d - 1], ar_r.at[sender], mate
        ).wait_recv()

    def far_round(r):
        return remote(piece_sum, far_in.at[r], far_s.at[r], far_r.at[r], far[r])

    def z_send(d):
        return remote(piece_sum, z_all.at[z], z_s.at[d], z_r.at[z], z_peers[d])

    def share(d):
        return remote(
            total.at[group], total.at[group], all_s.at[d - 1], all_r.at[group], around[d - 1]
        )

    def share_wait(d):
        sender = lax.rem(group + pieces - d, pieces)
        share(d).wait_send()
        remote(
            total.at[sender], total.at[sender], all_s.at[d - 1], all_r.at[sender], mate
        ).wait_recv()

    def project_back(s, first, count, started):
        rows_p = slice(first, first + count)

        @pl.loop(0, blocks)
        def _(c):
            here = pl.ds(pl.multiple_of(c * 256, 256), 256)
            if started:
                made = acc[rows_p, here]
            else:
                made = dot(dq[s, rows_p], wf[here, 0:width], NT)
            made += dot(dk[s, rows_p], wf[here, width : 2 * width], NT)
            made += dot(dv[s, rows_p], wf[here, 2 * width : 3 * width], NT)
            acc[rows_p, here] = made

        normed, inverse = norm_stats(tokin[s, rows_p].astype(F32))
        rows_s = pl.ds(pl.multiple_of(s * span + first, count), count)
        back = norm_back(acc[rows_p], normed, inverse, row(gain))
        tg[s, rows_p] = (resid[rows_s] + back).astype(BF)

    project_back(cross, 0, span // 2, True)
    for i in (0, 1):
        out_send[i].wait_send()
    tg_copy(cross, 0).start()
    project_back(cross, span // 2, span // 2, True)
    for k, (grad, down, up) in enumerate(((dq, down_q, up_q), (dv, down_v, up_v))):
        up_total = down_total = 0.0
        for i in (0, 1):
            inner = dot(n1[i], down[...], NT).astype(BF)
            lift = dot(grad[i], up[...], NT).astype(BF)
            up_total = up_total + dot(inner, grad[i], TN)
            down_total = down_total + dot(lift, n1[i], TN)
        for c in range(pieces):
            lanes = slice(c * PAIR, (c + 1) * PAIR)
            ar[c, 8 * k : 8 * k + 4] = ADAPTER * up_total[:, lanes]
            ar[c, 8 * k + 4 : 8 * k + 8] = ADAPTER * down_total[:, lanes]
    for d in range(1, pieces):
        spread(d).start()
    ar_in[group] = ar[group]
    tg_copy(cross, 1).start()
    project_back(near, 0, span, False)
    for d in range(1, pieces):
        spread_wait(d)
    added = ar_in[0]
    for d in range(1, pieces):
        added = added + ar_in[d]
    piece_sum[...] = added
    for r in range(len(far)):
        far_round(r).start()
        far_round(r).wait()
        piece_sum[...] += far_in[r]
    for d in range(depth - 1):
        z_send(d).start()
    for k in range(4):
        tg_copy(near, k).start()
    for k in (2, 3):
        tg_copy(cross, k).start()
    z_all[z] = piece_sum[...]
    for d in range(depth - 1):
        z_send(d).wait_send()
        from_z = lax.rem(z + depth - 1 - d, depth)
        remote(z_all.at[from_z], z_all.at[from_z], z_s.at[d], z_r.at[from_z], mate).wait_recv()
    summed = z_all[0]
    for d in range(1, depth):
        summed = summed + z_all[d]
    total[group] = summed
    for d in range(1, pieces):
        share(d).start()
    for d in range(1, pieces):
        share_wait(d)
    sums_o[...] = total[...]

    for i in (0, 1):
        remote(out_o.at[i], out_o.at[i], out_s.at[i], out_r.at[i], mate).wait_recv()
        for k in range(4):
            tg_copy(i, k).wait_send()
            landed = tg_o.at[i, pl.ds(k * piece, piece)]
            remote(landed, landed, tg_s.at[i, k], tg_r.at[i, k], mate).wait_recv()


def deliver_kernel(out_i, tg_i, sums, out_o, tg_o, down_q, up_q, down_v, up_v):
    out_o[...] = out_i[...]
    tg_o[...] = tg_i[...]
    for c in range(sums.shape[0]):
        lanes = slice(c * PAIR, (c + 1) * PAIR)
        for k, ref in enumerate((up_q, down_q, up_v, down_v)):
            ref[:, lanes] = sums[c, 4 * k : 4 * k + 4]


VMEM = pl.BlockSpec(memory_space=pltpu.VMEM)
ANY = pl.BlockSpec(memory_space=pl.ANY)
DMA = pltpu.SemaphoreType.DMA
LIMIT = 60 * 1024 * 1024
GELU = 0.7978845608028654


def on_device(
    tokens, doc_starts, attn_gain, attn_shift, qkv_weight, qkv_bias,
    query_down_factor, query_up_factor, value_down_factor, value_up_factor,
    out_weight, out_bias, mlp_gain, mlp_shift, fc_weight, fc_bias, proj_weight, proj_bias, out_grad,
):
    slots, span, width = tokens.shape
    hidden = fc_weight.shape[1]
    rank = query_down_factor.shape[1]
    pairs_n = width // PAIR
    chunk = 1024
    blocks = width // 256
    shape = jax.ShapeDtypeStruct
    two = (slots, span, width)
    flat = (2 * span, width)
    q_shape = (pairs_n, 2, span, PAIR)
    k_shape = (pairs_n, 4, span, PAIR)
    depth = lax.axis_size("blk")
    pieces = width // PAIR
    rounds = []
    while pieces << len(rounds) < lax.axis_size("batch"):
        rounds.append(pieces << len(rounds))
    n_rounds = max(len(rounds), 1)

    def fused(*refs):
        fused_kernel(rounds, *refs)

    bf = lambda *dims: pltpu.VMEM(dims, BF)
    f32 = lambda *dims: pltpu.VMEM(dims, F32)
    out_l, tg_l, sums, _ = pl.pallas_call(
        fused,
        out_shape=(
            shape(two, BF), shape(two, BF), shape((pieces, 16, PAIR), F32),
            shape((max(pairs_n - 4, 1), 2, 5, span, span), BF),
        ),
        in_specs=[ANY] * 19,
        out_specs=(ANY, ANY, VMEM, ANY),
        scratch_shapes=[
            bf(*two), bf(*two), bf(width, 3 * width), bf(width, width),
            bf(2, width, chunk), bf(2, chunk, width), bf(*two), bf(*two),
            bf(*q_shape), bf(*k_shape), bf(*k_shape),
            bf(2, 2, PAIR, span), bf(4, PAIR, span),
            f32(2, 5, span, span), bf(4, 2, 5, span, span), f32(5, span, span),
            bf(pairs_n, 2, PAIR, span), bf(*two), f32(pairs_n, 8, span),
            f32(*flat), f32(*flat), bf(hidden // chunk, 2 * span, chunk), bf(*two),
            bf(*two),
            bf(2, PAIR, 2 * span), bf(2, 2 * span, PAIR), bf(2, 2 * span, PAIR), bf(5, span, 2 * span),
            bf(pairs_n, 2, 2, span, PAIR), bf(pairs_n, 2, 2, span, PAIR),
            f32(pieces, 16, PAIR), f32(pieces, 16, PAIR), f32(16, PAIR), f32(n_rounds, 16, PAIR),
            f32(depth, 16, PAIR), f32(pieces, 16, PAIR),
            pltpu.VMEM(doc_starts.shape, jnp.int32),
            DMA((2,)), DMA((2,)), DMA((2,)), DMA((2,)),
            DMA((2, blocks, 2)), DMA((2, blocks, 2)), DMA((2,)), DMA((1,)), DMA((2,)), DMA((2,)), DMA((4,)),
            DMA((2,)), DMA((2,)), DMA((2, 4)), DMA((2, 4)),
            DMA((pairs_n,)), DMA((pairs_n,)), DMA((pieces - 1,)), DMA((pieces,)), DMA((n_rounds,)), DMA((n_rounds,)),
            DMA((depth - 1,)), DMA((depth,)), DMA((pieces - 1,)), DMA((pieces,)), pltpu.SemaphoreType.REGULAR,
            pltpu.VMEM(doc_starts.shape, jnp.int32), bf(width), bf(width), bf(3 * width), bf(width), bf(width), bf(width),
            bf(hidden), bf(width), bf(rank, width), bf(rank, width), bf(rank, width), bf(rank, width), DMA((13,)),
        ],
        compiler_params=pltpu.CompilerParams(
            collective_id=0, has_side_effects=True, vmem_limit_bytes=LIMIT
        ),
    )(
        tokens, out_grad, qkv_weight, out_weight, fc_weight, proj_weight, doc_starts,
        attn_gain, attn_shift, qkv_bias, out_bias, mlp_gain, mlp_shift, fc_bias, proj_bias,
        query_down_factor.T, query_up_factor, value_down_factor.T, value_up_factor,
    )

    small = shape((rank, width), F32)
    block = pl.BlockSpec((1, span, width), lambda i: (i, 0, 0))
    whole = lambda *dims: pl.BlockSpec(dims, lambda i: (0,) * len(dims))
    out, tg, down_q, up_q, down_v, up_v = pl.pallas_call(
        deliver_kernel,
        grid=(slots,),
        out_shape=(shape(two, BF), shape(two, BF), small, small, small, small),
        in_specs=[block, block, whole(pieces, 16, PAIR)],
        out_specs=(block, block) + (whole(rank, width),) * 4,
    )(out_l, tg_l, sums)
    return out, tg, down_q.T, up_q, down_v.T, up_v


def solution(mesh):
    rows = P("batch", "blk", None)
    return jax.shard_map(
        on_device,
        mesh=mesh,
        in_specs=(rows, P("batch", None)) + (P(),) * 16 + (rows,),
        out_specs=(rows, rows, P(), P(), P(), P()),
        check_vma=False,
    )
```
